32 devices in a mesh: row: 4 (over y, x), col: 8 (over z, core).
Axes of the slice: x: 2, y: 2, z: 4, core: 2. Of those that a mesh axis runs over, the one named last changes fastest.
Arguments:
- features: bfloat16 [16384, 256], P(('col', 'row')), may hold values from -6 to 6
- weight: bfloat16 [256, 256], replicated, may hold values from -0.375 to 0.375
- bias: float32 [256], replicated, may hold values from -4 to 4
- cotangent: bfloat16 [16384, 256], P(('row', 'col')), may hold values from -6 to 6
- tiles: bfloat16 [4, 8, 384, 128, 128], P('row', 'col'), may hold values from -0.0546875 to 0.0546875
- tile_rows: int32 [4, 8, 384], P('row', 'col'), may hold values from 0 to 31, as said below
- tile_cols: int32 [4, 8, 384], P('row', 'col'), may hold values from 0 to 15
- tile_counts: int32 [4, 8], P('row', 'col'), may hold values from 24 to 384, as said below
Outputs:
- hidden: bfloat16 [16384, 256], P(('row', 'col'))
- grad_weight: float32 [256, 256], replicated
- grad_bias: float32 [256], replicated
- grad_features: bfloat16 [16384, 256], P(('col', 'row'))
The draws below stay inside these ranges and needn't reach their ends.
Inputs may be any that keep to these rules, and one draw needn't show every extreme that they name: `tile_rows`: on each grid cell the slots name distinct blocks. `tile_counts`: slots at or after a cell's count are unused; some cell uses all 384 slots.
All inputs are finite; a program needn't handle non-finite values.
Results may differ from the reference program's by a relative error of at most 0.013.
Values may be sent and summed in bfloat16 or wider, within the bound.
No kernel may reach another device: no remote copies, remote signals or barrier semaphores. Data moves between devices by JAX's collectives and lax.ppermute only.
A program may use at most 128 MiB of HBM per device.

```python
import math
import jax
import jax.numpy as jnp
from jax import lax

F = 256
BLOCK = 128
NODE_DEV = 512
TILES_CAP = 384
NODES = 16384
BLK_ROWS = 32
BLK_COLS = 16
N_ROW = 4
N_COL = 8


def tile_slots(key):
    cell_keys = jax.random.split(jax.random.fold_in(key, 7), N_ROW * N_COL)

    def one_cell(cell_key):
        return jax.random.permutation(cell_key, BLK_ROWS * BLK_COLS)[:TILES_CAP]
    chosen = jax.vmap(one_cell)(cell_keys)
    return chosen.reshape(N_ROW, N_COL, TILES_CAP).astype(jnp.int32)


def draw_tile_rows(key, part):
    return (tile_slots(key) // BLK_COLS).astype(jnp.int32)


def draw_tile_cols(key, part):
    return (tile_slots(key) % BLK_COLS).astype(jnp.int32)


def draw_tile_counts(key, part):
    first_key = jax.random.fold_in(key, 11)
    second_key = jax.random.fold_in(key, 13)
    third_key = jax.random.fold_in(key, 17)
    first = jax.random.randint(first_key, (N_ROW * N_COL,), 1, 5)
    second = jax.random.randint(second_key, (N_ROW * N_COL,), 1, 5)
    fullest = jax.random.randint(third_key, (), 0, N_ROW * N_COL)
    shares = first * second
    shares = jnp.where(jnp.arange(N_ROW * N_COL) == fullest, 16, shares)
    return (TILES_CAP * shares // 16).reshape(N_ROW, N_COL).astype(jnp.int32)


def levels(own_key, extent, pieces, smallest, top_value):
    def one(dim, blocks):
        heights = jax.random.uniform(jax.random.fold_in(jax.random.fold_in(own_key, 6), dim), (blocks,), jnp.float32, smallest / len(pieces), top_value / len(pieces))
        return jnp.repeat(jnp.exp(heights), extent[dim] // blocks).reshape((-1,) + (1,) * (len(extent) - dim - 1))

    level = one(*pieces[0])
    for cut in pieces[1:]:
        level = level * one(*cut)
    return level


def gaussian(key, dims, spread, reach, cuts=(), kind=jnp.bfloat16):
    drawn = spread * jax.random.normal(key, dims, jnp.float32)
    if cuts:
        drawn = drawn * levels(key, dims, cuts, -0.22, 0.18)
    return jnp.clip(drawn, -reach, reach).astype(kind)


def setup_inputs(seed: int = 0) -> dict:
    key_of = jax.random.split(jax.random.key(seed), 9)
    features = gaussian(key_of[0], (NODES, F), 1.0, 6.0, ((0, 32),))
    weight = gaussian(key_of[1], (F, F), F ** -0.5, 0.375)
    bias = gaussian(key_of[2], (F,), 1.0, 4.0, (), jnp.float32)
    cotangent = gaussian(key_of[3], (NODES, F), 1.0, 6.0, ((0, 32),))
    tiles = gaussian(key_of[4], (N_ROW, N_COL, TILES_CAP, BLOCK, BLOCK), (TILES_CAP * BLOCK * BLOCK // NODE_DEV) ** -0.5, 0.0546875, ((0, 4), (1, 8)))
    tile_rows = draw_tile_rows(jax.random.fold_in(key_of[8], 71), 0)
    tile_cols = draw_tile_cols(jax.random.fold_in(key_of[8], 71), 0)
    tile_counts = draw_tile_counts(jax.random.fold_in(key_of[8], 71), 0)
    return {"features": features, "weight": weight, "bias": bias, "cotangent": cotangent, "tiles": tiles, "tile_rows": tile_rows, "tile_cols": tile_cols, "tile_counts": tile_counts}


def reference(features, weight, bias, cotangent, tiles, tile_rows, tile_cols, tile_counts):
    nodes = features.shape[0]
    feat_blocks = features.reshape(nodes // BLOCK, BLOCK, F)
    cells = jnp.arange(N_ROW * N_COL, dtype=jnp.int32)
    slot_ids = jnp.arange(TILES_CAP, dtype=jnp.int32)

    def cell_parts(index):
        row_pos = index // N_COL
        col_pos = index % N_COL
        tile_set = tiles[row_pos, col_pos].astype(jnp.float32)
        dest = (row_pos * BLK_ROWS + tile_rows[row_pos, col_pos]).astype(jnp.int32)
        source = (col_pos * BLK_COLS + tile_cols[row_pos, col_pos]).astype(jnp.int32)
        live = slot_ids < tile_counts[row_pos, col_pos]
        return (tile_set, dest, source, live)

    def forward_cell(total, index):
        tile_set, dest, source, live = cell_parts(index)
        contrib = jnp.einsum('tij,tjf->tif', tile_set, feat_blocks[source].astype(jnp.float32))
        contrib = jnp.where(live[:, None, None], contrib, jnp.zeros_like(contrib))
        return (total.at[dest].add(contrib), None)
    start_total = jnp.zeros((nodes // BLOCK, BLOCK, F), jnp.float32)
    total, unused = lax_scan(forward_cell, start_total, cells)
    aggregated = total.reshape(nodes, F).astype(jnp.bfloat16)
    preact = jnp.dot(aggregated, weight, preferred_element_type=jnp.float32) + bias.astype(jnp.float32)
    hidden = jax.nn.silu(preact).astype(jnp.bfloat16)
    sigma = jax.nn.sigmoid(preact)
    slope = sigma * (1.0 + preact * (1.0 - sigma))
    grad_pre = (cotangent.astype(jnp.float32) * slope).astype(jnp.bfloat16)
    factor = 1.0 / math.sqrt(nodes)
    grad_weight = jnp.dot(aggregated.T, grad_pre, preferred_element_type=jnp.float32) * factor
    grad_bias = lax.optimization_barrier(jnp.sum(grad_pre.astype(jnp.float32), axis=0)) * factor
    grad_agg = jnp.dot(grad_pre, weight.T, preferred_element_type=jnp.float32).astype(jnp.bfloat16)
    grad_blocks = grad_agg.reshape(nodes // BLOCK, BLOCK, F)

    def backward_cell(total_back, index):
        tile_set, dest, source, live = cell_parts(index)
        contrib = jnp.einsum('tji,tjf->tif', tile_set, grad_blocks[dest].astype(jnp.float32))
        contrib = jnp.where(live[:, None, None], contrib, jnp.zeros_like(contrib))
        return (total_back.at[source].add(contrib), None)
    total_back, unused = lax_scan(backward_cell, jnp.zeros((nodes // BLOCK, BLOCK, F), jnp.float32), cells)
    grad_features = total_back.reshape(nodes, F).astype(jnp.bfloat16)
    return (hidden, grad_weight, grad_bias, grad_features)

def lax_scan(function, carry, values):
    return jax.lax.scan(function, carry, values)
```

```python
import math

import jax
import jax.numpy as jnp
from jax import lax
from jax.experimental import pallas as pl
from jax.experimental.pallas import tpu as pltpu
from jax.sharding import PartitionSpec as P


def densify_kernel(count_ref, rows_ref, cols_ref, tiles_ref, cell_ref, present, zero, sem):
    slots, block, _ = tiles_ref.shape
    blocks_down = cell_ref.shape[0] // block
    blocks_across = cell_ref.shape[1] // block
    blocks = blocks_down * blocks_across

    def place(row, col):
        return cell_ref.at[
            pl.ds(pl.multiple_of(row * block, block), block),
            pl.ds(pl.multiple_of(col * block, block), block),
        ]

    def clear(index, carry):
        present[index] = 0
        return carry

    lax.fori_loop(0, blocks, clear, 0, unroll=8)
    zero[...] = jnp.zeros_like(zero)
    count = count_ref[0]

    def put_tile(slot, carry):
        row = rows_ref[slot]
        col = cols_ref[slot]
        present[row * blocks_across + col] = 1
        pltpu.make_async_copy(tiles_ref.at[slot], place(row, col), sem).start()
        return carry

    lax.fori_loop(0, count, put_tile, 0)

    def put_zero(index, carry):
        @pl.when(present[index] == 0)
        def _():
            row = index // blocks_across
            col = index % blocks_across
            pltpu.make_async_copy(zero, place(row, col), sem).start()

        return carry

    lax.fori_loop(0, blocks, put_zero, 0)

    def wait_one(index, carry):
        pltpu.make_async_copy(zero, place(0, 0), sem).wait()
        return carry

    lax.fori_loop(0, blocks, wait_one, 0)


def densify(tiles, rows, cols, count, blocks_down, blocks_across):
    block = tiles.shape[-1]
    shape = (blocks_down * block, blocks_across * block)
    size = shape[0] * shape[1] * 2
    return pl.pallas_call(
        densify_kernel,
        out_shape=jax.ShapeDtypeStruct(shape, tiles.dtype),
        in_specs=[
            pl.BlockSpec(memory_space=pltpu.SMEM),
            pl.BlockSpec(memory_space=pltpu.SMEM),
            pl.BlockSpec(memory_space=pltpu.SMEM),
            pl.BlockSpec(memory_space=pl.ANY),
        ],
        out_specs=pl.BlockSpec(memory_space=pl.ANY),
        scratch_shapes=[
            pltpu.SMEM((blocks_down * blocks_across,), jnp.int32),
            pltpu.VMEM((block, block), tiles.dtype),
            pltpu.SemaphoreType.DMA,
        ],
        cost_estimate=pl.CostEstimate(flops=0, bytes_accessed=2 * size, transcendentals=0),
        name="densify",
    )(count, rows, cols, tiles)


def swap(value, axis, mask):
    count = lax.axis_size(axis)
    return lax.ppermute(value, axis, [(i, i ^ mask) for i in range(count)])


def per_device(features, weight, bias, cotangent, tiles, tile_rows, tile_cols, tile_counts):
    tile_set = tiles[0, 0]
    block = tile_set.shape[-1]
    nodes, width = features.shape
    row_count = lax.axis_size("row")
    col_count = lax.axis_size("col")
    half = col_count // 2
    row_pos = lax.axis_index("row")
    col_pos = lax.axis_index("col")
    per = nodes // block
    factor = 1.0 / math.sqrt(nodes * row_count * col_count)
    f32 = jnp.float32
    bf16 = jnp.bfloat16

    down = (tile_rows[0, 0] // per) ^ col_pos
    down = (down & 1) * half + (down >> 1)
    rows = down * per + tile_rows[0, 0] % per
    across = (tile_cols[0, 0] // per) ^ row_pos
    cols = across * per + tile_cols[0, 0] % per

    panels = [features] + [swap(features, "row", k) for k in range(1, row_count)]
    cell = densify(
        tile_set, rows, cols, tile_counts[0], per * col_count, per * row_count
    )
    own_cell = cell[: half * nodes]
    mate_cell = cell[half * nodes :]
    source = jnp.concatenate(panels, axis=0)

    for_mate = jnp.dot(mate_cell, source, preferred_element_type=f32).astype(bf16)
    from_mate = swap(for_mate, "col", 1)
    own_part = jnp.dot(own_cell, source, preferred_element_type=f32)
    own_part = own_part + from_mate.astype(f32)
    total = own_part[:nodes]
    arrived = [
        swap(own_part[k * nodes : (k + 1) * nodes].astype(bf16), "col", 2 * k)
        for k in range(1, half)
    ]
    for part in arrived:
        total = total + part.astype(f32)

    aggregated = total.astype(bf16)
    preact = jnp.dot(aggregated, weight, preferred_element_type=f32) + bias
    sigma = jax.nn.sigmoid(preact)
    hidden = (preact * sigma).astype(bf16)
    slope = sigma * (1.0 + preact * (1.0 - sigma))
    grad_pre = (cotangent.astype(f32) * slope).astype(bf16)
    grad_agg = lax.dot_general(
        weight, grad_pre, (((1,), (1,)), ((), ())), preferred_element_type=f32
    ).astype(bf16)

    own_grads = [grad_agg] + [swap(grad_agg, "col", 2 * k) for k in range(1, half)]
    mate_grads = [swap(part, "col", 1) for part in own_grads]

    local_weight = jnp.einsum("nf,ng->fg", aggregated, grad_pre, preferred_element_type=f32)
    local_bias = jnp.sum(grad_pre.astype(f32), axis=0, keepdims=True)
    local = jnp.concatenate(
        [local_weight, jnp.broadcast_to(local_bias, (8, width))], axis=0
    )
    summed = lax.psum(local, ("row", "col")) * factor
    grad_weight = summed[:width]
    grad_bias = summed[width]

    back = jnp.dot(
        jnp.concatenate(own_grads, axis=1), own_cell, preferred_element_type=f32
    )
    back = back + jnp.dot(
        jnp.concatenate(mate_grads, axis=1), mate_cell, preferred_element_type=f32
    )
    result = back[:, :nodes]
    pieces = [
        swap(back[:, k * nodes : (k + 1) * nodes].astype(bf16), "row", k)
        for k in range(1, row_count)
    ]
    for piece in pieces:
        result = result + piece.astype(f32)
    grad_features = result.astype(bf16).T
    return (hidden, grad_weight, grad_bias, grad_features)


def solution(mesh):
    in_specs = (
        P(("col", "row"), None),
        P(),
        P(),
        P(("row", "col"), None),
        P("row", "col", None, None, None),
        P("row", "col", None),
        P("row", "col", None),
        P("row", "col"),
    )
    out_specs = (P(("row", "col"), None), P(), P(), P(("col", "row"), None))
    return jax.shard_map(
        per_device, mesh=mesh, in_specs=in_specs, out_specs=out_specs, check_vma=False
    )
```

```python
import math

import jax
import jax.numpy as jnp
from jax import lax
from jax.experimental import pallas as pl
from jax.experimental.pallas import tpu as pltpu
from jax.sharding import PartitionSpec as P

BF16 = jnp.bfloat16
F32 = jnp.float32


def densify_kernel(per, half, one_band, rows_ref, cols_ref, count_ref, tiles_ref, cell_ref):
    group, block, _ = tiles_ref.shape
    band = pl.program_id(0)
    step = pl.program_id(1)
    row_pos = lax.axis_index("row")
    col_pos = lax.axis_index("col")
    start = step * group

    @pl.when(step == 0)
    def _():
        def clear(index, carry):
            cell_ref[pl.ds(pl.multiple_of(index * block, block), block), :] = jnp.zeros(
                (block, cell_ref.shape[1]), cell_ref.dtype
            )
            return carry

        lax.fori_loop(0, cell_ref.shape[0] // block, clear, 0)

    def put(index):
        row = rows_ref[0, 0, start + index]
        col = cols_ref[0, 0, start + index]
        down = (row // per) ^ col_pos
        down = (down & 1) * half + (down >> 1)
        across = (col // per) ^ row_pos
        top = (down * per + row % per) * block - band * cell_ref.shape[0]
        left = (across * per + col % per) * block

        def store():
            cell_ref[
                pl.ds(pl.multiple_of(top, block), block),
                pl.ds(pl.multiple_of(left, block), block),
            ] = tiles_ref[index]

        if one_band:
            store()
        else:
            pl.when((top >= 0) & (top < cell_ref.shape[0]))(store)

    live = jnp.clip(count_ref[0, 0] - start, 0, group)

    def put_four(index, carry):
        for part in range(4):
            put(index * 4 + part)
        return carry

    lax.fori_loop(0, live // 4, put_four, 0)

    def put_one(index, carry):
        put(index)
        return carry

    lax.fori_loop(live // 4 * 4, live, put_one, 0)


def densify(tiles, rows, cols, count, per, col_count, row_count):
    slots, block, _ = tiles.shape
    group = math.gcd(slots, 32)
    shape = (per * col_count * block, per * row_count * block)
    size = shape[0] * shape[1] * 2
    bands = max(1, size >> 24)

    def tile_map(band, step, rows_ref, cols_ref, count_ref):
        last = jnp.maximum(count_ref[0, 0] - 1, 0) // group
        return (jnp.minimum(step, last), 0, 0)

    return pl.pallas_call(
        lambda *refs: densify_kernel(per, col_count // 2, bands == 1, *refs),
        out_shape=jax.ShapeDtypeStruct(shape, tiles.dtype),
        grid_spec=pltpu.PrefetchScalarGridSpec(
            num_scalar_prefetch=3,
            grid=(bands, slots // group),
            in_specs=[pl.BlockSpec((group, block, block), tile_map)],
            out_specs=pl.BlockSpec(
                (shape[0] // bands, shape[1]),
                lambda band, step, *refs: (band, 0),
                pipeline_mode=pl.Buffered(1),
            ),
        ),
        compiler_params=pltpu.CompilerParams(vmem_limit_bytes=size // bands + (8 << 20)),
        cost_estimate=pl.CostEstimate(
            flops=0, bytes_accessed=2 * size, transcendentals=0
        ),
        name="densify",
    )(rows, cols, count, tiles)


def dense_kernel(part_count, *refs):
    own_ref = refs[0]
    part_refs = refs[1 : 1 + part_count]
    weight_ref, bias_ref, cotangent_ref = refs[1 + part_count : 4 + part_count]
    hidden_ref, grad_ref, keep_ref, give_ref, local = refs[4 + part_count :]
    total = own_ref[...]
    for part_ref in part_refs:
        total = total + part_ref[...].astype(F32)
    aggregated = total.astype(BF16)
    weight = weight_ref[...]
    preact = jnp.dot(aggregated, weight, preferred_element_type=F32) + bias_ref[...]
    sigma = jax.nn.sigmoid(preact)
    hidden_ref[...] = (preact * sigma).astype(BF16)
    slope = sigma * (1.0 + preact * (1.0 - sigma))
    grad_pre = (cotangent_ref[...].astype(F32) * slope).astype(BF16)
    grad_ref[...] = lax.dot_general(
        weight, grad_pre, (((1,), (1,)), ((), ())), preferred_element_type=F32
    ).astype(BF16)
    width = weight.shape[0]
    local[:width] = lax.dot_general(
        aggregated, grad_pre, (((0,), (0,)), ((), ())), preferred_element_type=F32
    )
    local[width:] = jnp.broadcast_to(
        jnp.sum(grad_pre.astype(F32), axis=0, keepdims=True),
        (local.shape[0] - width, width),
    )
    rows = local.shape[0] // 2
    core = lax.axis_index("col") % 2
    keep_ref[...] = local[pl.ds(pl.multiple_of(core * rows, 8), rows)]
    give_ref[...] = local[pl.ds(pl.multiple_of((1 - core) * rows, 8), rows)]


def dense(own, parts, weight, bias, cotangent):
    nodes, width = own.shape
    rows = width // 2 + 16
    spec = pl.BlockSpec(memory_space=pltpu.VMEM)
    shapes = (
        jax.ShapeDtypeStruct((nodes, width), BF16),
        jax.ShapeDtypeStruct((width, nodes), BF16),
        jax.ShapeDtypeStruct((rows, width), F32),
        jax.ShapeDtypeStruct((rows, width), F32),
    )
    return pl.pallas_call(
        lambda *refs: dense_kernel(len(parts), *refs),
        out_shape=shapes,
        in_specs=[spec] * (4 + len(parts)),
        out_specs=(spec,) * 4,
        scratch_shapes=[pltpu.VMEM((2 * rows, width), F32)],
        compiler_params=pltpu.CompilerParams(vmem_limit_bytes=16 << 20),
        cost_estimate=pl.CostEstimate(
            flops=6 * nodes * width * width,
            bytes_accessed=8 * nodes * width,
            transcendentals=nodes * width,
        ),
        name="dense",
    )(own, *parts, weight, bias.reshape(1, width), cotangent)


def swap(value, axis, mask):
    count = lax.axis_size(axis)
    return lax.ppermute(value, axis, [(i, i ^ mask) for i in range(count)])


def tree_sum(values):
    values = [value.astype(F32) for value in values]
    while len(values) > 1:
        values = [a + b for a, b in zip(values[::2], values[1::2])]
    return values[0]


def reduce_weight(keep, give, factor):
    row_count = lax.axis_size("row")
    half = lax.axis_size("col") // 2
    part = (keep + swap(give, "col", 1)).astype(BF16)
    part = tree_sum([part] + [swap(part, "row", k) for k in range(1, row_count)])
    part = part.astype(BF16)
    part = tree_sum([part] + [swap(part, "col", 2 * k) for k in range(1, half)])
    part = part * factor
    other = swap(part, "col", 1)
    first = lax.axis_index("col") % 2 == 0
    return jnp.concatenate(
        [jnp.where(first, part, other), jnp.where(first, other, part)], axis=0
    )


def per_device(features, weight, bias, cotangent, tiles, tile_rows, tile_cols, tile_counts):
    block = tiles.shape[-1]
    nodes, width = features.shape
    row_count = lax.axis_size("row")
    col_count = lax.axis_size("col")
    half = col_count // 2
    factor = 1.0 / math.sqrt(nodes * row_count * col_count)

    panels = [features] + [swap(features, "row", k) for k in range(1, row_count)]
    cell = densify(
        tiles[0, 0], tile_rows, tile_cols, tile_counts, nodes // block, col_count, row_count
    )

    def cell_rows(core, k):
        top = (core * half + k) * nodes
        return cell[top : top + nodes]

    source = jnp.concatenate(panels, axis=0)
    for_mate = jnp.dot(cell[half * nodes :], source, preferred_element_type=F32)
    from_mate = swap(for_mate.astype(BF16), "col", 1)

    def own_part(k):
        value = jnp.dot(cell_rows(0, k), source, preferred_element_type=F32)
        return value + from_mate[k * nodes : (k + 1) * nodes].astype(F32)

    arrived = [swap(own_part(k).astype(BF16), "col", 2 * k) for k in range(1, half)]
    hidden, grad_agg, keep, give = dense(own_part(0), arrived, weight, bias, cotangent)

    own_grads = [grad_agg] + [swap(grad_agg, "col", 2 * k) for k in range(1, half)]
    mate_grads = [swap(part, "col", 1) for part in own_grads]
    summed = reduce_weight(keep, give, factor)

    back = jnp.dot(own_grads[0], cell_rows(0, 0), preferred_element_type=F32)
    for k in range(1, half):
        back = back + jnp.dot(own_grads[k], cell_rows(0, k), preferred_element_type=F32)
    for k in range(half):
        back = back + jnp.dot(mate_grads[k], cell_rows(1, k), preferred_element_type=F32)
    result = back[:, :nodes]
    pieces = [
        swap(back[:, k * nodes : (k + 1) * nodes].astype(BF16), "row", k)
        for k in range(1, row_count)
    ]
    for piece in pieces:
        result = result + piece.astype(F32)
    grad_features = result.astype(BF16).T
    return (hidden, summed[:width], summed[width], grad_features)


def solution(mesh):
    in_specs = (
        P(("col", "row"), None),
        P(),
        P(),
        P(("row", "col"), None),
        P("row", "col", None, None, None),
        P("row", "col", None),
        P("row", "col", None),
        P("row", "col"),
    )
    out_specs = (P(("row", "col"), None), P(), P(), P(("col", "row"), None))
    return jax.shard_map(
        per_device, mesh=mesh, in_specs=in_specs, out_specs=out_specs, check_vma=False
    )
```

```python
import math

import jax
import jax.numpy as jnp
from jax import lax
from jax.experimental import pallas as pl
from jax.experimental.pallas import tpu as pltpu
from jax.sharding import PartitionSpec as P

BF16 = jnp.bfloat16
F32 = jnp.float32
CELL_IN_VMEM = 1 << 24


def densify_kernel(per, half, one_band, rows_ref, cols_ref, count_ref, tiles_ref, cell_ref):
    group, block, _ = tiles_ref.shape
    band = pl.program_id(0)
    step = pl.program_id(1)
    row_pos = lax.axis_index("row")
    col_pos = lax.axis_index("col")
    start = step * group

    @pl.when(step == 0)
    def _():
        def clear(index, carry):
            cell_ref[pl.ds(pl.multiple_of(index * block, block), block), :] = jnp.zeros(
                (block, cell_ref.shape[1]), cell_ref.dtype
            )
            return carry

        lax.fori_loop(0, cell_ref.shape[0] // block, clear, 0)

    def put(index):
        row = rows_ref[0, 0, start + index]
        col = cols_ref[0, 0, start + index]
        panel = lax.div(row, per)
        down = panel ^ col_pos
        down = (down & 1) * half + (down >> 1)
        top = ((down - panel) * per + row) * block - band * cell_ref.shape[0]
        panel = lax.div(col, per)
        left = (((panel ^ row_pos) - panel) * per + col) * block

        def store():
            cell_ref[
                pl.ds(pl.multiple_of(top, block), block),
                pl.ds(pl.multiple_of(left, block), block),
            ] = tiles_ref[index]

        if one_band:
            store()
        else:
            pl.when((top >= 0) & (top < cell_ref.shape[0]))(store)

    live = jnp.clip(count_ref[0, 0] - start, 0, group)

    def put_eight(index, carry):
        for part in range(8):
            put(index * 8 + part)
        return carry

    lax.fori_loop(0, live >> 3, put_eight, 0)

    def put_one(index, carry):
        put(index)
        return carry

    lax.fori_loop((live >> 3) << 3, live, put_one, 0)


def densify(tiles, rows, cols, count, per, col_count, row_count):
    slots, block, _ = tiles.shape
    group = math.gcd(slots, 32)
    shape = (per * col_count * block, per * row_count * block)
    size = shape[0] * shape[1] * 2
    bands = max(1, size // CELL_IN_VMEM)
    space = pltpu.VMEM if bands == 1 else pltpu.HBM

    def tile_map(band, step, rows_ref, cols_ref, count_ref):
        last = jnp.maximum(count_ref[0, 0] - 1, 0) // group
        return (jnp.minimum(step, last), 0, 0)

    return pl.pallas_call(
        lambda *refs: densify_kernel(per, col_count // 2, bands == 1, *refs),
        out_shape=space(shape, tiles.dtype),
        grid_spec=pltpu.PrefetchScalarGridSpec(
            num_scalar_prefetch=3,
            grid=(bands, slots // group),
            in_specs=[pl.BlockSpec((group, block, block), tile_map)],
            out_specs=pl.BlockSpec(
                (shape[0] // bands, shape[1]),
                lambda band, step, *refs: (band, 0),
                pipeline_mode=pl.Buffered(1),
            ),
        ),
        compiler_params=pltpu.CompilerParams(vmem_limit_bytes=size // bands + (8 << 20)),
        cost_estimate=pl.CostEstimate(
            flops=0, bytes_accessed=2 * size, transcendentals=0
        ),
        name="densify",
    )(rows, cols, count, pltpu.with_memory_space_constraint(tiles, pltpu.HBM))


def dense_kernel(part_count, *refs):
    own_ref = refs[0]
    part_refs = refs[1 : 1 + part_count]
    weight_ref, bias_ref, cotangent_ref = refs[1 + part_count : 4 + part_count]
    hidden_ref, grad_ref, local_ref = refs[4 + part_count :]
    total = own_ref[...]
    for part_ref in part_refs:
        total = total + part_ref[...].astype(F32)
    aggregated = total.astype(BF16)
    weight = weight_ref[...]
    preact = jnp.dot(aggregated, weight, preferred_element_type=F32) + bias_ref[...]
    sigma = jax.nn.sigmoid(preact)
    hidden_ref[...] = (preact * sigma).astype(BF16)
    slope = sigma * (1.0 + preact * (1.0 - sigma))
    grad_pre = (cotangent_ref[...].astype(F32) * slope).astype(BF16)
    grad_ref[...] = lax.dot_general(
        weight, grad_pre, (((1,), (1,)), ((), ())), preferred_element_type=F32
    ).astype(BF16)
    width = weight.shape[0]
    local_ref[:width] = lax.dot_general(
        aggregated, grad_pre, (((0,), (0,)), ((), ())), preferred_element_type=F32
    )
    local_ref[width:] = jnp.broadcast_to(
        jnp.sum(grad_pre.astype(F32), axis=0, keepdims=True),
        (local_ref.shape[0] - width, width),
    )


def dense(own, parts, weight, bias, cotangent):
    nodes, width = own.shape
    spec = pl.BlockSpec(memory_space=pltpu.VMEM)
    shapes = (
        jax.ShapeDtypeStruct((nodes, width), BF16),
        jax.ShapeDtypeStruct((width, nodes), BF16),
        jax.ShapeDtypeStruct((width + 16, width), F32),
    )
    return pl.pallas_call(
        lambda *refs: dense_kernel(len(parts), *refs),
        out_shape=shapes,
        in_specs=[spec] * (4 + len(parts)),
        out_specs=(spec,) * 3,
        compiler_params=pltpu.CompilerParams(vmem_limit_bytes=16 << 20),
        cost_estimate=pl.CostEstimate(
            flops=6 * nodes * width * width,
            bytes_accessed=8 * nodes * width,
            transcendentals=nodes * width,
        ),
        name="dense",
    )(own, *parts, weight, bias.reshape(1, width), cotangent)


def back_own_kernel(*refs):
    *grad_refs, cell_ref, total_ref = refs
    width, nodes = grad_refs[0].shape
    grads = jnp.concatenate([ref[...] for ref in grad_refs], axis=1)
    for left in range(0, total_ref.shape[1], nodes):
        total_ref[:, left : left + nodes] = jnp.dot(
            grads,
            cell_ref[: grads.shape[1], left : left + nodes],
            preferred_element_type=F32,
        )


def back_mate_kernel(chosen, *refs):
    total_ref, cell_ref = refs[:2]
    grad_refs = refs[2 : -len(chosen)]
    out_refs = refs[-len(chosen) :]
    width, nodes = grad_refs[0].shape
    grads = jnp.concatenate([ref[...] for ref in grad_refs], axis=1)
    for panel, out_ref in zip(chosen, out_refs):
        columns = slice(panel * nodes, (panel + 1) * nodes)
        value = total_ref[:, columns] + jnp.dot(
            grads, cell_ref[grads.shape[1] :, columns], preferred_element_type=F32
        )
        out_ref[...] = value.T.astype(out_ref.dtype)


def back_call(kernel, outs, operands, flops, name):
    spec = pl.BlockSpec(memory_space=pltpu.VMEM)
    return pl.pallas_call(
        kernel,
        out_shape=outs,
        in_specs=[spec] * len(operands),
        out_specs=[spec] * len(outs),
        compiler_params=pltpu.CompilerParams(vmem_limit_bytes=24 << 20),
        cost_estimate=pl.CostEstimate(
            flops=flops, bytes_accessed=flops // 512, transcendentals=0
        ),
        name=name,
    )(*operands)


def back_own(grads, cell):
    width = grads[0].shape[0]
    columns = cell.shape[1]
    outs = (pltpu.VMEM((width, columns), F32),)
    flops = cell.shape[0] * columns * width
    return back_call(back_own_kernel, outs, (*grads, cell), flops, "back_own")[0]


def back_mate(chosen, total, cell, grads):
    width, nodes = grads[0].shape
    outs = tuple(
        pltpu.VMEM((nodes, width), F32 if panel == 0 else BF16) for panel in chosen
    )
    flops = cell.shape[0] * nodes * len(chosen) * width
    kernel = lambda *refs: back_mate_kernel(chosen, *refs)
    return back_call(kernel, outs, (total, cell, *grads), flops, "back_mate")


def swap(value, axis, mask):
    count = lax.axis_size(axis)
    return lax.ppermute(value, axis, [(i, i ^ mask) for i in range(count)])


def tree_sum(values):
    values = [value.astype(F32) for value in values]
    while len(values) > 1:
        values = [a + b for a, b in zip(values[::2], values[1::2])]
    return values[0]


def sum_over(value, axis, masks):
    return tree_sum([value] + [swap(value, axis, mask) for mask in masks])


def per_device(features, weight, bias, cotangent, tiles, tile_rows, tile_cols, tile_counts):
    block = tiles.shape[-1]
    nodes, width = features.shape
    row_count = lax.axis_size("row")
    col_count = lax.axis_size("col")
    half = col_count // 2
    factor = 1.0 / math.sqrt(nodes * row_count * col_count)

    panels = [features] + [swap(features, "row", k) for k in range(1, row_count)]
    cell = densify(
        tiles[0, 0], tile_rows, tile_cols, tile_counts, nodes // block, col_count, row_count
    )

    def cell_rows(core, k):
        top = (core * half + k) * nodes
        return cell[top : top + nodes]

    source = jnp.concatenate(panels, axis=0)

    def cell_product(core, k):
        return jnp.dot(cell_rows(core, k), source, preferred_element_type=F32)

    order = list(range(half - 1, -1, -1))
    from_mate = {k: swap(cell_product(1, k).astype(BF16), "col", 1) for k in order}
    own_part = {k: cell_product(0, k) + from_mate[k].astype(F32) for k in order}
    arrived = [swap(own_part[k].astype(BF16), "col", 2 * k) for k in range(1, half)]
    hidden, grad_agg, local = dense(own_part[0], arrived, weight, bias, cotangent)

    own_grads = [grad_agg] + [swap(grad_agg, "col", 2 * k) for k in range(1, half)]
    local, own_grads[1] = lax.optimization_barrier((local, own_grads[1]))
    mate_grads = [swap(part, "col", 1) for part in own_grads]
    part = sum_over(local, "col", [1]).astype(BF16)
    part = sum_over(part, "row", range(1, row_count)).astype(BF16)

    if cell.size * 2 <= CELL_IN_VMEM:
        total = back_own(own_grads, cell)
        pieces = {}
        rest = total
        for chosen in ([row_count - 1], list(range(row_count - 2, 0, -1)), [0]):
            pieces.update(zip(chosen, back_mate(chosen, rest, cell, mate_grads)))
            rest, pieces[chosen[-1]] = lax.optimization_barrier((total, pieces[chosen[-1]]))
    else:
        own = jnp.concatenate(own_grads, axis=1)
        mate = jnp.concatenate(mate_grads, axis=1)
        total = jnp.dot(own, cell[: half * nodes], preferred_element_type=F32)
        total = total + jnp.dot(mate, cell[half * nodes :], preferred_element_type=F32)
        pieces = {
            k: total[:, k * nodes : (k + 1) * nodes].T.astype(F32 if k == 0 else BF16)
            for k in range(row_count)
        }
    part, pieces[1] = lax.optimization_barrier((part, pieces[1]))
    landed = {k: swap(pieces[k], "row", k) for k in range(row_count - 1, 0, -1)}
    result = pieces[0]
    for k in range(1, row_count):
        result = result + landed[k].astype(F32)
    summed = sum_over(part, "col", range(2, col_count, 2)) * factor
    return (hidden, summed[:width], summed[width], result.astype(BF16))


def solution(mesh):
    in_specs = (
        P(("col", "row"), None),
        P(),
        P(),
        P(("row", "col"), None),
        P("row", "col", None, None, None),
        P("row", "col", None),
        P("row", "col", None),
        P("row", "col"),
    )
    out_specs = (P(("row", "col"), None), P(), P(), P(("col", "row"), None))
    return jax.shard_map(
        per_device, mesh=mesh, in_specs=in_specs, out_specs=out_specs, check_vma=False
    )
```

```python
import math

import jax
import jax.numpy as jnp
from jax import lax
from jax.experimental import pallas as pl
from jax.experimental.pallas import tpu as pltpu
from jax.sharding import PartitionSpec as P

BF16 = jnp.bfloat16
F32 = jnp.float32
CELL_IN_VMEM = 1 << 24


def densify_kernel(per, half, one_band, rows_ref, cols_ref, count_ref, tiles_ref, cell_ref):
    group, block, _ = tiles_ref.shape
    band = pl.program_id(0)
    step = pl.program_id(1)
    row_pos = lax.axis_index("row")
    col_pos = lax.axis_index("col")
    start = step * group

    @pl.when(step == 0)
    def _():
        def clear(index, carry):
            cell_ref[pl.ds(pl.multiple_of(index * block, block), block), :] = jnp.zeros(
                (block, cell_ref.shape[1]), cell_ref.dtype
            )
            return carry

        lax.fori_loop(0, cell_ref.shape[0] // block, clear, 0)

    def put(first, number):
        places = []
        for index in range(number):
            row = rows_ref[0, 0, start + first + index]
            col = cols_ref[0, 0, start + first + index]
            panel = lax.div(row, per)
            down = panel ^ col_pos
            down = (down & 1) * half + (down >> 1)
            top = ((down - panel) * per + row) * block - band * cell_ref.shape[0]
            panel = lax.div(col, per)
            left = (((panel ^ row_pos) - panel) * per + col) * block
            places.append((top, left))
        values = [tiles_ref[first + index] for index in range(number)]
        for (top, left), value in zip(places, values):

            def store(top=top, left=left, value=value):
                cell_ref[
                    pl.ds(pl.multiple_of(top, block), block),
                    pl.ds(pl.multiple_of(left, block), block),
                ] = value

            if one_band:
                store()
            else:
                pl.when((top >= 0) & (top < cell_ref.shape[0]))(store)

    live = jnp.clip(count_ref[0, 0] - start, 0, group)

    def put_four(index, carry):
        put(index * 4, 4)
        return carry

    lax.fori_loop(0, live >> 2, put_four, 0)

    def put_one(index, carry):
        put(index, 1)
        return carry

    lax.fori_loop((live >> 2) << 2, live, put_one, 0)


def densify(tiles, rows, cols, count, per, col_count, row_count):
    slots, block, _ = tiles.shape
    group = math.gcd(slots, 32)
    shape = (per * col_count * block, per * row_count * block)
    size = shape[0] * shape[1] * 2
    bands = max(1, size // CELL_IN_VMEM)
    space = pltpu.VMEM if bands == 1 else pltpu.HBM

    def tile_map(band, step, rows_ref, cols_ref, count_ref):
        last = jnp.maximum(count_ref[0, 0] - 1, 0) // group
        return (jnp.minimum(step, last), 0, 0)

    return pl.pallas_call(
        lambda *refs: densify_kernel(per, col_count // 2, bands == 1, *refs),
        out_shape=space(shape, tiles.dtype),
        grid_spec=pltpu.PrefetchScalarGridSpec(
            num_scalar_prefetch=3,
            grid=(bands, slots // group),
            in_specs=[pl.BlockSpec((group, block, block), tile_map)],
            out_specs=pl.BlockSpec(
                (shape[0] // bands, shape[1]),
                lambda band, step, *refs: (band, 0),
                pipeline_mode=pl.Buffered(1),
            ),
        ),
        compiler_params=pltpu.CompilerParams(vmem_limit_bytes=size // bands + (8 << 20)),
        cost_estimate=pl.CostEstimate(
            flops=0, bytes_accessed=2 * size, transcendentals=0
        ),
        name="densify",
    )(
        pltpu.with_memory_space_constraint(rows, pltpu.HBM),
        pltpu.with_memory_space_constraint(cols, pltpu.HBM),
        count,
        pltpu.with_memory_space_constraint(tiles, pltpu.HBM),
    )


def dense_kernel(part_count, *refs):
    own_ref = refs[0]
    part_refs = refs[1 : 1 + part_count]
    weight_ref, bias_ref, cotangent_ref = refs[1 + part_count : 4 + part_count]
    hidden_ref, grad_ref, local_ref = refs[4 + part_count :]
    total = own_ref[...]
    for part_ref in part_refs:
        total = total + part_ref[...].astype(F32)
    aggregated = total.astype(BF16)
    weight = weight_ref[...]
    preact = jnp.dot(aggregated, weight, preferred_element_type=F32) + bias_ref[...]
    sigma = jax.nn.sigmoid(preact)
    hidden_ref[...] = (preact * sigma).astype(BF16)
    slope = sigma * (1.0 + preact * (1.0 - sigma))
    grad_pre = (cotangent_ref[...].astype(F32) * slope).astype(BF16)
    grad_ref[...] = lax.dot_general(
        weight, grad_pre, (((1,), (1,)), ((), ())), preferred_element_type=F32
    ).astype(BF16)
    width = weight.shape[0]
    local_ref[:width] = lax.dot_general(
        aggregated, grad_pre, (((0,), (0,)), ((), ())), preferred_element_type=F32
    )
    local_ref[width:] = jnp.broadcast_to(
        jnp.sum(grad_pre.astype(F32), axis=0, keepdims=True),
        (local_ref.shape[0] - width, width),
    )


def dense(own, parts, weight, bias, cotangent):
    nodes, width = own.shape
    spec = pl.BlockSpec(memory_space=pltpu.VMEM)
    shapes = (
        jax.ShapeDtypeStruct((nodes, width), BF16),
        jax.ShapeDtypeStruct((width, nodes), BF16),
        jax.ShapeDtypeStruct((width + 16, width), F32),
    )
    return pl.pallas_call(
        lambda *refs: dense_kernel(len(parts), *refs),
        out_shape=shapes,
        in_specs=[spec] * (4 + len(parts)),
        out_specs=(spec,) * 3,
        compiler_params=pltpu.CompilerParams(vmem_limit_bytes=16 << 20),
        cost_estimate=pl.CostEstimate(
            flops=6 * nodes * width * width,
            bytes_accessed=8 * nodes * width,
            transcendentals=nodes * width,
        ),
        name="dense",
    )(own, *parts, weight, bias.reshape(1, width), cotangent)


def back_own_kernel(*refs):
    *grad_refs, cell_ref, total_ref = refs
    width, nodes = grad_refs[0].shape
    grads = jnp.concatenate([ref[...] for ref in grad_refs], axis=1)
    for left in range(0, total_ref.shape[1], nodes):
        total_ref[:, left : left + nodes] = jnp.dot(
            grads,
            cell_ref[: grads.shape[1], left : left + nodes],
            preferred_element_type=F32,
        )


def back_mate_kernel(chosen, *refs):
    total_ref, cell_ref = refs[:2]
    grad_refs = refs[2 : -len(chosen)]
    out_refs = refs[-len(chosen) :]
    width, nodes = grad_refs[0].shape
    grads = jnp.concatenate([ref[...] for ref in grad_refs], axis=1)
    for panel, out_ref in zip(chosen, out_refs):
        columns = slice(panel * nodes, (panel + 1) * nodes)
        value = total_ref[:, columns] + jnp.dot(
            grads, cell_ref[grads.shape[1] :, columns], preferred_element_type=F32
        )
        out_ref[...] = value.T.astype(out_ref.dtype)


def back_call(kernel, outs, operands, flops, name):
    spec = pl.BlockSpec(memory_space=pltpu.VMEM)
    return pl.pallas_call(
        kernel,
        out_shape=outs,
        in_specs=[spec] * len(operands),
        out_specs=[spec] * len(outs),
        compiler_params=pltpu.CompilerParams(vmem_limit_bytes=24 << 20),
        cost_estimate=pl.CostEstimate(
            flops=flops, bytes_accessed=flops // 512, transcendentals=0
        ),
        name=name,
    )(*operands)


def back_own(grads, cell):
    width = grads[0].shape[0]
    columns = cell.shape[1]
    outs = (pltpu.VMEM((width, columns), F32),)
    flops = 16 * cell.shape[0] * columns * width
    return back_call(back_own_kernel, outs, (*grads, cell), flops, "back_own")[0]


def back_mate(chosen, total, cell, grads):
    width, nodes = grads[0].shape
    outs = tuple(
        pltpu.VMEM((nodes, width), F32 if panel == 0 else BF16) for panel in chosen
    )
    flops = cell.shape[0] * nodes * len(chosen) * width
    kernel = lambda *refs: back_mate_kernel(chosen, *refs)
    return back_call(kernel, outs, (total, cell, *grads), flops, "back_mate")


def finish_kernel(factor, part_count, *refs):
    own_ref = refs[0]
    part_refs = refs[1 : 1 + part_count]
    weight_refs = refs[1 + part_count : -3]
    out_ref, weight_ref, bias_ref = refs[-3:]
    value = own_ref[...]
    for part_ref in part_refs:
        value = value + part_ref[...].astype(F32)
    out_ref[...] = value.astype(out_ref.dtype)
    summed = tree_sum([ref[...] for ref in weight_refs]) * factor
    width = weight_ref.shape[0]
    weight_ref[...] = summed[:width]
    bias_ref[...] = summed[width : width + 1]


def finish(own, parts, weight_parts, factor):
    spec = pl.BlockSpec(memory_space=pltpu.VMEM)
    width = own.shape[1]
    return pl.pallas_call(
        lambda *refs: finish_kernel(factor, len(parts), *refs),
        out_shape=(
            jax.ShapeDtypeStruct(own.shape, BF16),
            jax.ShapeDtypeStruct((width, width), F32),
            jax.ShapeDtypeStruct((1, width), F32),
        ),
        in_specs=[spec] * (1 + len(parts) + len(weight_parts)),
        out_specs=(spec,) * 3,
        compiler_params=pltpu.CompilerParams(vmem_limit_bytes=16 << 20),
        cost_estimate=pl.CostEstimate(
            flops=8 * own.size, bytes_accessed=16 * own.size, transcendentals=0
        ),
        name="finish",
    )(own, *parts, *weight_parts)


def swap(value, axis, mask):
    count = lax.axis_size(axis)
    return lax.ppermute(value, axis, [(i, i ^ mask) for i in range(count)])


def tree_sum(values):
    values = [value.astype(F32) for value in values]
    while len(values) > 1:
        values = [a + b for a, b in zip(values[::2], values[1::2])]
    return values[0]


def sum_over(value, axis, masks):
    return tree_sum([value] + [swap(value, axis, mask) for mask in masks])


def per_device(features, weight, bias, cotangent, tiles, tile_rows, tile_cols, tile_counts):
    block = tiles.shape[-1]
    nodes, width = features.shape
    row_count = lax.axis_size("row")
    col_count = lax.axis_size("col")
    half = col_count // 2
    factor = 1.0 / math.sqrt(nodes * row_count * col_count)

    panels = [features] + [swap(features, "row", k) for k in range(1, row_count)]
    cell = densify(
        tiles[0, 0], tile_rows, tile_cols, tile_counts, nodes // block, col_count, row_count
    )

    def cell_rows(core, k):
        top = (core * half + k) * nodes
        return cell[top : top + nodes]

    source = jnp.concatenate(panels, axis=0)

    def cell_product(core, k):
        return jnp.dot(cell_rows(core, k), source, preferred_element_type=F32)

    order = list(range(half - 1, -1, -1))
    from_mate = {k: swap(cell_product(1, k).astype(BF16), "col", 1) for k in order}
    own_part = {k: cell_product(0, k) + from_mate[k].astype(F32) for k in order}
    arrived = [swap(own_part[k].astype(BF16), "col", 2 * k) for k in range(1, half)]
    hidden, grad_agg, local = dense(own_part[0], arrived, weight, bias, cotangent)

    own_grads = [grad_agg] + [swap(grad_agg, "col", 2 * k) for k in range(1, half)]
    mate_grads = [swap(part, "col", 1) for part in own_grads]
    part = sum_over(local, "col", [1]).astype(BF16)
    part, own_grads[1] = lax.optimization_barrier((part, own_grads[1]))
    part = sum_over(part, "row", range(1, row_count)).astype(BF16)
    part, mate_grads[0] = lax.optimization_barrier((part, mate_grads[0]))

    if cell.size * 2 <= CELL_IN_VMEM:
        total = back_own(own_grads, cell)
        pieces = {}
        rest = total
        for chosen in ([row_count - 1], list(range(row_count - 2, 0, -1)), [0]):
            pieces.update(zip(chosen, back_mate(chosen, rest, cell, mate_grads)))
            rest, pieces[chosen[-1]] = lax.optimization_barrier((total, pieces[chosen[-1]]))
    else:
        own = jnp.concatenate(own_grads, axis=1)
        mate = jnp.concatenate(mate_grads, axis=1)
        total = jnp.dot(own, cell[: half * nodes], preferred_element_type=F32)
        total = total + jnp.dot(mate, cell[half * nodes :], preferred_element_type=F32)
        pieces = {
            k: total[:, k * nodes : (k + 1) * nodes].T.astype(F32 if k == 0 else BF16)
            for k in range(row_count)
        }
    part, pieces[1] = lax.optimization_barrier((part, pieces[1]))
    landed = [swap(pieces[k], "row", k) for k in range(row_count - 1, 0, -1)]
    parts = [part] + [swap(part, "col", mask) for mask in range(2, col_count, 2)]
    grad_features, grad_weight, grad_bias = finish(pieces[0], landed, parts, factor)
    return (hidden, grad_weight, grad_bias[0], grad_features)


def solution(mesh):
    in_specs = (
        P(("col", "row"), None),
        P(),
        P(),
        P(("row", "col"), None),
        P("row", "col", None, None, None),
        P("row", "col", None),
        P("row", "col", None),
        P("row", "col"),
    )
    out_specs = (P(("row", "col"), None), P(), P(), P(("col", "row"), None))
    return jax.shard_map(
        per_device, mesh=mesh, in_specs=in_specs, out_specs=out_specs, check_vma=False
    )
```

```python
import math

import jax
import jax.numpy as jnp
from jax import lax
from jax.experimental import pallas as pl
from jax.experimental.pallas import tpu as pltpu
from jax.sharding import PartitionSpec as P

BF16 = jnp.bfloat16
F32 = jnp.float32
CELL_IN_VMEM = 1 << 24


def densify_kernel(per, half, one_band, rows_ref, cols_ref, count_ref, *refs):
    *window_refs, cell_ref = refs
    group, block, _ = window_refs[0].shape
    band = pl.program_id(0)
    step = pl.program_id(1)
    row_pos = lax.axis_index("row")
    col_pos = lax.axis_index("col")

    @pl.when(step == 0)
    def _():
        def clear(index, carry):
            cell_ref[pl.ds(pl.multiple_of(index * block, block), block), :] = jnp.zeros(
                (block, cell_ref.shape[1]), cell_ref.dtype
            )
            return carry

        lax.fori_loop(0, cell_ref.shape[0] // block, clear, 0)

    def put(window_ref, start, first, number):
        places = []
        for index in range(number):
            row = rows_ref[0, 0, start + first + index]
            col = cols_ref[0, 0, start + first + index]
            panel = lax.div(row, per)
            down = panel ^ col_pos
            down = (down & 1) * half + (down >> 1)
            top = ((down - panel) * per + row) * block - band * cell_ref.shape[0]
            panel = lax.div(col, per)
            left = (((panel ^ row_pos) - panel) * per + col) * block
            places.append((top, left))
        values = [window_ref[first + index] for index in range(number)]
        for (top, left), value in zip(places, values):

            def store(top=top, left=left, value=value):
                cell_ref[
                    pl.ds(pl.multiple_of(top, block), block),
                    pl.ds(pl.multiple_of(left, block), block),
                ] = value

            if one_band:
                store()
            else:
                pl.when((top >= 0) & (top < cell_ref.shape[0]))(store)

    for part, window_ref in enumerate(window_refs):
        start = (step * len(window_refs) + part) * group
        live = jnp.clip(count_ref[0, 0] - start, 0, group)

        def put_four(index, carry, window_ref=window_ref, start=start):
            put(window_ref, start, index * 4, 4)
            return carry

        lax.fori_loop(0, live >> 2, put_four, 0)

        def put_one(index, carry, window_ref=window_ref, start=start):
            put(window_ref, start, index, 1)
            return carry

        lax.fori_loop((live >> 2) << 2, live, put_one, 0)


def densify(tiles, rows, cols, count, per, col_count, row_count):
    slots, block, _ = tiles.shape
    group = math.gcd(slots, 32)
    windows = math.gcd(slots // group, 3)
    shape = (per * col_count * block, per * row_count * block)
    size = shape[0] * shape[1] * 2
    bands = max(1, size // CELL_IN_VMEM)
    space = pltpu.VMEM if bands == 1 else pltpu.HBM

    def tile_spec(part):
        def tile_map(band, step, rows_ref, cols_ref, count_ref):
            last = jnp.maximum(count_ref[0, 0] - 1, 0) // group
            return (jnp.minimum(step * windows + part, last), 0, 0)

        return pl.BlockSpec((group, block, block), tile_map)

    tiles = pltpu.with_memory_space_constraint(tiles, pltpu.HBM)
    return pl.pallas_call(
        lambda *refs: densify_kernel(per, col_count // 2, bands == 1, *refs),
        out_shape=space(shape, tiles.dtype),
        grid_spec=pltpu.PrefetchScalarGridSpec(
            num_scalar_prefetch=3,
            grid=(bands, slots // (group * windows)),
            in_specs=[tile_spec(part) for part in range(windows)],
            out_specs=pl.BlockSpec(
                (shape[0] // bands, shape[1]),
                lambda band, step, *refs: (band, 0),
                pipeline_mode=pl.Buffered(1),
            ),
        ),
        compiler_params=pltpu.CompilerParams(
            vmem_limit_bytes=size // bands + (10 << 20)
        ),
        cost_estimate=pl.CostEstimate(
            flops=0, bytes_accessed=2 * size, transcendentals=0
        ),
        name="densify",
    )(
        pltpu.with_memory_space_constraint(rows, pltpu.HBM),
        pltpu.with_memory_space_constraint(cols, pltpu.HBM),
        count,
        *[tiles] * windows,
    )


def dense_kernel(part_count, *refs):
    own_ref = refs[0]
    part_refs = refs[1 : 1 + part_count]
    weight_ref, bias_ref, cotangent_ref = refs[1 + part_count : 4 + part_count]
    hidden_ref, grad_ref, local_ref = refs[4 + part_count :]
    total = own_ref[...]
    for part_ref in part_refs:
        total = total + part_ref[...].astype(F32)
    aggregated = total.astype(BF16)
    weight = weight_ref[...]
    preact = jnp.dot(aggregated, weight, preferred_element_type=F32) + bias_ref[...]
    sigma = jax.nn.sigmoid(preact)
    hidden_ref[...] = (preact * sigma).astype(BF16)
    slope = sigma * (1.0 + preact * (1.0 - sigma))
    grad_pre = (cotangent_ref[...].astype(F32) * slope).astype(BF16)
    grad_ref[...] = lax.dot_general(
        weight, grad_pre, (((1,), (1,)), ((), ())), preferred_element_type=F32
    ).astype(BF16)
    width = weight.shape[0]
    local_ref[:width] = lax.dot_general(
        aggregated, grad_pre, (((0,), (0,)), ((), ())), preferred_element_type=F32
    )
    local_ref[width:] = jnp.broadcast_to(
        jnp.sum(grad_pre.astype(F32), axis=0, keepdims=True),
        (local_ref.shape[0] - width, width),
    )


def dense(own, parts, weight, bias, cotangent):
    nodes, width = own.shape
    spec = pl.BlockSpec(memory_space=pltpu.VMEM)
    shapes = (
        jax.ShapeDtypeStruct((nodes, width), BF16),
        jax.ShapeDtypeStruct((width, nodes), BF16),
        jax.ShapeDtypeStruct((width + 16, width), F32),
    )
    return pl.pallas_call(
        lambda *refs: dense_kernel(len(parts), *refs),
        out_shape=shapes,
        in_specs=[spec] * (4 + len(parts)),
        out_specs=(spec,) * 3,
        compiler_params=pltpu.CompilerParams(vmem_limit_bytes=16 << 20),
        cost_estimate=pl.CostEstimate(
            flops=6 * nodes * width * width,
            bytes_accessed=8 * nodes * width,
            transcendentals=nodes * width,
        ),
        name="dense",
    )(own, *parts, weight, bias.reshape(1, width), cotangent)


def back_kernel(panels, chosen, last, *refs):
    cell_ref, *grad_refs = refs[: 1 + len(panels)]
    rest = refs[1 + len(panels) :]
    width, nodes = grad_refs[0].shape
    runs = []
    for panel, ref in zip(panels, grad_refs):
        if runs and runs[-1][0] + len(runs[-1][1]) == panel:
            runs[-1][1].append(ref[...])
        else:
            runs.append((panel, [ref[...]]))
    runs = [(panel * nodes, jnp.concatenate(grads, axis=1)) for panel, grads in runs]

    def product(columns):
        value = None
        for top, grads in runs:
            part = jnp.dot(
                grads,
                cell_ref[top : top + grads.shape[1], columns],
                preferred_element_type=F32,
            )
            value = part if value is None else value + part
        return value

    for index, panel in enumerate(chosen):
        columns = slice(panel * nodes, (panel + 1) * nodes)
        if last:
            total_ref, *out_refs = rest
            value = total_ref[:, columns] + product(columns)
            out_refs[index][...] = value.T.astype(out_refs[index].dtype)
        else:
            rest[0][:, columns] = product(columns)


def back(panels, chosen, grads, cell, total=None):
    width, nodes = grads[0].shape
    spec = pl.BlockSpec(memory_space=pltpu.VMEM)
    operands = (cell, *grads) if total is None else (cell, *grads, total)
    if total is None:
        outs = (pltpu.VMEM((width, cell.shape[1]), F32),)
    else:
        outs = tuple(
            pltpu.VMEM((nodes, width), F32 if panel == 0 else BF16) for panel in chosen
        )
    flops = 2 * len(panels) * len(chosen) * nodes * nodes * width
    return pl.pallas_call(
        lambda *refs: back_kernel(panels, chosen, total is not None, *refs),
        out_shape=outs,
        in_specs=[spec] * len(operands),
        out_specs=[spec] * len(outs),
        compiler_params=pltpu.CompilerParams(vmem_limit_bytes=24 << 20),
        cost_estimate=pl.CostEstimate(
            flops=flops, bytes_accessed=flops // 512, transcendentals=0
        ),
        name="back_first" if total is None else "back_last",
    )(*operands)


def finish_kernel(factor, part_count, *refs):
    own_ref = refs[0]
    part_refs = refs[1 : 1 + part_count]
    weight_refs = refs[1 + part_count : -3]
    out_ref, weight_ref, bias_ref = refs[-3:]
    value = own_ref[...]
    for part_ref in part_refs:
        value = value + part_ref[...].astype(F32)
    out_ref[...] = value.astype(out_ref.dtype)
    summed = tree_sum([ref[...] for ref in weight_refs]) * factor
    width = weight_ref.shape[0]
    weight_ref[...] = summed[:width]
    bias_ref[...] = summed[width : width + 1]


def finish(own, parts, weight_parts, factor):
    spec = pl.BlockSpec(memory_space=pltpu.VMEM)
    width = own.shape[1]
    return pl.pallas_call(
        lambda *refs: finish_kernel(factor, len(parts), *refs),
        out_shape=(
            jax.ShapeDtypeStruct(own.shape, BF16),
            jax.ShapeDtypeStruct((width, width), F32),
            jax.ShapeDtypeStruct((1, width), F32),
        ),
        in_specs=[spec] * (1 + len(parts) + len(weight_parts)),
        out_specs=(spec,) * 3,
        compiler_params=pltpu.CompilerParams(vmem_limit_bytes=16 << 20),
        cost_estimate=pl.CostEstimate(
            flops=8 * own.size, bytes_accessed=16 * own.size, transcendentals=0
        ),
        name="finish",
    )(own, *parts, *weight_parts)


def swap(value, axis, mask):
    count = lax.axis_size(axis)
    return lax.ppermute(value, axis, [(i, i ^ mask) for i in range(count)])


def move(value, pairs):
    pairs = [(2 * a + core, 2 * b + core) for a, b in pairs for core in range(2)]
    return lax.ppermute(value, "col", pairs)


def sum_far(chunks):
    if len(chunks) != 4:
        return [swap(chunks[k].astype(BF16), "col", 2 * k) for k in range(1, len(chunks))]
    far = chunks[3].astype(BF16)
    passed = move(far, [(0, 1), (3, 2)])
    middle = move(far, [(1, 2), (2, 1)])
    near, passed = lax.optimization_barrier((chunks[1].astype(BF16), passed))
    across = swap((chunks[2] + passed.astype(F32)).astype(BF16), "col", 4)
    return [swap(near, "col", 2), across, middle]


def gather_far(value, count):
    if count != 4:
        return [value] + [swap(value, "col", 2 * k) for k in range(1, count)]
    across = swap(value, "col", 4)
    near = swap(value, "col", 2)
    later, across = lax.optimization_barrier((value, across))
    passed = move(across, [(1, 0), (2, 3)])
    middle = move(later, [(1, 2), (2, 1)])
    return [value, near, across, passed + middle]


def tree_sum(values):
    values = [value.astype(F32) for value in values]
    while len(values) > 1:
        values = [a + b for a, b in zip(values[::2], values[1::2])]
    return values[0]


def sum_over(value, axis, masks):
    return tree_sum([value] + [swap(value, axis, mask) for mask in masks])


def per_device(features, weight, bias, cotangent, tiles, tile_rows, tile_cols, tile_counts):
    block = tiles.shape[-1]
    nodes, width = features.shape
    row_count = lax.axis_size("row")
    col_count = lax.axis_size("col")
    half = col_count // 2
    factor = 1.0 / math.sqrt(nodes * row_count * col_count)

    panels = [features] + [swap(features, "row", k) for k in range(1, row_count)]
    cell = densify(
        tiles[0, 0], tile_rows, tile_cols, tile_counts, nodes // block, col_count, row_count
    )

    def cell_rows(core, k):
        top = (core * half + k) * nodes
        return cell[top : top + nodes]

    source = jnp.concatenate(panels, axis=0)

    def cell_product(core, k):
        return jnp.dot(cell_rows(core, k), source, preferred_element_type=F32)

    far = half - 1
    from_mate = {k: swap(cell_product(1, k).astype(BF16), "col", 1) for k in (far, far - 1)}
    source, from_mate[far] = lax.optimization_barrier((source, from_mate[far]))
    for k in range(far - 2, -1, -1):
        from_mate[k] = swap(cell_product(1, k).astype(BF16), "col", 1)
    chunks = [cell_product(0, k) + from_mate[k].astype(F32) for k in range(half)]
    hidden, grad_agg, local = dense(chunks[0], sum_far(chunks), weight, bias, cotangent)

    own_grads = gather_far(grad_agg, half)
    mate_grads = [swap(part, "col", 1) for part in own_grads[:far]]
    part = sum_over(local, "col", [1]).astype(BF16)
    part = sum_over(part, "row", range(1, row_count)).astype(BF16)
    part, mate_grads[0] = lax.optimization_barrier((part, mate_grads[0]))

    if cell.size * 2 <= CELL_IN_VMEM:
        panels = [*range(far), *range(half, half + far)]
        grads = own_grads[:far] + mate_grads[:far]
        (total,) = back(panels, list(range(row_count)), grads, cell)
        total, last = lax.optimization_barrier((total, own_grads[far]))
        panels = [far, half + far]
        grads = [last, swap(last, "col", 1)]
        pieces = {}
        rest = total
        for chosen in ([row_count - 1], list(range(row_count - 2, 0, -1)), [0]):
            pieces.update(zip(chosen, back(panels, chosen, grads, cell, rest)))
            rest, pieces[chosen[-1]] = lax.optimization_barrier((total, pieces[chosen[-1]]))
    else:
        own = jnp.concatenate(own_grads, axis=1)
        mate_grads.append(swap(own_grads[far], "col", 1))
        mate = jnp.concatenate(mate_grads, axis=1)
        total = jnp.dot(own, cell[: half * nodes], preferred_element_type=F32)
        total = total + jnp.dot(mate, cell[half * nodes :], preferred_element_type=F32)
        pieces = {
            k: total[:, k * nodes : (k + 1) * nodes].T.astype(F32 if k == 0 else BF16)
            for k in range(row_count)
        }
    part, pieces[1] = lax.optimization_barrier((part, pieces[1]))
    landed = [swap(pieces[k], "row", k) for k in range(row_count - 1, 0, -1)]
    parts = [part] + [swap(part, "col", mask) for mask in range(2, col_count, 2)]
    grad_features, grad_weight, grad_bias = finish(pieces[0], landed, parts, factor)
    return (hidden, grad_weight, grad_bias[0], grad_features)


def solution(mesh):
    in_specs = (
        P(("col", "row"), None),
        P(),
        P(),
        P(("row", "col"), None),
        P("row", "col", None, None, None),
        P("row", "col", None),
        P("row", "col", None),
        P("row", "col"),
    )
    out_specs = (P(("row", "col"), None), P(), P(), P(("col", "row"), None))
    return jax.shard_map(
        per_device, mesh=mesh, in_specs=in_specs, out_specs=out_specs, check_vma=False
    )
```

```python
import math

import jax
import jax.numpy as jnp
from jax import lax
from jax.experimental import pallas as pl
from jax.experimental.pallas import tpu as pltpu
from jax.sharding import PartitionSpec as P

BF16 = jnp.bfloat16
F32 = jnp.float32
CELL_IN_VMEM = 1 << 24


def densify_kernel(per, half, one_band, rows_ref, cols_ref, count_ref, *refs):
    *window_refs, cell_ref = refs
    group, block, _ = window_refs[0].shape
    band = pl.program_id(0)
    step = pl.program_id(1)
    row_pos = lax.axis_index("row")
    core = lax.axis_index("col") & 1

    @pl.when(step == 0)
    def _():
        def clear(index, carry):
            cell_ref[pl.ds(pl.multiple_of(index * block, block), block), :] = jnp.zeros(
                (block, cell_ref.shape[1]), cell_ref.dtype
            )
            return carry

        lax.fori_loop(0, cell_ref.shape[0] // block, clear, 0)

    def put(window_ref, start, first, number):
        places = []
        for index in range(number):
            row = rows_ref[0, 0, start + first + index]
            col = cols_ref[0, 0, start + first + index]
            panel = lax.div(row, per)
            down = ((panel & 1) ^ core) * half + (panel >> 1)
            top = ((down - panel) * per + row) * block - band * cell_ref.shape[0]
            panel = lax.div(col, per)
            left = (((panel ^ row_pos) - panel) * per + col) * block
            places.append((top, left))
        values = [window_ref[first + index] for index in range(number)]
        for (top, left), value in zip(places, values):

            def store(top=top, left=left, value=value):
                cell_ref[
                    pl.ds(pl.multiple_of(top, block), block),
                    pl.ds(pl.multiple_of(left, block), block),
                ] = value

            if one_band:
                store()
            else:
                pl.when((top >= 0) & (top < cell_ref.shape[0]))(store)

    for part, window_ref in enumerate(window_refs):
        start = (step * len(window_refs) + part) * group
        live = jnp.clip(count_ref[0, 0] - start, 0, group)

        def put_four(index, carry, window_ref=window_ref, start=start):
            put(window_ref, start, index * 4, 4)
            return carry

        lax.fori_loop(0, live >> 2, put_four, 0)

        def put_one(index, carry, window_ref=window_ref, start=start):
            put(window_ref, start, index, 1)
            return carry

        lax.fori_loop((live >> 2) << 2, live, put_one, 0)


def densify(tiles, rows, cols, count, per, col_count, row_count):
    slots, block, _ = tiles.shape
    group = math.gcd(slots, 32)
    windows = math.gcd(slots // group, 3)
    shape = (per * col_count * block, per * row_count * block)
    size = shape[0] * shape[1] * 2
    bands = max(1, size // CELL_IN_VMEM)
    space = pltpu.VMEM if bands == 1 else pltpu.HBM

    def tile_spec(part):
        def tile_map(band, step, rows_ref, cols_ref, count_ref):
            last = jnp.maximum(count_ref[0, 0] - 1, 0) // group
            return (jnp.minimum(step * windows + part, last), 0, 0)

        return pl.BlockSpec((group, block, block), tile_map)

    tiles = pltpu.with_memory_space_constraint(tiles, pltpu.HBM)
    return pl.pallas_call(
        lambda *refs: densify_kernel(per, col_count // 2, bands == 1, *refs),
        out_shape=space(shape, tiles.dtype),
        grid_spec=pltpu.PrefetchScalarGridSpec(
            num_scalar_prefetch=3,
            grid=(bands, slots // (group * windows)),
            in_specs=[tile_spec(part) for part in range(windows)],
            out_specs=pl.BlockSpec(
                (shape[0] // bands, shape[1]),
                lambda band, step, *refs: (band, 0),
                pipeline_mode=pl.Buffered(1),
            ),
        ),
        compiler_params=pltpu.CompilerParams(
            vmem_limit_bytes=size // bands + (10 << 20)
        ),
        cost_estimate=pl.CostEstimate(
            flops=0, bytes_accessed=2 * size, transcendentals=0
        ),
        name="densify",
    )(
        pltpu.with_memory_space_constraint(rows, pltpu.HBM),
        pltpu.with_memory_space_constraint(cols, pltpu.HBM),
        count,
        *[tiles] * windows,
    )


def dense_kernel(*refs):
    parts_ref, weight_ref, bias_ref, cotangent_ref, hidden_ref, grad_ref, local_ref = refs
    total = parts_ref[0].astype(F32)
    for part in range(1, parts_ref.shape[0]):
        total = total + parts_ref[part].astype(F32)
    aggregated = total.astype(BF16)
    weight = weight_ref[...]
    preact = jnp.dot(aggregated, weight, preferred_element_type=F32) + bias_ref[...]
    sigma = jax.nn.sigmoid(preact)
    hidden_ref[...] = (preact * sigma).astype(BF16)
    slope = sigma * (1.0 + preact * (1.0 - sigma))
    grad_pre = (cotangent_ref[...].astype(F32) * slope).astype(BF16)
    grad_ref[...] = lax.dot_general(
        weight, grad_pre, (((1,), (1,)), ((), ())), preferred_element_type=F32
    ).astype(BF16)
    width = weight.shape[0]
    local_ref[:width] = lax.dot_general(
        aggregated, grad_pre, (((0,), (0,)), ((), ())), preferred_element_type=F32
    )
    local_ref[width:] = jnp.broadcast_to(
        jnp.sum(grad_pre.astype(F32), axis=0, keepdims=True),
        (local_ref.shape[0] - width, width),
    )


def dense(parts, weight, bias, cotangent):
    _, nodes, width = parts.shape
    spec = pl.BlockSpec(memory_space=pltpu.VMEM)
    shapes = (
        jax.ShapeDtypeStruct((nodes, width), BF16),
        jax.ShapeDtypeStruct((width, nodes), BF16),
        jax.ShapeDtypeStruct((width + 16, width), F32),
    )
    return pl.pallas_call(
        dense_kernel,
        out_shape=shapes,
        in_specs=[spec] * 4,
        out_specs=(spec,) * 3,
        compiler_params=pltpu.CompilerParams(vmem_limit_bytes=16 << 20),
        cost_estimate=pl.CostEstimate(
            flops=6 * nodes * width * width,
            bytes_accessed=8 * nodes * width,
            transcendentals=nodes * width,
        ),
        name="dense",
    )(parts, weight, bias.reshape(1, width), cotangent)


def back_own_kernel(grads_ref, cell_ref, total_ref):
    count, width, nodes = grads_ref.shape
    grads = jnp.concatenate([grads_ref[part] for part in range(count)], axis=1)
    for left in range(0, total_ref.shape[1], nodes):
        total_ref[:, left : left + nodes] = jnp.dot(
            grads, cell_ref[: count * nodes, left : left + nodes], preferred_element_type=F32
        )


def back_mate_kernel(grads_ref, cell_ref, total_ref, pieces_ref):
    count, width, nodes = grads_ref.shape
    grads = jnp.concatenate([grads_ref[part] for part in range(count)], axis=1)
    for panel in range(pieces_ref.shape[0]):
        columns = slice(panel * nodes, (panel + 1) * nodes)
        value = total_ref[:, columns] + jnp.dot(
            grads, cell_ref[count * nodes :, columns], preferred_element_type=F32
        )
        pieces_ref[panel ^ lax.axis_index("row")] = value.T.astype(pieces_ref.dtype)


def back_call(kernel, out, operands, name):
    spec = pl.BlockSpec(memory_space=pltpu.VMEM)
    count, width, nodes = operands[0].shape
    flops = 2 * count * nodes * width * operands[1].shape[1]
    return pl.pallas_call(
        kernel,
        out_shape=out,
        in_specs=[spec] * len(operands),
        out_specs=spec,
        compiler_params=pltpu.CompilerParams(vmem_limit_bytes=24 << 20),
        cost_estimate=pl.CostEstimate(
            flops=flops, bytes_accessed=flops // 512, transcendentals=0
        ),
        name=name,
    )(*operands)


def finish_weight_kernel(factor, *refs):
    *part_refs, weight_ref, bias_ref = refs
    summed = tree_sum([ref[...] for ref in part_refs]) * factor
    width = weight_ref.shape[0]
    weight_ref[...] = summed[:width]
    bias_ref[...] = summed[width : width + 1]


def finish_weight(parts, factor):
    spec = pl.BlockSpec(memory_space=pltpu.VMEM)
    width = parts[0].shape[1]
    return pl.pallas_call(
        lambda *refs: finish_weight_kernel(factor, *refs),
        out_shape=(
            jax.ShapeDtypeStruct((width, width), F32),
            jax.ShapeDtypeStruct((1, width), F32),
        ),
        in_specs=[spec] * len(parts),
        out_specs=(spec,) * 2,
        compiler_params=pltpu.CompilerParams(vmem_limit_bytes=16 << 20),
        cost_estimate=pl.CostEstimate(
            flops=4 * width * width, bytes_accessed=4 * width * width, transcendentals=0
        ),
        name="finish_weight",
    )(*parts)


def swap(value, axis, mask):
    count = lax.axis_size(axis)
    return lax.ppermute(value, axis, [(i, i ^ mask) for i in range(count)])


def exchange(value, axis, groups=None):
    return lax.all_to_all(value, axis, 0, 0, axis_index_groups=groups, tiled=True)


def tree_sum(values):
    values = [value.astype(F32) for value in values]
    while len(values) > 1:
        values = [a + b for a, b in zip(values[::2], values[1::2])]
    return values[0]


def sum_over(value, axis, masks):
    return tree_sum([value] + [swap(value, axis, mask) for mask in masks])


def per_device(features, weight, bias, cotangent, tiles, tile_rows, tile_cols, tile_counts):
    block = tiles.shape[-1]
    nodes, width = features.shape
    row_count = lax.axis_size("row")
    col_count = lax.axis_size("col")
    half = col_count // 2
    factor = 1.0 / math.sqrt(nodes * row_count * col_count)

    panels = [features] + [swap(features, "row", k) for k in range(1, row_count)]
    cell = densify(
        tiles[0, 0], tile_rows, tile_cols, tile_counts, nodes // block, col_count, row_count
    )
    groups = [[2 * place + core for place in range(half)] for core in range(2)]
    source = jnp.concatenate(panels, axis=0)

    for_mate = [
        jnp.dot(cell[top : top + nodes], source, preferred_element_type=F32).astype(BF16)
        for top in range(half * nodes, 2 * half * nodes, nodes)
    ]
    from_mate = [swap(part, "col", 1) for part in for_mate]
    chunks = [
        jnp.dot(cell[k * nodes : (k + 1) * nodes], source, preferred_element_type=F32)
        + from_mate[k].astype(F32)
        for k in range(half)
    ]
    chunks = jnp.stack([chunk.astype(BF16) for chunk in chunks])
    parts = exchange(chunks, "col", groups)
    hidden, grad_agg, local = dense(parts, weight, bias, cotangent)

    part = sum_over(local, "col", [1]).astype(BF16)
    part = sum_over(part, "row", range(1, row_count)).astype(BF16)
    own_grads = exchange(jnp.broadcast_to(grad_agg, (half, width, nodes)), "col", groups)
    mate_grads = swap(own_grads, "col", 1)

    if cell.size * 2 <= CELL_IN_VMEM:
        total = back_call(
            back_own_kernel,
            pltpu.VMEM((width, row_count * nodes), F32),
            (own_grads, cell),
            "back_own",
        )
        pieces = back_call(
            back_mate_kernel,
            pltpu.VMEM((row_count, nodes, width), BF16),
            (mate_grads, cell, total),
            "back_mate",
        )
    else:
        total = jnp.dot(
            own_grads.swapaxes(0, 1).reshape(width, half * nodes),
            cell[: half * nodes],
            preferred_element_type=F32,
        ) + jnp.dot(
            mate_grads.swapaxes(0, 1).reshape(width, half * nodes),
            cell[half * nodes :],
            preferred_element_type=F32,
        )
        pieces = total.astype(BF16).T.reshape(row_count, nodes, width)
        pieces = pieces[jnp.arange(row_count) ^ lax.axis_index("row")]
    part, pieces = lax.optimization_barrier((part, pieces))
    landed = exchange(pieces, "row")
    grad_features = jnp.sum(landed.astype(F32), axis=0).astype(BF16)
    parts = [part] + [swap(part, "col", mask) for mask in range(2, col_count, 2)]
    grad_weight, grad_bias = finish_weight(parts, factor)
    return (hidden, grad_weight, grad_bias[0], grad_features)


def solution(mesh):
    in_specs = (
        P(("col", "row"), None),
        P(),
        P(),
        P(("row", "col"), None),
        P("row", "col", None, None, None),
        P("row", "col", None),
        P("row", "col", None),
        P("row", "col"),
    )
    out_specs = (P(("row", "col"), None), P(), P(), P(("col", "row"), None))
    return jax.shard_map(
        per_device, mesh=mesh, in_specs=in_specs, out_specs=out_specs, check_vma=False
    )
```

```python
import math

import jax
import jax.numpy as jnp
from jax import lax
from jax.experimental import pallas as pl
from jax.experimental.pallas import tpu as pltpu
from jax.sharding import PartitionSpec as P

BF16 = jnp.bfloat16
F32 = jnp.float32
CELL_IN_VMEM = 1 << 24


def densify_kernel(per, half, one_band, rows_ref, cols_ref, count_ref, *refs):
    *window_refs, cell_ref = refs
    group, block, _ = window_refs[0].shape
    band = pl.program_id(0)
    step = pl.program_id(1)
    row_pos = lax.axis_index("row")
    col_pos = lax.axis_index("col")

    @pl.when(step == 0)
    def _():
        def clear(index, carry):
            cell_ref[pl.ds(pl.multiple_of(index * block, block), block), :] = jnp.zeros(
                (block, cell_ref.shape[1]), cell_ref.dtype
            )
            return carry

        lax.fori_loop(0, cell_ref.shape[0] // block, clear, 0)

    def put(window_ref, start, first, number):
        places = []
        for index in range(number):
            row = rows_ref[0, 0, start + first + index]
            col = cols_ref[0, 0, start + first + index]
            panel = lax.div(row, per)
            down = panel ^ col_pos
            down = (down & 1) * half + (down >> 1)
            top = ((down - panel) * per + row) * block - band * cell_ref.shape[0]
            panel = lax.div(col, per)
            left = (((panel ^ row_pos) - panel) * per + col) * block
            places.append((top, left))
        values = [window_ref[first + index] for index in range(number)]
        for (top, left), value in zip(places, values):

            def store(top=top, left=left, value=value):
                cell_ref[
                    pl.ds(pl.multiple_of(top, block), block),
                    pl.ds(pl.multiple_of(left, block), block),
                ] = value

            if one_band:
                store()
            else:
                pl.when((top >= 0) & (top < cell_ref.shape[0]))(store)

    for part, window_ref in enumerate(window_refs):
        start = (step * len(window_refs) + part) * group
        live = jnp.clip(count_ref[0, 0] - start, 0, group)

        def put_four(index, carry, window_ref=window_ref, start=start):
            put(window_ref, start, index * 4, 4)
            return carry

        lax.fori_loop(0, live >> 2, put_four, 0)

        def put_one(index, carry, window_ref=window_ref, start=start):
            put(window_ref, start, index, 1)
            return carry

        lax.fori_loop((live >> 2) << 2, live, put_one, 0)


def densify(tiles, rows, cols, count, per, col_count, row_count):
    slots, block, _ = tiles.shape
    group = math.gcd(slots, 32)
    windows = math.gcd(slots // group, 3)
    shape = (per * col_count * block, per * row_count * block)
    size = shape[0] * shape[1] * 2
    bands = max(1, size // CELL_IN_VMEM)
    space = pltpu.VMEM if bands == 1 else pltpu.HBM

    def tile_spec(part):
        def tile_map(band, step, rows_ref, cols_ref, count_ref):
            last = jnp.maximum(count_ref[0, 0] - 1, 0) // group
            return (jnp.minimum(step * windows + part, last), 0, 0)

        return pl.BlockSpec((group, block, block), tile_map)

    tiles = pltpu.with_memory_space_constraint(tiles, pltpu.HBM)
    return pl.pallas_call(
        lambda *refs: densify_kernel(per, col_count // 2, bands == 1, *refs),
        out_shape=space(shape, tiles.dtype),
        grid_spec=pltpu.PrefetchScalarGridSpec(
            num_scalar_prefetch=3,
            grid=(bands, slots // (group * windows)),
            in_specs=[tile_spec(part) for part in range(windows)],
            out_specs=pl.BlockSpec(
                (shape[0] // bands, shape[1]),
                lambda band, step, *refs: (band, 0),
                pipeline_mode=pl.Buffered(1),
            ),
        ),
        compiler_params=pltpu.CompilerParams(
            vmem_limit_bytes=size // bands + (10 << 20)
        ),
        cost_estimate=pl.CostEstimate(
            flops=0, bytes_accessed=2 * size, transcendentals=0
        ),
        name="densify",
    )(
        pltpu.with_memory_space_constraint(rows, pltpu.HBM),
        pltpu.with_memory_space_constraint(cols, pltpu.HBM),
        count,
        *[tiles] * windows,
    )


def dense_kernel(part_count, *refs):
    own_ref = refs[0]
    part_refs = refs[1 : 1 + part_count]
    weight_ref, bias_ref, cotangent_ref = refs[1 + part_count : 4 + part_count]
    hidden_ref, grad_ref, local_ref = refs[4 + part_count :]
    total = own_ref[...]
    for part_ref in part_refs:
        total = total + part_ref[...].astype(F32)
    aggregated = total.astype(BF16)
    weight = weight_ref[...]
    preact = jnp.dot(aggregated, weight, preferred_element_type=F32) + bias_ref[...]
    sigma = jax.nn.sigmoid(preact)
    hidden_ref[...] = (preact * sigma).astype(BF16)
    slope = sigma * (1.0 + preact * (1.0 - sigma))
    grad_pre = (cotangent_ref[...].astype(F32) * slope).astype(BF16)
    grad_ref[...] = lax.dot_general(
        weight, grad_pre, (((1,), (1,)), ((), ())), preferred_element_type=F32
    ).astype(BF16)
    width = weight.shape[0]
    local_ref[:width] = lax.dot_general(
        aggregated, grad_pre, (((0,), (0,)), ((), ())), preferred_element_type=F32
    )
    local_ref[width:] = jnp.broadcast_to(
        jnp.sum(grad_pre.astype(F32), axis=0, keepdims=True),
        (local_ref.shape[0] - width, width),
    )


def dense(own, parts, weight, bias, cotangent):
    nodes, width = own.shape
    spec = pl.BlockSpec(memory_space=pltpu.VMEM)
    shapes = (
        jax.ShapeDtypeStruct((nodes, width), BF16),
        jax.ShapeDtypeStruct((width, nodes), BF16),
        jax.ShapeDtypeStruct((width + 16, width), F32),
    )
    return pl.pallas_call(
        lambda *refs: dense_kernel(len(parts), *refs),
        out_shape=shapes,
        in_specs=[spec] * (4 + len(parts)),
        out_specs=(spec,) * 3,
        compiler_params=pltpu.CompilerParams(vmem_limit_bytes=16 << 20),
        cost_estimate=pl.CostEstimate(
            flops=6 * nodes * width * width,
            bytes_accessed=8 * nodes * width,
            transcendentals=nodes * width,
        ),
        name="dense",
    )(own, *parts, weight, bias.reshape(1, width), cotangent)


def back_kernel(panels, chosen, last, with_total, *refs):
    cell_ref, *grad_refs = refs[: 1 + len(panels)]
    rest = refs[1 + len(panels) :]
    width, nodes = grad_refs[0].shape
    runs = []
    for panel, ref in zip(panels, grad_refs):
        if runs and runs[-1][0] + len(runs[-1][1]) == panel:
            runs[-1][1].append(ref[...])
        else:
            runs.append((panel, [ref[...]]))
    runs = [(panel * nodes, jnp.concatenate(grads, axis=1)) for panel, grads in runs]

    def product(columns):
        value = None
        for top, grads in runs:
            part = jnp.dot(
                grads,
                cell_ref[top : top + grads.shape[1], columns],
                preferred_element_type=F32,
            )
            value = part if value is None else value + part
        return value

    out_refs = rest[with_total:]
    for index, panel in enumerate(chosen):
        columns = slice(panel * nodes, (panel + 1) * nodes)
        value = product(columns)
        if with_total:
            value = rest[0][:, columns] + value
        if last:
            out_refs[index][...] = value.T.astype(out_refs[index].dtype)
        else:
            out_refs[0][:, columns] = value


def back(panels, chosen, grads, cell, total=None, last=False):
    width, nodes = grads[0].shape
    spec = pl.BlockSpec(memory_space=pltpu.VMEM)
    operands = (cell, *grads) if total is None else (cell, *grads, total)
    if not last:
        outs = (pltpu.VMEM((width, cell.shape[1]), F32),)
    else:
        outs = tuple(
            pltpu.VMEM((nodes, width), F32 if panel == 0 else BF16) for panel in chosen
        )
    flops = 2 * len(panels) * len(chosen) * nodes * nodes * width
    return pl.pallas_call(
        lambda *refs: back_kernel(panels, chosen, last, total is not None, *refs),
        out_shape=outs,
        in_specs=[spec] * len(operands),
        out_specs=[spec] * len(outs),
        compiler_params=pltpu.CompilerParams(vmem_limit_bytes=24 << 20),
        cost_estimate=pl.CostEstimate(
            flops=flops, bytes_accessed=flops // 512, transcendentals=0
        ),
        name="back_last" if last else "back",
    )(*operands)


def finish_kernel(own_ref, *refs):
    *part_refs, out_ref = refs
    value = own_ref[...]
    for part_ref in part_refs:
        value = value + part_ref[...].astype(F32)
    out_ref[...] = value.astype(out_ref.dtype)


def finish(own, parts):
    spec = pl.BlockSpec(memory_space=pltpu.VMEM)
    return pl.pallas_call(
        finish_kernel,
        out_shape=jax.ShapeDtypeStruct(own.shape, BF16),
        in_specs=[spec] * (1 + len(parts)),
        out_specs=spec,
        compiler_params=pltpu.CompilerParams(vmem_limit_bytes=16 << 20),
        cost_estimate=pl.CostEstimate(
            flops=8 * own.size, bytes_accessed=16 * own.size, transcendentals=0
        ),
        name="finish",
    )(own, *parts)


def finish_weight_kernel(factor, own_ref, other_ref, weight_ref, bias_ref):
    summed = (own_ref[...].astype(F32) + other_ref[...].astype(F32)) * factor
    width = weight_ref.shape[0]
    weight_ref[...] = summed[:width]
    bias_ref[...] = summed[width : width + 1]


def finish_weight(own, other, factor):
    spec = pl.BlockSpec(memory_space=pltpu.VMEM)
    width = own.shape[1]
    return pl.pallas_call(
        lambda *refs: finish_weight_kernel(factor, *refs),
        out_shape=(
            jax.ShapeDtypeStruct((width, width), F32),
            jax.ShapeDtypeStruct((1, width), F32),
        ),
        in_specs=[spec] * 2,
        out_specs=(spec,) * 2,
        compiler_params=pltpu.CompilerParams(vmem_limit_bytes=16 << 20),
        cost_estimate=pl.CostEstimate(
            flops=4 * width * width, bytes_accessed=4 * width * width, transcendentals=0
        ),
        name="finish_weight",
    )(own, other)


def swap(value, axis, mask):
    count = lax.axis_size(axis)
    return lax.ppermute(value, axis, [(i, i ^ mask) for i in range(count)])


def move(value, pairs):
    pairs = [(2 * a + core, 2 * b + core) for a, b in pairs for core in range(2)]
    return lax.ppermute(value, "col", pairs)


def sum_far(far, chunk, ready):
    if lax.axis_size("col") != 8:
        count = lax.axis_size("col") // 2
        parts = [swap(chunk(k, far).astype(BF16), "col", 2 * k) for k in range(1, count - 1)]
        return [*parts, swap(far, "col", 2 * (count - 1))], chunk(0, far)
    passed = move(far, [(0, 1), (3, 2)])
    later, ready = lax.optimization_barrier((far, ready))
    middle = move(later, [(1, 2), (2, 1)])
    both = (chunk(2, passed) + passed.astype(F32)).astype(BF16)
    across = swap(both, "col", 4)
    near = swap(chunk(1, both).astype(BF16), "col", 2)
    return [near, across, middle], chunk(0, both)


def gather_far(value, count):
    if count != 4:
        return [value] + [swap(value, "col", 2 * k) for k in range(1, count)]
    across = swap(value, "col", 4)
    near = swap(value, "col", 2)
    passed = move(across, [(1, 0), (2, 3)])
    middle = move(value, [(1, 2), (2, 1)])
    return [value, near, across, passed + middle]


def sum_over(value, axis, masks):
    for mask in masks:
        value = value.astype(BF16)
        value = value.astype(F32) + swap(value, axis, mask).astype(F32)
    return value


def doublings(first, end):
    return [first << power for power in range((end // first).bit_length() - 1)]


def per_device(features, weight, bias, cotangent, tiles, tile_rows, tile_cols, tile_counts):
    block = tiles.shape[-1]
    nodes, width = features.shape
    row_count = lax.axis_size("row")
    col_count = lax.axis_size("col")
    half = col_count // 2
    factor = 1.0 / math.sqrt(nodes * row_count * col_count)

    panels = [features] + [swap(features, "row", k) for k in range(1, row_count)]
    cell = densify(
        tiles[0, 0], tile_rows, tile_cols, tile_counts, nodes // block, col_count, row_count
    )

    def cell_rows(core, k):
        top = (core * half + k) * nodes
        return cell[top : top + nodes]

    source = jnp.concatenate(panels, axis=0)

    def cell_product(core, k, source):
        return jnp.dot(cell_rows(core, k), source, preferred_element_type=F32)

    far = half - 1
    from_mate = {
        k: swap(cell_product(1, k, source).astype(BF16), "col", 1) for k in (far, far - 1)
    }
    own_far = lax.optimization_barrier(cell_product(0, far, source))
    own_far = (own_far + from_mate[far].astype(F32)).astype(BF16)

    later, from_mate[far - 1] = lax.optimization_barrier((source, from_mate[far - 1]))
    for k in range(far - 1):
        from_mate[k] = swap(cell_product(1, k, later).astype(BF16), "col", 1)

    def chunk(k, hold):
        after, hold = lax.optimization_barrier((source, hold))
        return cell_product(0, k, after) + from_mate[k].astype(F32)

    parts, own = sum_far(own_far, chunk, from_mate[far - 1])
    hidden, grad_agg, local = dense(own, parts, weight, bias, cotangent)

    part = local + swap(local, "col", 1)
    part = sum_over(part, "row", doublings(1, row_count)).astype(BF16)
    own_grads = gather_far(grad_agg, half)
    mate_grads = [swap(grads, "col", 1) for grads in own_grads[:far]]

    if cell.size * 2 <= CELL_IN_VMEM:
        every = list(range(row_count))
        (total,) = back(list(range(far)), every, own_grads[:far], cell)
        (total,) = back(list(range(half, half + far)), every, mate_grads, cell, total)
        panels = [far, half + far]
        grads = [own_grads[far], swap(own_grads[far], "col", 1)]
        pieces = {}
        rest = total
        for chosen in ([row_count - 1], list(range(row_count - 2, 0, -1)), [0]):
            pieces.update(zip(chosen, back(panels, chosen, grads, cell, rest, True)))
            rest, pieces[chosen[-1]] = lax.optimization_barrier((total, pieces[chosen[-1]]))
    else:
        own = jnp.concatenate(own_grads, axis=1)
        mate_grads.append(swap(own_grads[far], "col", 1))
        mate = jnp.concatenate(mate_grads, axis=1)
        total = jnp.dot(own, cell[: half * nodes], preferred_element_type=F32)
        total = total + jnp.dot(mate, cell[half * nodes :], preferred_element_type=F32)
        pieces = {
            k: total[:, k * nodes : (k + 1) * nodes].T.astype(F32 if k == 0 else BF16)
            for k in range(row_count)
        }
    part, pieces[1] = lax.optimization_barrier((part, pieces[1]))
    landed = [swap(pieces[k], "row", k) for k in range(row_count - 1, 0, -1)]
    *masks, mask = doublings(2, col_count)
    part = sum_over(part, "col", masks).astype(BF16)
    grad_weight, grad_bias = finish_weight(part, swap(part, "col", mask), factor)
    grad_features = finish(pieces[0], landed)
    return (hidden, grad_weight, grad_bias[0], grad_features)


def solution(mesh):
    in_specs = (
        P(("col", "row"), None),
        P(),
        P(),
        P(("row", "col"), None),
        P("row", "col", None, None, None),
        P("row", "col", None),
        P("row", "col", None),
        P("row", "col"),
    )
    out_specs = (P(("row", "col"), None), P(), P(), P(("col", "row"), None))
    return jax.shard_map(
        per_device, mesh=mesh, in_specs=in_specs, out_specs=out_specs, check_vma=False
    )
```

```python
import math

import jax
import jax.numpy as jnp
from jax import lax
from jax.experimental import pallas as pl
from jax.experimental.pallas import tpu as pltpu
from jax.sharding import PartitionSpec as P

BF16 = jnp.bfloat16
F32 = jnp.float32
CELL_IN_VMEM = 1 << 24


def densify_kernel(per, half, one_band, rows_ref, cols_ref, count_ref, *refs):
    *window_refs, cell_ref = refs
    group, block, _ = window_refs[0].shape
    band = pl.program_id(0)
    step = pl.program_id(1)
    row_pos = lax.axis_index("row")
    col_pos = lax.axis_index("col")

    @pl.when(step == 0)
    def _():
        def clear(index, carry):
            cell_ref[pl.ds(pl.multiple_of(index * block, block), block), :] = jnp.zeros(
                (block, cell_ref.shape[1]), cell_ref.dtype
            )
            return carry

        lax.fori_loop(0, cell_ref.shape[0] // block, clear, 0)

    def put(window_ref, start, first, number):
        places = []
        for index in range(number):
            row = rows_ref[0, 0, start + first + index]
            col = cols_ref[0, 0, start + first + index]
            panel = lax.div(row, per)
            down = panel ^ col_pos
            down = (down & 1) * half + (down >> 1)
            top = ((down - panel) * per + row) * block - band * cell_ref.shape[0]
            panel = lax.div(col, per)
            left = (((panel ^ row_pos) - panel) * per + col) * block
            places.append((top, left))
        values = [window_ref[first + index] for index in range(number)]
        for (top, left), value in zip(places, values):

            def store(top=top, left=left, value=value):
                cell_ref[
                    pl.ds(pl.multiple_of(top, block), block),
                    pl.ds(pl.multiple_of(left, block), block),
                ] = value

            if one_band:
                store()
            else:
                pl.when((top >= 0) & (top < cell_ref.shape[0]))(store)

    for part, window_ref in enumerate(window_refs):
        start = (step * len(window_refs) + part) * group
        live = jnp.clip(count_ref[0, 0] - start, 0, group)

        def put_four(index, carry, window_ref=window_ref, start=start):
            put(window_ref, start, index * 4, 4)
            return carry

        lax.fori_loop(0, live >> 2, put_four, 0)

        def put_one(index, carry, window_ref=window_ref, start=start):
            put(window_ref, start, index, 1)
            return carry

        lax.fori_loop((live >> 2) << 2, live, put_one, 0)


def densify(tiles, rows, cols, count, per, col_count, row_count):
    slots, block, _ = tiles.shape
    group = math.gcd(slots, 32)
    windows = math.gcd(slots // group, 3)
    shape = (per * col_count * block, per * row_count * block)
    size = shape[0] * shape[1] * 2
    bands = max(1, size // CELL_IN_VMEM)
    space = pltpu.VMEM if bands == 1 else pltpu.HBM

    def tile_spec(part):
        def tile_map(band, step, rows_ref, cols_ref, count_ref):
            last = jnp.maximum(count_ref[0, 0] - 1, 0) // group
            return (jnp.minimum(step * windows + part, last), 0, 0)

        return pl.BlockSpec((group, block, block), tile_map)

    tiles = pltpu.with_memory_space_constraint(tiles, pltpu.HBM)
    return pl.pallas_call(
        lambda *refs: densify_kernel(per, col_count // 2, bands == 1, *refs),
        out_shape=space(shape, tiles.dtype),
        grid_spec=pltpu.PrefetchScalarGridSpec(
            num_scalar_prefetch=3,
            grid=(bands, slots // (group * windows)),
            in_specs=[tile_spec(part) for part in range(windows)],
            out_specs=pl.BlockSpec(
                (shape[0] // bands, shape[1]),
                lambda band, step, *refs: (band, 0),
                pipeline_mode=pl.Buffered(1),
            ),
        ),
        compiler_params=pltpu.CompilerParams(
            vmem_limit_bytes=size // bands + (10 << 20)
        ),
        cost_estimate=pl.CostEstimate(
            flops=0, bytes_accessed=2 * size, transcendentals=0
        ),
        name="densify",
    )(
        pltpu.with_memory_space_constraint(rows, pltpu.HBM),
        pltpu.with_memory_space_constraint(cols, pltpu.HBM),
        count,
        *[tiles] * windows,
    )


def dense_kernel(part_count, *refs):
    own_ref = refs[0]
    part_refs = refs[1 : 1 + part_count]
    weight_ref, bias_ref, cotangent_ref = refs[1 + part_count : 4 + part_count]
    hidden_ref, grad_ref, local_ref = refs[4 + part_count :]
    total = own_ref[...]
    for part_ref in part_refs:
        total = total + part_ref[...].astype(F32)
    aggregated = total.astype(BF16)
    weight = weight_ref[...]
    preact = jnp.dot(aggregated, weight, preferred_element_type=F32) + bias_ref[...]
    sigma = jax.nn.sigmoid(preact)
    hidden_ref[...] = (preact * sigma).astype(BF16)
    slope = sigma * (1.0 + preact * (1.0 - sigma))
    grad_pre = (cotangent_ref[...].astype(F32) * slope).astype(BF16)
    grad_ref[...] = lax.dot_general(
        weight, grad_pre, (((1,), (1,)), ((), ())), preferred_element_type=F32
    ).astype(BF16)
    width = weight.shape[0]
    local_ref[:width] = lax.dot_general(
        aggregated, grad_pre, (((0,), (0,)), ((), ())), preferred_element_type=F32
    )
    local_ref[width:] = jnp.broadcast_to(
        jnp.sum(grad_pre.astype(F32), axis=0, keepdims=True),
        (local_ref.shape[0] - width, width),
    )


def dense(own, parts, weight, bias, cotangent):
    nodes, width = own.shape
    spec = pl.BlockSpec(memory_space=pltpu.VMEM)
    shapes = (
        jax.ShapeDtypeStruct((nodes, width), BF16),
        jax.ShapeDtypeStruct((width, nodes), BF16),
        jax.ShapeDtypeStruct((width + 16, width), F32),
    )
    return pl.pallas_call(
        lambda *refs: dense_kernel(len(parts), *refs),
        out_shape=shapes,
        in_specs=[spec] * (4 + len(parts)),
        out_specs=(spec,) * 3,
        compiler_params=pltpu.CompilerParams(vmem_limit_bytes=16 << 20),
        cost_estimate=pl.CostEstimate(
            flops=6 * nodes * width * width,
            bytes_accessed=8 * nodes * width,
            transcendentals=nodes * width,
        ),
        name="dense",
    )(own, *parts, weight, bias.reshape(1, width), cotangent)


def back_kernel(panels, chosen, last, with_total, *refs):
    cell_ref, *grad_refs = refs[: 1 + len(panels)]
    rest = refs[1 + len(panels) :]
    width, nodes = grad_refs[0].shape
    runs = []
    for panel, ref in zip(panels, grad_refs):
        if runs and runs[-1][0] + len(runs[-1][1]) == panel:
            runs[-1][1].append(ref[...])
        else:
            runs.append((panel, [ref[...]]))
    runs = [(panel * nodes, jnp.concatenate(grads, axis=1)) for panel, grads in runs]

    def product(columns):
        value = None
        for top, grads in runs:
            part = jnp.dot(
                grads,
                cell_ref[top : top + grads.shape[1], columns],
                preferred_element_type=F32,
            )
            value = part if value is None else value + part
        return value

    out_refs = rest[with_total:]
    for index, panel in enumerate(chosen):
        columns = slice(panel * nodes, (panel + 1) * nodes)
        value = product(columns)
        if with_total:
            value = rest[0][:, columns] + value
        if last:
            out_refs[index][...] = value.T.astype(out_refs[index].dtype)
        else:
            out_refs[0][:, columns] = value


def back(panels, chosen, grads, cell, total=None, last=False):
    width, nodes = grads[0].shape
    spec = pl.BlockSpec(memory_space=pltpu.VMEM)
    operands = (cell, *grads) if total is None else (cell, *grads, total)
    if not last:
        outs = (pltpu.VMEM((width, cell.shape[1]), F32),)
    else:
        outs = tuple(
            pltpu.VMEM((nodes, width), F32 if panel == 0 else BF16) for panel in chosen
        )
    flops = 2 * len(panels) * len(chosen) * nodes * nodes * width
    return pl.pallas_call(
        lambda *refs: back_kernel(panels, chosen, last, total is not None, *refs),
        out_shape=outs,
        in_specs=[spec] * len(operands),
        out_specs=[spec] * len(outs),
        compiler_params=pltpu.CompilerParams(vmem_limit_bytes=24 << 20),
        cost_estimate=pl.CostEstimate(
            flops=flops, bytes_accessed=flops // 512, transcendentals=0
        ),
        name="back_last" if last else "back",
    )(*operands)


def finish_kernel(factor, value_ref, *refs):
    *part_refs, out_ref, weight_ref, bias_ref = refs
    out_ref[...] = value_ref[...].astype(out_ref.dtype)
    summed = tree_sum([ref[...] for ref in part_refs]) * factor
    width = weight_ref.shape[0]
    weight_ref[...] = summed[:width]
    bias_ref[...] = summed[width : width + 1]


def finish(value, parts, factor):
    spec = pl.BlockSpec(memory_space=pltpu.VMEM)
    nodes, width = value.shape
    return pl.pallas_call(
        lambda *refs: finish_kernel(factor, *refs),
        out_shape=(
            jax.ShapeDtypeStruct((nodes, width), BF16),
            jax.ShapeDtypeStruct((width, width), F32),
            jax.ShapeDtypeStruct((1, width), F32),
        ),
        in_specs=[spec] * (len(parts) + 1),
        out_specs=(spec,) * 3,
        compiler_params=pltpu.CompilerParams(vmem_limit_bytes=16 << 20),
        cost_estimate=pl.CostEstimate(
            flops=8 * nodes * width, bytes_accessed=16 * nodes * width, transcendentals=0
        ),
        name="finish",
    )(value, *parts)


def swap(value, axis, mask):
    count = lax.axis_size(axis)
    return lax.ppermute(value, axis, [(i, i ^ mask) for i in range(count)])


def move(value, pairs):
    pairs = [(2 * a + core, 2 * b + core) for a, b in pairs for core in range(2)]
    return lax.ppermute(value, "col", pairs)


def sum_far(far, chunk, ready):
    if lax.axis_size("col") != 8:
        count = lax.axis_size("col") // 2
        parts = [swap(chunk(k, far).astype(BF16), "col", 2 * k) for k in range(1, count - 1)]
        return [*parts, swap(far, "col", 2 * (count - 1))], chunk(0, far)
    passed = jnp.where(at_end(), 0.0, swap(far, "col", 2).astype(F32))
    later, ready = lax.optimization_barrier((far, ready))
    middle = move(later, [(1, 2), (2, 1)])
    both = (chunk(2, passed) + passed).astype(BF16)
    across = swap(both, "col", 4)
    near = swap(chunk(1, both).astype(BF16), "col", 2)
    return [near, across, middle], chunk(0, both)


def gather_far(value, count, hold):
    if count != 4:
        return [value] + [swap(value, "col", 2 * k) for k in range(1, count)], hold
    across = swap(value, "col", 4)
    near = swap(value, "col", 2)
    passed = swap(across, "col", 2)
    later, hold = lax.optimization_barrier((value, hold))
    middle = move(later, [(1, 2), (2, 1)])
    return [value, near, across, jnp.where(at_end(), passed, middle)], hold


def at_end():
    place = lax.axis_index("col") // 2
    return (place == 0) | (place == lax.axis_size("col") // 2 - 1)


def tree_sum(values):
    values = [value.astype(F32) for value in values]
    while len(values) > 1:
        values = [a + b for a, b in zip(values[::2], values[1::2])]
    return values[0]


def sum_over(value, axis, masks):
    for mask in masks:
        value = value.astype(BF16)
        value = value.astype(F32) + swap(value, axis, mask).astype(F32)
    return value


def doublings(first, end):
    return [first << power for power in range((end // first).bit_length() - 1)]


def per_device(features, weight, bias, cotangent, tiles, tile_rows, tile_cols, tile_counts):
    block = tiles.shape[-1]
    nodes, width = features.shape
    row_count = lax.axis_size("row")
    col_count = lax.axis_size("col")
    half = col_count // 2
    factor = 1.0 / math.sqrt(nodes * row_count * col_count)

    panels = [swap(features, "row", k) for k in range(row_count - 1, 0, -1)]
    panels = [features, *panels[::-1]]
    cell = densify(
        tiles[0, 0], tile_rows, tile_cols, tile_counts, nodes // block, col_count, row_count
    )

    def cell_rows(core, k):
        top = (core * half + k) * nodes
        return cell[top : top + nodes]

    source = jnp.concatenate(panels, axis=0)

    def cell_product(core, k, source):
        return jnp.dot(cell_rows(core, k), source, preferred_element_type=F32)

    far = half - 1
    from_mate = {
        k: swap(cell_product(1, k, source).astype(BF16), "col", 1) for k in (far, far - 1)
    }
    own_far = lax.optimization_barrier(cell_product(0, far, source))
    own_far = (own_far + from_mate[far].astype(F32)).astype(BF16)

    later, from_mate[far - 1] = lax.optimization_barrier((source, from_mate[far - 1]))
    for k in range(far - 1):
        from_mate[k] = swap(cell_product(1, k, later).astype(BF16), "col", 1)

    def chunk(k, hold):
        after, hold = lax.optimization_barrier((source, hold))
        return cell_product(0, k, after) + from_mate[k].astype(F32)

    parts, own = sum_far(own_far, chunk, from_mate[far - 1])
    hidden, grad_agg, local = dense(own, parts, weight, bias, cotangent)

    part = local + swap(local, "col", 1)
    first, *masks = doublings(1, row_count)
    part = sum_over(part, "row", [first])
    own_grads, part = gather_far(grad_agg, half, part)
    part = sum_over(part, "row", masks).astype(BF16)
    mate_grads = [swap(grads, "col", 1) for grads in own_grads[:far]]

    if cell.size * 2 <= CELL_IN_VMEM:
        every = list(range(row_count))
        (total,) = back(list(range(far)), every, own_grads[:far], cell)
        (total,) = back(list(range(half, half + far)), every, mate_grads, cell, total)
        panels = [far, half + far]
        grads = [own_grads[far], swap(own_grads[far], "col", 1)]
        pieces = {}
        rest = total
        for chosen in ([row_count - 1], list(range(row_count - 2, 0, -1)), [0]):
            pieces.update(zip(chosen, back(panels, chosen, grads, cell, rest, True)))
            rest, pieces[chosen[-1]] = lax.optimization_barrier((total, pieces[chosen[-1]]))
    else:
        own = jnp.concatenate(own_grads, axis=1)
        mate_grads.append(swap(own_grads[far], "col", 1))
        mate = jnp.concatenate(mate_grads, axis=1)
        total = jnp.dot(own, cell[: half * nodes], preferred_element_type=F32)
        total = total + jnp.dot(mate, cell[half * nodes :], preferred_element_type=F32)
        pieces = {
            k: total[:, k * nodes : (k + 1) * nodes].T.astype(F32 if k == 0 else BF16)
            for k in range(row_count)
        }
    part, pieces[1] = lax.optimization_barrier((part, pieces[1]))
    landed = [swap(pieces[k], "row", k) for k in range(row_count - 1, 0, -1)]
    parts = [part] + [swap(part, "col", mask) for mask in range(2, col_count, 2)]
    value = pieces[0]
    for piece in landed:
        value = value + piece.astype(F32)
    grad_features, grad_weight, grad_bias = finish(value, parts, factor)
    return (hidden, grad_weight, grad_bias[0], grad_features)


def solution(mesh):
    in_specs = (
        P(("col", "row"), None),
        P(),
        P(),
        P(("row", "col"), None),
        P("row", "col", None, None, None),
        P("row", "col", None),
        P("row", "col", None),
        P("row", "col"),
    )
    out_specs = (P(("row", "col"), None), P(), P(), P(("col", "row"), None))
    return jax.shard_map(
        per_device, mesh=mesh, in_specs=in_specs, out_specs=out_specs, check_vma=False
    )
```

```python
import math

import jax
import jax.numpy as jnp
from jax import lax
from jax.experimental import pallas as pl
from jax.experimental.pallas import tpu as pltpu
from jax.sharding import PartitionSpec as P

BF16 = jnp.bfloat16
F32 = jnp.float32
CELL_IN_VMEM = 1 << 24


def densify_kernel(per, half, one_band, rows_ref, cols_ref, count_ref, *refs):
    *window_refs, cell_ref = refs
    group, block, _ = window_refs[0].shape
    band = pl.program_id(0)
    step = pl.program_id(1)
    row_pos = lax.axis_index("row")
    col_pos = lax.axis_index("col")

    @pl.when(step == 0)
    def _():
        def clear(index, carry):
            cell_ref[pl.ds(pl.multiple_of(index * block, block), block), :] = jnp.zeros(
                (block, cell_ref.shape[1]), cell_ref.dtype
            )
            return carry

        lax.fori_loop(0, cell_ref.shape[0] // block, clear, 0)

    def put(window_ref, start, first, number):
        places = []
        for index in range(number):
            row = rows_ref[0, 0, start + first + index]
            col = cols_ref[0, 0, start + first + index]
            panel = lax.div(row, per)
            down = panel ^ col_pos
            down = (down & 1) * half + (down >> 1)
            top = ((down - panel) * per + row) * block - band * cell_ref.shape[0]
            panel = lax.div(col, per)
            left = (((panel ^ row_pos) - panel) * per + col) * block
            places.append((top, left))
        values = [window_ref[first + index] for index in range(number)]
        for (top, left), value in zip(places, values):

            def store(top=top, left=left, value=value):
                cell_ref[
                    pl.ds(pl.multiple_of(top, block), block),
                    pl.ds(pl.multiple_of(left, block), block),
                ] = value

            if one_band:
                store()
            else:
                pl.when((top >= 0) & (top < cell_ref.shape[0]))(store)

    for part, window_ref in enumerate(window_refs):
        start = (step * len(window_refs) + part) * group
        live = jnp.clip(count_ref[0, 0] - start, 0, group)

        def put_four(index, carry, window_ref=window_ref, start=start):
            put(window_ref, start, index * 4, 4)
            return carry

        lax.fori_loop(0, live >> 2, put_four, 0)

        def put_one(index, carry, window_ref=window_ref, start=start):
            put(window_ref, start, index, 1)
            return carry

        lax.fori_loop((live >> 2) << 2, live, put_one, 0)


def densify(tiles, rows, cols, count, per, col_count, row_count):
    slots, block, _ = tiles.shape
    group = math.gcd(slots, 32)
    windows = math.gcd(slots // group, 3)
    shape = (per * col_count * block, per * row_count * block)
    size = shape[0] * shape[1] * 2
    bands = max(1, size // CELL_IN_VMEM)
    space = pltpu.VMEM if bands == 1 else pltpu.HBM

    def tile_spec(part):
        def tile_map(band, step, rows_ref, cols_ref, count_ref):
            last = jnp.maximum(count_ref[0, 0] - 1, 0) // group
            return (jnp.minimum(step * windows + part, last), 0, 0)

        return pl.BlockSpec((group, block, block), tile_map)

    tiles = pltpu.with_memory_space_constraint(tiles, pltpu.HBM)
    return pl.pallas_call(
        lambda *refs: densify_kernel(per, col_count // 2, bands == 1, *refs),
        out_shape=space(shape, tiles.dtype),
        grid_spec=pltpu.PrefetchScalarGridSpec(
            num_scalar_prefetch=3,
            grid=(bands, slots // (group * windows)),
            in_specs=[tile_spec(part) for part in range(windows)],
            out_specs=pl.BlockSpec(
                (shape[0] // bands, shape[1]),
                lambda band, step, *refs: (band, 0),
                pipeline_mode=pl.Buffered(1),
            ),
        ),
        compiler_params=pltpu.CompilerParams(
            vmem_limit_bytes=size // bands + (10 << 20)
        ),
        cost_estimate=pl.CostEstimate(
            flops=0, bytes_accessed=2 * size, transcendentals=0
        ),
        name="densify",
    )(
        pltpu.with_memory_space_constraint(rows, pltpu.HBM),
        pltpu.with_memory_space_constraint(cols, pltpu.HBM),
        count,
        *[tiles] * windows,
    )


def dense_kernel(part_count, *refs):
    own_ref = refs[0]
    part_refs = refs[1 : 1 + part_count]
    weight_ref, bias_ref, cotangent_ref = refs[1 + part_count : 4 + part_count]
    hidden_ref, grad_ref, local_ref = refs[4 + part_count :]
    total = own_ref[...]
    for part_ref in part_refs:
        total = total + part_ref[...].astype(F32)
    aggregated = total.astype(BF16)
    weight = weight_ref[...]
    preact = jnp.dot(aggregated, weight, preferred_element_type=F32) + bias_ref[...]
    sigma = jax.nn.sigmoid(preact)
    hidden_ref[...] = (preact * sigma).astype(BF16)
    slope = sigma * (1.0 + preact * (1.0 - sigma))
    grad_pre = (cotangent_ref[...].astype(F32) * slope).astype(BF16)
    grad_ref[...] = lax.dot_general(
        weight, grad_pre, (((1,), (1,)), ((), ())), preferred_element_type=F32
    ).astype(BF16)
    width = weight.shape[0]
    local_ref[:width] = lax.dot_general(
        aggregated, grad_pre, (((0,), (0,)), ((), ())), preferred_element_type=F32
    )
    local_ref[width:] = jnp.broadcast_to(
        jnp.sum(grad_pre.astype(F32), axis=0, keepdims=True),
        (local_ref.shape[0] - width, width),
    )


def dense(own, parts, weight, bias, cotangent):
    nodes, width = own.shape
    spec = pl.BlockSpec(memory_space=pltpu.VMEM)
    shapes = (
        jax.ShapeDtypeStruct((nodes, width), BF16),
        jax.ShapeDtypeStruct((width, nodes), BF16),
        jax.ShapeDtypeStruct((width + 16, width), F32),
    )
    return pl.pallas_call(
        lambda *refs: dense_kernel(len(parts), *refs),
        out_shape=shapes,
        in_specs=[spec] * (4 + len(parts)),
        out_specs=(spec,) * 3,
        compiler_params=pltpu.CompilerParams(vmem_limit_bytes=16 << 20),
        cost_estimate=pl.CostEstimate(
            flops=6 * nodes * width * width,
            bytes_accessed=8 * nodes * width,
            transcendentals=nodes * width,
        ),
        name="dense",
    )(own, *parts, weight, bias.reshape(1, width), cotangent)


def back_kernel(panels, chosen, last, with_total, *refs):
    cell_ref, *grad_refs = refs[: 1 + len(panels)]
    rest = refs[1 + len(panels) :]
    width, nodes = grad_refs[0].shape
    runs = []
    for panel, ref in zip(panels, grad_refs):
        if runs and runs[-1][0] + len(runs[-1][1]) == panel:
            runs[-1][1].append(ref[...])
        else:
            runs.append((panel, [ref[...]]))
    runs = [(panel * nodes, jnp.concatenate(grads, axis=1)) for panel, grads in runs]

    def product(columns):
        value = None
        for top, grads in runs:
            part = jnp.dot(
                grads,
                cell_ref[top : top + grads.shape[1], columns],
                preferred_element_type=F32,
            )
            value = part if value is None else value + part
        return value

    out_refs = rest[with_total:]
    for index, panel in enumerate(chosen):
        columns = slice(panel * nodes, (panel + 1) * nodes)
        value = product(columns)
        if with_total:
            value = rest[0][:, columns] + value
        if last:
            out_refs[index][...] = value.T.astype(out_refs[index].dtype)
        else:
            out_refs[0][:, columns] = value


def back(panels, chosen, grads, cell, total=None, last=False):
    width, nodes = grads[0].shape
    spec = pl.BlockSpec(memory_space=pltpu.VMEM)
    operands = (cell, *grads) if total is None else (cell, *grads, total)
    if not last:
        outs = (pltpu.VMEM((width, cell.shape[1]), F32),)
    else:
        outs = tuple(
            pltpu.VMEM((nodes, width), F32 if panel == 0 else BF16) for panel in chosen
        )
    flops = 2 * len(panels) * len(chosen) * nodes * nodes * width
    return pl.pallas_call(
        lambda *refs: back_kernel(panels, chosen, last, total is not None, *refs),
        out_shape=outs,
        in_specs=[spec] * len(operands),
        out_specs=[spec] * len(outs),
        compiler_params=pltpu.CompilerParams(vmem_limit_bytes=24 << 20),
        cost_estimate=pl.CostEstimate(
            flops=flops, bytes_accessed=flops // 512, transcendentals=0
        ),
        name="back_last" if last else "back",
    )(*operands)


def finish_kernel(factor, value_ref, part_ref, other_ref, out_ref, weight_ref, bias_ref):
    out_ref[...] = value_ref[...].astype(out_ref.dtype)
    summed = (part_ref[...].astype(F32) + other_ref[...].astype(F32)) * factor
    width = weight_ref.shape[0]
    weight_ref[...] = summed[:width]
    bias_ref[...] = summed[width : width + 1]


def finish(value, part, other, factor):
    spec = pl.BlockSpec(memory_space=pltpu.VMEM)
    nodes, width = value.shape
    return pl.pallas_call(
        lambda *refs: finish_kernel(factor, *refs),
        out_shape=(
            jax.ShapeDtypeStruct((nodes, width), BF16),
            jax.ShapeDtypeStruct((width, width), F32),
            jax.ShapeDtypeStruct((1, width), F32),
        ),
        in_specs=[spec] * 3,
        out_specs=(spec,) * 3,
        compiler_params=pltpu.CompilerParams(vmem_limit_bytes=16 << 20),
        cost_estimate=pl.CostEstimate(
            flops=8 * nodes * width, bytes_accessed=16 * nodes * width, transcendentals=0
        ),
        name="finish",
    )(value, part, other)


def swap(value, axis, mask):
    count = lax.axis_size(axis)
    return lax.ppermute(value, axis, [(i, i ^ mask) for i in range(count)])


def move(value, pairs):
    pairs = [(2 * a + core, 2 * b + core) for a, b in pairs for core in range(2)]
    return lax.ppermute(value, "col", pairs)


def sum_far(far, chunk, ready):
    if lax.axis_size("col") != 8:
        count = lax.axis_size("col") // 2
        parts = [swap(chunk(k, far).astype(BF16), "col", 2 * k) for k in range(1, count - 1)]
        return [*parts, swap(far, "col", 2 * (count - 1))], chunk(0, far)
    passed = jnp.where(at_end(), 0.0, swap(far, "col", 2).astype(F32))
    later, ready = lax.optimization_barrier((far, ready))
    middle = move(later, [(1, 2), (2, 1)])
    both = (chunk(2, passed) + passed).astype(BF16)
    across = swap(both, "col", 4)
    near = swap(chunk(1, both).astype(BF16), "col", 2)
    return [near, across, middle], chunk(0, both)


def gather_far(value, count):
    if count != 4:
        return [value] + [swap(value, "col", 2 * k) for k in range(1, count)]
    across = swap(value, "col", 4)
    near = swap(value, "col", 2)
    passed = swap(across, "col", 2)
    middle = move(value, [(1, 2), (2, 1)])
    return [value, near, across, jnp.where(at_end(), passed, middle)]


def at_end():
    place = lax.axis_index("col") // 2
    return (place == 0) | (place == lax.axis_size("col") // 2 - 1)


def sum_over(value, axis, masks):
    for mask in masks:
        value = value.astype(BF16)
        value = value.astype(F32) + swap(value, axis, mask).astype(F32)
    return value


def doublings(first, end):
    return [first << power for power in range((end // first).bit_length() - 1)]


def per_device(features, weight, bias, cotangent, tiles, tile_rows, tile_cols, tile_counts):
    block = tiles.shape[-1]
    nodes, width = features.shape
    row_count = lax.axis_size("row")
    col_count = lax.axis_size("col")
    half = col_count // 2
    factor = 1.0 / math.sqrt(nodes * row_count * col_count)

    source = jnp.zeros((row_count * nodes, width), BF16).at[:nodes].set(features)
    for k in range(row_count - 1, 0, -1):
        source = source.at[k * nodes : (k + 1) * nodes].set(swap(features, "row", k))
    cell = densify(
        tiles[0, 0], tile_rows, tile_cols, tile_counts, nodes // block, col_count, row_count
    )

    def cell_rows(core, k):
        top = (core * half + k) * nodes
        return cell[top : top + nodes]


    def cell_product(core, k, source):
        return jnp.dot(cell_rows(core, k), source, preferred_element_type=F32)

    far = half - 1
    from_mate = {
        k: swap(cell_product(1, k, source).astype(BF16), "col", 1) for k in (far, far - 1)
    }
    own_far = lax.optimization_barrier(cell_product(0, far, source))
    own_far = (own_far + from_mate[far].astype(F32)).astype(BF16)

    later, from_mate[far - 1] = lax.optimization_barrier((source, from_mate[far - 1]))
    for k in range(far - 1):
        from_mate[k] = swap(cell_product(1, k, later).astype(BF16), "col", 1)

    def chunk(k, hold):
        after, hold = lax.optimization_barrier((source, hold))
        return cell_product(0, k, after) + from_mate[k].astype(F32)

    parts, own = sum_far(own_far, chunk, from_mate[far - 1])
    hidden, grad_agg, local = dense(own, parts, weight, bias, cotangent)

    part = local + swap(local, "col", 1)
    part = sum_over(part, "row", doublings(1, row_count)).astype(BF16)
    own_grads = gather_far(grad_agg, half)
    mate_grads = [swap(grads, "col", 1) for grads in own_grads[:far]]

    if cell.size * 2 <= CELL_IN_VMEM:
        every = list(range(row_count))
        (total,) = back(list(range(far)), every, own_grads[:far], cell)
        (total,) = back(list(range(half, half + far)), every, mate_grads, cell, total)
        panels = [far, half + far]
        grads = [own_grads[far], swap(own_grads[far], "col", 1)]
        pieces = {}
        rest = total
        for chosen in ([row_count - 1], list(range(row_count - 2, 0, -1)), [0]):
            pieces.update(zip(chosen, back(panels, chosen, grads, cell, rest, True)))
            rest, pieces[chosen[-1]] = lax.optimization_barrier((total, pieces[chosen[-1]]))
    else:
        own = jnp.concatenate(own_grads, axis=1)
        mate_grads.append(swap(own_grads[far], "col", 1))
        mate = jnp.concatenate(mate_grads, axis=1)
        total = jnp.dot(own, cell[: half * nodes], preferred_element_type=F32)
        total = total + jnp.dot(mate, cell[half * nodes :], preferred_element_type=F32)
        pieces = {
            k: total[:, k * nodes : (k + 1) * nodes].T.astype(F32 if k == 0 else BF16)
            for k in range(row_count)
        }
    part, pieces[1] = lax.optimization_barrier((part, pieces[1]))
    landed = [swap(pieces[k], "row", k) for k in range(row_count - 1, 0, -1)]
    *masks, mask = doublings(2, col_count)
    part = sum_over(part, "col", masks).astype(BF16)
    value = pieces[0]
    for piece in landed:
        value = value + piece.astype(F32)
    grad_features, grad_weight, grad_bias = finish(value, part, swap(part, "col", mask), factor)
    return (hidden, grad_weight, grad_bias[0], grad_features)


def solution(mesh):
    in_specs = (
        P(("col", "row"), None),
        P(),
        P(),
        P(("row", "col"), None),
        P("row", "col", None, None, None),
        P("row", "col", None),
        P("row", "col", None),
        P("row", "col"),
    )
    out_specs = (P(("row", "col"), None), P(), P(), P(("col", "row"), None))
    return jax.shard_map(
        per_device, mesh=mesh, in_specs=in_specs, out_specs=out_specs, check_vma=False
    )
```

```python
import math

import jax
import jax.numpy as jnp
from jax import lax
from jax.experimental import pallas as pl
from jax.experimental.pallas import tpu as pltpu
from jax.sharding import PartitionSpec as P

BF16 = jnp.bfloat16
F32 = jnp.float32
CELL_IN_VMEM = 1 << 24


def densify_kernel(per, half, one_band, rows_ref, cols_ref, count_ref, *refs):
    *window_refs, cell_ref = refs
    group, block, _ = window_refs[0].shape
    band = pl.program_id(0)
    step = pl.program_id(1)
    row_pos = lax.axis_index("row")
    col_pos = lax.axis_index("col")

    @pl.when(step == 0)
    def _():
        def clear(index, carry):
            cell_ref[pl.ds(pl.multiple_of(index * block, block), block), :] = jnp.zeros(
                (block, cell_ref.shape[1]), cell_ref.dtype
            )
            return carry

        lax.fori_loop(0, cell_ref.shape[0] // block, clear, 0)

    def put(window_ref, start, first, number):
        places = []
        for index in range(number):
            row = rows_ref[0, 0, start + first + index]
            col = cols_ref[0, 0, start + first + index]
            panel = lax.div(row, per)
            down = panel ^ col_pos
            down = (down & 1) * half + (down >> 1)
            top = ((down - panel) * per + row) * block - band * cell_ref.shape[0]
            panel = lax.div(col, per)
            left = (((panel ^ row_pos) - panel) * per + col) * block
            places.append((top, left))
        values = [window_ref[first + index] for index in range(number)]
        for (top, left), value in zip(places, values):

            def store(top=top, left=left, value=value):
                cell_ref[
                    pl.ds(pl.multiple_of(top, block), block),
                    pl.ds(pl.multiple_of(left, block), block),
                ] = value

            if one_band:
                store()
            else:
                pl.when((top >= 0) & (top < cell_ref.shape[0]))(store)

    for part, window_ref in enumerate(window_refs):
        start = (step * len(window_refs) + part) * group
        live = jnp.clip(count_ref[0, 0] - start, 0, group)

        def put_four(index, carry, window_ref=window_ref, start=start):
            put(window_ref, start, index * 4, 4)
            return carry

        lax.fori_loop(0, live >> 2, put_four, 0)

        def put_one(index, carry, window_ref=window_ref, start=start):
            put(window_ref, start, index, 1)
            return carry

        lax.fori_loop((live >> 2) << 2, live, put_one, 0)


def densify(tiles, rows, cols, count, per, col_count, row_count):
    slots, block, _ = tiles.shape
    group = math.gcd(slots, 32)
    windows = math.gcd(slots // group, 3)
    shape = (per * col_count * block, per * row_count * block)
    size = shape[0] * shape[1] * 2
    bands = max(1, size // CELL_IN_VMEM)
    space = pltpu.VMEM if bands == 1 else pltpu.HBM

    def tile_spec(part):
        def tile_map(band, step, rows_ref, cols_ref, count_ref):
            last = jnp.maximum(count_ref[0, 0] - 1, 0) // group
            return (jnp.minimum(step * windows + part, last), 0, 0)

        return pl.BlockSpec((group, block, block), tile_map)

    tiles = pltpu.with_memory_space_constraint(tiles, pltpu.HBM)
    return pl.pallas_call(
        lambda *refs: densify_kernel(per, col_count // 2, bands == 1, *refs),
        out_shape=space(shape, tiles.dtype),
        grid_spec=pltpu.PrefetchScalarGridSpec(
            num_scalar_prefetch=3,
            grid=(bands, slots // (group * windows)),
            in_specs=[tile_spec(part) for part in range(windows)],
            out_specs=pl.BlockSpec(
                (shape[0] // bands, shape[1]),
                lambda band, step, *refs: (band, 0),
                pipeline_mode=pl.Buffered(1),
            ),
        ),
        compiler_params=pltpu.CompilerParams(
            vmem_limit_bytes=size // bands + (10 << 20)
        ),
        cost_estimate=pl.CostEstimate(
            flops=0, bytes_accessed=2 * size, transcendentals=0
        ),
        name="densify",
    )(
        pltpu.with_memory_space_constraint(rows, pltpu.HBM),
        pltpu.with_memory_space_constraint(cols, pltpu.HBM),
        count,
        *[tiles] * windows,
    )


def dense_kernel(part_count, *refs):
    own_ref = refs[0]
    part_refs = refs[1 : 1 + part_count]
    weight_ref, bias_ref, cotangent_ref = refs[1 + part_count : 4 + part_count]
    hidden_ref, grad_ref, local_ref = refs[4 + part_count :]
    total = own_ref[...]
    for part_ref in part_refs:
        total = total + part_ref[...].astype(F32)
    aggregated = total.astype(BF16)
    weight = weight_ref[...]
    preact = jnp.dot(aggregated, weight, preferred_element_type=F32) + bias_ref[...]
    sigma = jax.nn.sigmoid(preact)
    hidden_ref[...] = (preact * sigma).astype(BF16)
    slope = sigma * (1.0 + preact * (1.0 - sigma))
    grad_pre = (cotangent_ref[...].astype(F32) * slope).astype(BF16)
    grad_ref[...] = lax.dot_general(
        weight, grad_pre, (((1,), (1,)), ((), ())), preferred_element_type=F32
    ).astype(BF16)
    width = weight.shape[0]
    local_ref[:width] = lax.dot_general(
        aggregated, grad_pre, (((0,), (0,)), ((), ())), preferred_element_type=F32
    ).astype(BF16)
    local_ref[width:] = jnp.broadcast_to(
        jnp.sum(grad_pre.astype(F32), axis=0, keepdims=True),
        (local_ref.shape[0] - width, width),
    ).astype(BF16)


def dense(own, parts, weight, bias, cotangent):
    nodes, width = own.shape
    spec = pl.BlockSpec(memory_space=pltpu.VMEM)
    shapes = (
        jax.ShapeDtypeStruct((nodes, width), BF16),
        jax.ShapeDtypeStruct((width, nodes), BF16),
        jax.ShapeDtypeStruct((width + 16, width), BF16),
    )
    return pl.pallas_call(
        lambda *refs: dense_kernel(len(parts), *refs),
        out_shape=shapes,
        in_specs=[spec] * (4 + len(parts)),
        out_specs=(spec,) * 3,
        compiler_params=pltpu.CompilerParams(vmem_limit_bytes=16 << 20),
        cost_estimate=pl.CostEstimate(
            flops=6 * nodes * width * width,
            bytes_accessed=8 * nodes * width,
            transcendentals=nodes * width,
        ),
        name="dense",
    )(own, *parts, weight, bias.reshape(1, width), cotangent)


def back_kernel(panels, chosen, last, with_total, *refs):
    cell_ref, *grad_refs = refs[: 1 + len(panels)]
    rest = refs[1 + len(panels) :]
    width, nodes = grad_refs[0].shape
    runs = []
    for panel, ref in zip(panels, grad_refs):
        if runs and runs[-1][0] + len(runs[-1][1]) == panel:
            runs[-1][1].append(ref[...])
        else:
            runs.append((panel, [ref[...]]))
    runs = [(panel * nodes, jnp.concatenate(grads, axis=1)) for panel, grads in runs]

    def product(columns):
        value = None
        for top, grads in runs:
            part = jnp.dot(
                grads,
                cell_ref[top : top + grads.shape[1], columns],
                preferred_element_type=F32,
            )
            value = part if value is None else value + part
        return value

    out_refs = rest[with_total:]
    for index, panel in enumerate(chosen):
        columns = slice(panel * nodes, (panel + 1) * nodes)
        value = product(columns)
        if with_total:
            value = rest[0][:, columns] + value
        if last:
            out_refs[index][...] = value.T.astype(out_refs[index].dtype)
        else:
            out_refs[0][:, columns] = value


def back(panels, chosen, grads, cell, total=None, last=False):
    width, nodes = grads[0].shape
    spec = pl.BlockSpec(memory_space=pltpu.VMEM)
    operands = (cell, *grads) if total is None else (cell, *grads, total)
    if not last:
        outs = (pltpu.VMEM((width, cell.shape[1]), F32),)
    else:
        outs = tuple(
            pltpu.VMEM((nodes, width), F32 if panel == 0 else BF16) for panel in chosen
        )
    flops = 2 * len(panels) * len(chosen) * nodes * nodes * width
    return pl.pallas_call(
        lambda *refs: back_kernel(panels, chosen, last, total is not None, *refs),
        out_shape=outs,
        in_specs=[spec] * len(operands),
        out_specs=[spec] * len(outs),
        compiler_params=pltpu.CompilerParams(vmem_limit_bytes=24 << 20),
        cost_estimate=pl.CostEstimate(
            flops=flops, bytes_accessed=flops // 512, transcendentals=0
        ),
        name="back_last" if last else "back",
    )(*operands)


def finish_kernel(factor, value_ref, part_ref, other_ref, out_ref, weight_ref, bias_ref):
    out_ref[...] = value_ref[...].astype(out_ref.dtype)
    summed = (part_ref[...].astype(F32) + other_ref[...].astype(F32)) * factor
    width = weight_ref.shape[0]
    weight_ref[...] = summed[:width]
    bias_ref[...] = summed[width : width + 1]


def finish(value, part, other, factor):
    spec = pl.BlockSpec(memory_space=pltpu.VMEM)
    nodes, width = value.shape
    return pl.pallas_call(
        lambda *refs: finish_kernel(factor, *refs),
        out_shape=(
            jax.ShapeDtypeStruct((nodes, width), BF16),
            jax.ShapeDtypeStruct((width, width), F32),
            jax.ShapeDtypeStruct((1, width), F32),
        ),
        in_specs=[spec] * 3,
        out_specs=(spec,) * 3,
        compiler_params=pltpu.CompilerParams(vmem_limit_bytes=16 << 20),
        cost_estimate=pl.CostEstimate(
            flops=8 * nodes * width, bytes_accessed=16 * nodes * width, transcendentals=0
        ),
        name="finish",
    )(value, part, other)


def swap(value, axis, mask):
    count = lax.axis_size(axis)
    return lax.ppermute(value, axis, [(i, i ^ mask) for i in range(count)])


def move(value, pairs):
    pairs = [(2 * a + core, 2 * b + core) for a, b in pairs for core in range(2)]
    return lax.ppermute(value, "col", pairs)


def sum_far(far, chunk, ready):
    if lax.axis_size("col") != 8:
        count = lax.axis_size("col") // 2
        parts = [swap(chunk(k, far).astype(BF16), "col", 2 * k) for k in range(1, count - 1)]
        return [*parts, swap(far, "col", 2 * (count - 1))], chunk(0, far)
    passed = jnp.where(at_end(), 0.0, swap(far, "col", 2).astype(F32))
    later, ready = lax.optimization_barrier((far, ready))
    middle = move(later, [(1, 2), (2, 1)])
    both = (chunk(2, passed) + passed).astype(BF16)
    across = swap(both, "col", 4)
    near = swap(chunk(1, both).astype(BF16), "col", 2)
    return [near, across, middle], chunk(0, both)


def gather_far(value, count, hold):
    if count != 4:
        return [value] + [swap(value, "col", 2 * k) for k in range(1, count)], hold
    across, hold = lax.optimization_barrier((swap(value, "col", 4), hold))
    near = swap(value, "col", 2)
    passed = swap(across, "col", 2)
    middle = move(value, [(1, 2), (2, 1)])
    return [value, near, across, jnp.where(at_end(), passed, middle)], hold


def at_end():
    place = lax.axis_index("col") // 2
    return (place == 0) | (place == lax.axis_size("col") // 2 - 1)


def sum_over(value, axis, masks):
    for mask in masks:
        value = value.astype(F32) + swap(value, axis, mask).astype(F32)
        value = lax.optimization_barrier(value.astype(BF16))
    return value


def doublings(first, end):
    return [first << power for power in range((end // first).bit_length() - 1)]


def per_device(features, weight, bias, cotangent, tiles, tile_rows, tile_cols, tile_counts):
    block = tiles.shape[-1]
    nodes, width = features.shape
    row_count = lax.axis_size("row")
    col_count = lax.axis_size("col")
    half = col_count // 2
    factor = 1.0 / math.sqrt(nodes * row_count * col_count)

    source = jnp.zeros((row_count * nodes, width), BF16).at[:nodes].set(features)
    for k in range(row_count - 1, 0, -1):
        source = source.at[k * nodes : (k + 1) * nodes].set(swap(features, "row", k))
    cell = densify(
        tiles[0, 0], tile_rows, tile_cols, tile_counts, nodes // block, col_count, row_count
    )

    def cell_rows(core, k):
        top = (core * half + k) * nodes
        return cell[top : top + nodes]


    def cell_product(core, k, source):
        return jnp.dot(cell_rows(core, k), source, preferred_element_type=F32)

    far = half - 1
    from_mate = {
        k: swap(cell_product(1, k, source).astype(BF16), "col", 1) for k in (far, far - 1)
    }
    own_far = lax.optimization_barrier(cell_product(0, far, source))
    own_far = (own_far + from_mate[far].astype(F32)).astype(BF16)

    later, from_mate[far - 1] = lax.optimization_barrier((source, from_mate[far - 1]))
    for k in range(far - 1):
        from_mate[k] = swap(cell_product(1, k, later).astype(BF16), "col", 1)

    def chunk(k, hold):
        after, hold = lax.optimization_barrier((source, hold))
        return cell_product(0, k, after) + from_mate[k].astype(F32)

    parts, own = sum_far(own_far, chunk, from_mate[far - 1])
    hidden, grad_agg, local = dense(own, parts, weight, bias, cotangent)

    first, *masks = doublings(1, row_count)
    part = sum_over(local, "row", [first])
    own_grads, part = gather_far(grad_agg, half, part)
    part = sum_over(part, "row", masks)
    part = sum_over(part, "col", [1])
    mate_grads = [swap(grads, "col", 1) for grads in own_grads[:far]]

    if cell.size * 2 <= CELL_IN_VMEM:
        every = list(range(row_count))
        (total,) = back(list(range(far)), every, own_grads[:far], cell)
        (total,) = back(list(range(half, half + far)), every, mate_grads, cell, total)
        panels = [far, half + far]
        grads = [own_grads[far], swap(own_grads[far], "col", 1)]
        pieces = {}
        rest = total
        for chosen in ([row_count - 1], list(range(row_count - 2, 0, -1)), [0]):
            pieces.update(zip(chosen, back(panels, chosen, grads, cell, rest, True)))
            rest, pieces[chosen[-1]] = lax.optimization_barrier((total, pieces[chosen[-1]]))
    else:
        own = jnp.concatenate(own_grads, axis=1)
        mate_grads.append(swap(own_grads[far], "col", 1))
        mate = jnp.concatenate(mate_grads, axis=1)
        total = jnp.dot(own, cell[: half * nodes], preferred_element_type=F32)
        total = total + jnp.dot(mate, cell[half * nodes :], preferred_element_type=F32)
        pieces = {
            k: total[:, k * nodes : (k + 1) * nodes].T.astype(F32 if k == 0 else BF16)
            for k in range(row_count)
        }
    part, pieces[1] = lax.optimization_barrier((part, pieces[1]))
    landed = [swap(pieces[k], "row", k) for k in range(row_count - 1, 0, -1)]
    *masks, mask = doublings(2, col_count)
    part = sum_over(part, "col", masks)
    value = pieces[0]
    for piece in landed:
        value = value + piece.astype(F32)
    grad_features, grad_weight, grad_bias = finish(value, part, swap(part, "col", mask), factor)
    return (hidden, grad_weight, grad_bias[0], grad_features)


def solution(mesh):
    in_specs = (
        P(("col", "row"), None),
        P(),
        P(),
        P(("row", "col"), None),
        P("row", "col", None, None, None),
        P("row", "col", None),
        P("row", "col", None),
        P("row", "col"),
    )
    out_specs = (P(("row", "col"), None), P(), P(), P(("col", "row"), None))
    return jax.shard_map(
        per_device, mesh=mesh, in_specs=in_specs, out_specs=out_specs, check_vma=False
    )
```

```python
import math

import jax
import jax.numpy as jnp
from jax import lax
from jax.experimental import pallas as pl
from jax.experimental.pallas import tpu as pltpu
from jax.sharding import PartitionSpec as P

BF16 = jnp.bfloat16
F32 = jnp.float32
CELL_IN_VMEM = 1 << 24


def densify_kernel(per, half, one_band, rows_ref, cols_ref, count_ref, *refs):
    *window_refs, cell_ref = refs
    group, block, _ = window_refs[0].shape
    band = pl.program_id(0)
    step = pl.program_id(1)
    row_pos = lax.axis_index("row")
    col_pos = lax.axis_index("col")

    @pl.when(step == 0)
    def _():
        def clear(index, carry):
            cell_ref[pl.ds(pl.multiple_of(index * block, block), block), :] = jnp.zeros(
                (block, cell_ref.shape[1]), cell_ref.dtype
            )
            return carry

        lax.fori_loop(0, cell_ref.shape[0] // block, clear, 0)

    def put(window_ref, start, first, number):
        places = []
        for index in range(number):
            row = rows_ref[0, 0, start + first + index]
            col = cols_ref[0, 0, start + first + index]
            panel = lax.div(row, per)
            down = panel ^ col_pos
            down = (down & 1) * half + (down >> 1)
            top = ((down - panel) * per + row) * block - band * cell_ref.shape[0]
            panel = lax.div(col, per)
            left = (((panel ^ row_pos) - panel) * per + col) * block
            places.append((top, left))
        values = [window_ref[first + index] for index in range(number)]
        for (top, left), value in zip(places, values):

            def store(top=top, left=left, value=value):
                cell_ref[
                    pl.ds(pl.multiple_of(top, block), block),
                    pl.ds(pl.multiple_of(left, block), block),
                ] = value

            if one_band:
                store()
            else:
                pl.when((top >= 0) & (top < cell_ref.shape[0]))(store)

    for part, window_ref in enumerate(window_refs):
        start = (step * len(window_refs) + part) * group
        live = jnp.clip(count_ref[0, 0] - start, 0, group)

        def put_four(index, carry, window_ref=window_ref, start=start):
            put(window_ref, start, index * 4, 4)
            return carry

        lax.fori_loop(0, live >> 2, put_four, 0)

        def put_one(index, carry, window_ref=window_ref, start=start):
            put(window_ref, start, index, 1)
            return carry

        lax.fori_loop((live >> 2) << 2, live, put_one, 0)


def densify(tiles, rows, cols, count, per, col_count, row_count):
    slots, block, _ = tiles.shape
    group = math.gcd(slots, 32)
    windows = math.gcd(slots // group, 3)
    shape = (per * col_count * block, per * row_count * block)
    size = shape[0] * shape[1] * 2
    bands = max(1, size // CELL_IN_VMEM)
    space = pltpu.VMEM if bands == 1 else pltpu.HBM

    def tile_spec(part):
        def tile_map(band, step, rows_ref, cols_ref, count_ref):
            last = jnp.maximum(count_ref[0, 0] - 1, 0) // group
            return (jnp.minimum(step * windows + part, last), 0, 0)

        return pl.BlockSpec((group, block, block), tile_map)

    tiles = pltpu.with_memory_space_constraint(tiles, pltpu.HBM)
    return pl.pallas_call(
        lambda *refs: densify_kernel(per, col_count // 2, bands == 1, *refs),
        out_shape=space(shape, tiles.dtype),
        grid_spec=pltpu.PrefetchScalarGridSpec(
            num_scalar_prefetch=3,
            grid=(bands, slots // (group * windows)),
            in_specs=[tile_spec(part) for part in range(windows)],
            out_specs=pl.BlockSpec(
                (shape[0] // bands, shape[1]),
                lambda band, step, *refs: (band, 0),
                pipeline_mode=pl.Buffered(1),
            ),
        ),
        compiler_params=pltpu.CompilerParams(
            vmem_limit_bytes=size // bands + (10 << 20)
        ),
        cost_estimate=pl.CostEstimate(
            flops=0, bytes_accessed=2 * size, transcendentals=0
        ),
        name="densify",
    )(
        pltpu.with_memory_space_constraint(rows, pltpu.HBM),
        pltpu.with_memory_space_constraint(cols, pltpu.HBM),
        count,
        *[tiles] * windows,
    )


def dense_kernel(part_count, *refs):
    own_ref = refs[0]
    part_refs = refs[1 : 1 + part_count]
    weight_ref, bias_ref, cotangent_ref = refs[1 + part_count : 4 + part_count]
    hidden_ref, grad_ref, local_ref = refs[4 + part_count :]
    total = own_ref[...]
    for part_ref in part_refs:
        total = total + part_ref[...].astype(F32)
    aggregated = total.astype(BF16)
    weight = weight_ref[...]
    preact = jnp.dot(aggregated, weight, preferred_element_type=F32) + bias_ref[...]
    sigma = jax.nn.sigmoid(preact)
    hidden_ref[...] = (preact * sigma).astype(BF16)
    slope = sigma * (1.0 + preact * (1.0 - sigma))
    grad_pre = (cotangent_ref[...].astype(F32) * slope).astype(BF16)
    grad_ref[...] = lax.dot_general(
        weight, grad_pre, (((1,), (1,)), ((), ())), preferred_element_type=F32
    ).astype(BF16)
    width = weight.shape[0]
    local_ref[:width] = lax.dot_general(
        aggregated, grad_pre, (((0,), (0,)), ((), ())), preferred_element_type=F32
    ).astype(BF16)
    local_ref[width:] = jnp.broadcast_to(
        jnp.sum(grad_pre.astype(F32), axis=0, keepdims=True),
        (local_ref.shape[0] - width, width),
    ).astype(BF16)


def dense(own, parts, weight, bias, cotangent):
    nodes, width = own.shape
    spec = pl.BlockSpec(memory_space=pltpu.VMEM)
    shapes = (
        jax.ShapeDtypeStruct((nodes, width), BF16),
        jax.ShapeDtypeStruct((width, nodes), BF16),
        jax.ShapeDtypeStruct((width + 16, width), BF16),
    )
    return pl.pallas_call(
        lambda *refs: dense_kernel(len(parts), *refs),
        out_shape=shapes,
        in_specs=[spec] * (4 + len(parts)),
        out_specs=(spec,) * 3,
        compiler_params=pltpu.CompilerParams(vmem_limit_bytes=16 << 20),
        cost_estimate=pl.CostEstimate(
            flops=6 * nodes * width * width,
            bytes_accessed=8 * nodes * width,
            transcendentals=nodes * width,
        ),
        name="dense",
    )(own, *parts, weight, bias.reshape(1, width), cotangent)


def back_kernel(panels, chosen, last, with_total, *refs):
    cell_ref, *grad_refs = refs[: 1 + len(panels)]
    rest = refs[1 + len(panels) :]
    width, nodes = grad_refs[0].shape
    runs = []
    for panel, ref in zip(panels, grad_refs):
        if runs and runs[-1][0] + len(runs[-1][1]) == panel:
            runs[-1][1].append(ref[...])
        else:
            runs.append((panel, [ref[...]]))
    runs = [(panel * nodes, jnp.concatenate(grads, axis=1)) for panel, grads in runs]

    def product(columns):
        value = None
        for top, grads in runs:
            part = jnp.dot(
                grads,
                cell_ref[top : top + grads.shape[1], columns],
                preferred_element_type=F32,
            )
            value = part if value is None else value + part
        return value

    out_refs = rest[with_total:]
    for index, panel in enumerate(chosen):
        columns = slice(panel * nodes, (panel + 1) * nodes)
        value = product(columns)
        if with_total:
            value = rest[0][:, columns] + value
        if last:
            out_refs[index][...] = value.T.astype(out_refs[index].dtype)
        else:
            out_refs[0][:, columns] = value


def back(panels, chosen, grads, cell, total=None, last=False):
    width, nodes = grads[0].shape
    spec = pl.BlockSpec(memory_space=pltpu.VMEM)
    operands = (cell, *grads) if total is None else (cell, *grads, total)
    if not last:
        outs = (pltpu.VMEM((width, cell.shape[1]), F32),)
    else:
        outs = tuple(
            pltpu.VMEM((nodes, width), F32 if panel == 0 else BF16) for panel in chosen
        )
    flops = 2 * len(panels) * len(chosen) * nodes * nodes * width
    return pl.pallas_call(
        lambda *refs: back_kernel(panels, chosen, last, total is not None, *refs),
        out_shape=outs,
        in_specs=[spec] * len(operands),
        out_specs=[spec] * len(outs),
        compiler_params=pltpu.CompilerParams(vmem_limit_bytes=24 << 20),
        cost_estimate=pl.CostEstimate(
            flops=flops, bytes_accessed=flops // 512, transcendentals=0
        ),
        name="back_last" if last else "back",
    )(*operands)


def finish_kernel(factor, value_ref, part_ref, other_ref, out_ref, weight_ref, bias_ref):
    out_ref[...] = value_ref[...].astype(out_ref.dtype)
    summed = (part_ref[...].astype(F32) + other_ref[...].astype(F32)) * factor
    width = weight_ref.shape[0]
    weight_ref[...] = summed[:width]
    bias_ref[...] = summed[width : width + 1]


def finish(value, part, other, factor):
    spec = pl.BlockSpec(memory_space=pltpu.VMEM)
    nodes, width = value.shape
    return pl.pallas_call(
        lambda *refs: finish_kernel(factor, *refs),
        out_shape=(
            jax.ShapeDtypeStruct((nodes, width), BF16),
            jax.ShapeDtypeStruct((width, width), F32),
            jax.ShapeDtypeStruct((1, width), F32),
        ),
        in_specs=[spec] * 3,
        out_specs=(spec,) * 3,
        compiler_params=pltpu.CompilerParams(vmem_limit_bytes=16 << 20),
        cost_estimate=pl.CostEstimate(
            flops=8 * nodes * width, bytes_accessed=16 * nodes * width, transcendentals=0
        ),
        name="finish",
    )(value, part, other)


def swap(value, axis, mask):
    count = lax.axis_size(axis)
    return lax.ppermute(value, axis, [(i, i ^ mask) for i in range(count)])


def move(value, pairs):
    pairs = [(2 * a + core, 2 * b + core) for a, b in pairs for core in range(2)]
    return lax.ppermute(value, "col", pairs)


def sum_far(far, chunk, ready):
    if lax.axis_size("col") != 8:
        count = lax.axis_size("col") // 2
        parts = [swap(chunk(k, far).astype(BF16), "col", 2 * k) for k in range(1, count - 1)]
        return [*parts, swap(far, "col", 2 * (count - 1))], chunk(0, far)
    passed = jnp.where(at_end(), 0.0, swap(far, "col", 2).astype(F32))
    later, ready = lax.optimization_barrier((far, ready))
    middle = move(later, [(1, 2), (2, 1)])
    both = (chunk(2, passed) + passed).astype(BF16)
    across = swap(both, "col", 4)
    near = swap(chunk(1, both).astype(BF16), "col", 2)
    return [near, across, middle], chunk(0, both)


def gather_far(value, count, hold):
    if count != 4:
        return [value] + [swap(value, "col", 2 * k) for k in range(1, count)], hold
    across, hold = lax.optimization_barrier((swap(value, "col", 4), hold))
    near = swap(value, "col", 2)
    passed = swap(across, "col", 2)
    middle = move(value, [(1, 2), (2, 1)])
    return [value, near, across, jnp.where(at_end(), passed, middle)], hold


def at_end():
    place = lax.axis_index("col") // 2
    return (place == 0) | (place == lax.axis_size("col") // 2 - 1)


def sum_over(value, axis, masks):
    for mask in masks:
        value = value.astype(F32) + swap(value, axis, mask).astype(F32)
        value = lax.optimization_barrier(value.astype(BF16))
    return value


def doublings(first, end):
    return [first << power for power in range((end // first).bit_length() - 1)]


def per_device(features, weight, bias, cotangent, tiles, tile_rows, tile_cols, tile_counts):
    block = tiles.shape[-1]
    nodes, width = features.shape
    row_count = lax.axis_size("row")
    col_count = lax.axis_size("col")
    half = col_count // 2
    factor = 1.0 / math.sqrt(nodes * row_count * col_count)

    source = jnp.zeros((row_count * nodes, width), BF16).at[:nodes].set(features)
    for k in range(row_count - 1, 0, -1):
        source = source.at[k * nodes : (k + 1) * nodes].set(swap(features, "row", k))
    cell = densify(
        tiles[0, 0], tile_rows, tile_cols, tile_counts, nodes // block, col_count, row_count
    )

    def cell_rows(core, k):
        top = (core * half + k) * nodes
        return cell[top : top + nodes]


    def cell_product(core, k, source):
        return jnp.dot(cell_rows(core, k), source, preferred_element_type=F32)

    far = half - 1
    for_mate = cell_product(1, far, source).astype(BF16)
    after, for_mate = lax.optimization_barrier((source, for_mate))
    from_mate = {far: swap(for_mate, "col", 1)}
    from_mate[far - 1] = swap(cell_product(1, far - 1, after).astype(BF16), "col", 1)
    own_far = lax.optimization_barrier(cell_product(0, far, after))
    later, from_mate[far] = lax.optimization_barrier((after, from_mate[far]))
    own_far = (own_far + from_mate[far].astype(F32)).astype(BF16)
    for k in range(far - 1):
        from_mate[k] = swap(cell_product(1, k, later).astype(BF16), "col", 1)

    def chunk(k, hold):
        after, hold = lax.optimization_barrier((source, hold))
        return cell_product(0, k, after) + from_mate[k].astype(F32)

    parts, own = sum_far(own_far, chunk, from_mate[far - 1])
    hidden, grad_agg, local = dense(own, parts, weight, bias, cotangent)

    first, *masks = doublings(1, row_count)
    part = sum_over(local, "row", [first])
    own_grads, part = gather_far(grad_agg, half, part)
    part = sum_over(part, "row", masks)
    part = sum_over(part, "col", [1])
    mate_grads = [swap(grads, "col", 1) for grads in own_grads[:far]]

    if cell.size * 2 <= CELL_IN_VMEM:
        every = list(range(row_count))
        (total,) = back(list(range(far)), every, own_grads[:far], cell)
        (total,) = back(list(range(half, half + far)), every, mate_grads, cell, total)
        panels = [far, half + far]
        grads = [own_grads[far], swap(own_grads[far], "col", 1)]
        pieces = {}
        rest = total
        for chosen in ([row_count - 1], list(range(row_count - 2, 0, -1)), [0]):
            pieces.update(zip(chosen, back(panels, chosen, grads, cell, rest, True)))
            rest, pieces[chosen[-1]] = lax.optimization_barrier((total, pieces[chosen[-1]]))
    else:
        own = jnp.concatenate(own_grads, axis=1)
        mate_grads.append(swap(own_grads[far], "col", 1))
        mate = jnp.concatenate(mate_grads, axis=1)
        total = jnp.dot(own, cell[: half * nodes], preferred_element_type=F32)
        total = total + jnp.dot(mate, cell[half * nodes :], preferred_element_type=F32)
        pieces = {
            k: total[:, k * nodes : (k + 1) * nodes].T.astype(F32 if k == 0 else BF16)
            for k in range(row_count)
        }
    part, pieces[1] = lax.optimization_barrier((part, pieces[1]))
    landed = [swap(pieces[k], "row", k) for k in range(row_count - 1, 0, -1)]
    *masks, mask = doublings(2, col_count)
    part = sum_over(part, "col", masks)
    value = pieces[0]
    for piece in landed:
        value = value + piece.astype(F32)
    grad_features, grad_weight, grad_bias = finish(value, part, swap(part, "col", mask), factor)
    return (hidden, grad_weight, grad_bias[0], grad_features)


def solution(mesh):
    in_specs = (
        P(("col", "row"), None),
        P(),
        P(),
        P(("row", "col"), None),
        P("row", "col", None, None, None),
        P("row", "col", None),
        P("row", "col", None),
        P("row", "col"),
    )
    out_specs = (P(("row", "col"), None), P(), P(), P(("col", "row"), None))
    return jax.shard_map(
        per_device, mesh=mesh, in_specs=in_specs, out_specs=out_specs, check_vma=False
    )
```

```python
import math

import jax
import jax.numpy as jnp
from jax import lax
from jax.experimental import pallas as pl
from jax.experimental.pallas import tpu as pltpu
from jax.sharding import PartitionSpec as P

BF16 = jnp.bfloat16
F32 = jnp.float32
CELL_IN_VMEM = 1 << 24


def densify_kernel(per, half, one_band, rows_ref, cols_ref, count_ref, *refs):
    *window_refs, cell_ref = refs
    group, block, _ = window_refs[0].shape
    band = pl.program_id(0)
    step = pl.program_id(1)
    row_pos = lax.axis_index("row")
    col_pos = lax.axis_index("col")

    @pl.when(step == 0)
    def _():
        def clear(index, carry):
            cell_ref[pl.ds(pl.multiple_of(index * block, block), block), :] = jnp.zeros(
                (block, cell_ref.shape[1]), cell_ref.dtype
            )
            return carry

        lax.fori_loop(0, cell_ref.shape[0] // block, clear, 0)

    def put(window_ref, start, first, number):
        places = []
        for index in range(number):
            row = rows_ref[0, 0, start + first + index]
            col = cols_ref[0, 0, start + first + index]
            panel = lax.div(row, per)
            down = panel ^ col_pos
            down = (down & 1) * half + (down >> 1)
            top = ((down - panel) * per + row) * block - band * cell_ref.shape[0]
            panel = lax.div(col, per)
            left = (((panel ^ row_pos) - panel) * per + col) * block
            places.append((top, left))
        values = [window_ref[first + index] for index in range(number)]
        for (top, left), value in zip(places, values):

            def store(top=top, left=left, value=value):
                cell_ref[
                    pl.ds(pl.multiple_of(top, block), block),
                    pl.ds(pl.multiple_of(left, block), block),
                ] = value

            if one_band:
                store()
            else:
                pl.when((top >= 0) & (top < cell_ref.shape[0]))(store)

    for part, window_ref in enumerate(window_refs):
        start = (step * len(window_refs) + part) * group
        live = jnp.clip(count_ref[0, 0] - start, 0, group)

        def put_four(index, carry, window_ref=window_ref, start=start):
            put(window_ref, start, index * 4, 4)
            return carry

        lax.fori_loop(0, live >> 2, put_four, 0)

        def put_one(index, carry, window_ref=window_ref, start=start):
            put(window_ref, start, index, 1)
            return carry

        lax.fori_loop((live >> 2) << 2, live, put_one, 0)


def densify(tiles, rows, cols, count, per, col_count, row_count):
    slots, block, _ = tiles.shape
    group = math.gcd(slots, 32)
    windows = math.gcd(slots // group, 3)
    shape = (per * col_count * block, per * row_count * block)
    size = shape[0] * shape[1] * 2
    bands = max(1, size // CELL_IN_VMEM)
    space = pltpu.VMEM if bands == 1 else pltpu.HBM

    def tile_spec(part):
        def tile_map(band, step, rows_ref, cols_ref, count_ref):
            last = jnp.maximum(count_ref[0, 0] - 1, 0) // group
            return (jnp.minimum(step * windows + part, last), 0, 0)

        return pl.BlockSpec((group, block, block), tile_map)

    tiles = pltpu.with_memory_space_constraint(tiles, pltpu.HBM)
    return pl.pallas_call(
        lambda *refs: densify_kernel(per, col_count // 2, bands == 1, *refs),
        out_shape=space(shape, tiles.dtype),
        grid_spec=pltpu.PrefetchScalarGridSpec(
            num_scalar_prefetch=3,
            grid=(bands, slots // (group * windows)),
            in_specs=[tile_spec(part) for part in range(windows)],
            out_specs=pl.BlockSpec(
                (shape[0] // bands, shape[1]),
                lambda band, step, *refs: (band, 0),
                pipeline_mode=pl.Buffered(1),
            ),
        ),
        compiler_params=pltpu.CompilerParams(
            vmem_limit_bytes=size // bands + (10 << 20)
        ),
        cost_estimate=pl.CostEstimate(
            flops=0, bytes_accessed=2 * size, transcendentals=0
        ),
        name="densify",
    )(
        pltpu.with_memory_space_constraint(rows, pltpu.HBM),
        pltpu.with_memory_space_constraint(cols, pltpu.HBM),
        count,
        *[tiles] * windows,
    )


def dense_kernel(part_count, *refs):
    own_ref = refs[0]
    part_refs = refs[1 : 1 + part_count]
    weight_ref, bias_ref, cotangent_ref = refs[1 + part_count : 4 + part_count]
    hidden_ref, grad_ref, local_ref = refs[4 + part_count :]
    total = own_ref[...]
    for part_ref in part_refs:
        total = total + part_ref[...].astype(F32)
    aggregated = total.astype(BF16)
    weight = weight_ref[...]
    preact = jnp.dot(aggregated, weight, preferred_element_type=F32) + bias_ref[...]
    sigma = jax.nn.sigmoid(preact)
    hidden_ref[...] = (preact * sigma).astype(BF16)
    slope = sigma * (1.0 + preact * (1.0 - sigma))
    grad_pre = (cotangent_ref[...].astype(F32) * slope).astype(BF16)
    grad_ref[...] = lax.dot_general(
        weight, grad_pre, (((1,), (1,)), ((), ())), preferred_element_type=F32
    ).astype(BF16)
    width = weight.shape[0]
    local_ref[:width] = lax.dot_general(
        aggregated, grad_pre, (((0,), (0,)), ((), ())), preferred_element_type=F32
    ).astype(BF16)
    local_ref[width:] = jnp.broadcast_to(
        jnp.sum(grad_pre.astype(F32), axis=0, keepdims=True),
        (local_ref.shape[0] - width, width),
    ).astype(BF16)


def dense(own, parts, weight, bias, cotangent):
    nodes, width = own.shape
    spec = pl.BlockSpec(memory_space=pltpu.VMEM)
    shapes = (
        jax.ShapeDtypeStruct((nodes, width), BF16),
        jax.ShapeDtypeStruct((width, nodes), BF16),
        jax.ShapeDtypeStruct((width + 16, width), BF16),
    )
    return pl.pallas_call(
        lambda *refs: dense_kernel(len(parts), *refs),
        out_shape=shapes,
        in_specs=[spec] * (4 + len(parts)),
        out_specs=(spec,) * 3,
        compiler_params=pltpu.CompilerParams(vmem_limit_bytes=16 << 20),
        cost_estimate=pl.CostEstimate(
            flops=6 * nodes * width * width,
            bytes_accessed=8 * nodes * width,
            transcendentals=nodes * width,
        ),
        name="dense",
    )(own, *parts, weight, bias.reshape(1, width), cotangent)


def back_kernel(panels, chosen, last, with_total, *refs):
    cell_ref, *grad_refs = refs[: 1 + len(panels)]
    rest = refs[1 + len(panels) :]
    width, nodes = grad_refs[0].shape
    runs = []
    for panel, ref in zip(panels, grad_refs):
        if runs and runs[-1][0] + len(runs[-1][1]) == panel:
            runs[-1][1].append(ref[...])
        else:
            runs.append((panel, [ref[...]]))
    runs = [(panel * nodes, jnp.concatenate(grads, axis=1)) for panel, grads in runs]

    def product(columns):
        value = None
        for top, grads in runs:
            part = jnp.dot(
                grads,
                cell_ref[top : top + grads.shape[1], columns],
                preferred_element_type=F32,
            )
            value = part if value is None else value + part
        return value

    out_refs = rest[with_total:]
    for index, panel in enumerate(chosen):
        columns = slice(panel * nodes, (panel + 1) * nodes)
        value = product(columns)
        if with_total:
            value = rest[0][:, columns] + value
        if last:
            out_refs[index][...] = value.T.astype(out_refs[index].dtype)
        else:
            out_refs[0][:, columns] = value


def back(panels, chosen, grads, cell, total=None, last=False):
    width, nodes = grads[0].shape
    spec = pl.BlockSpec(memory_space=pltpu.VMEM)
    operands = (cell, *grads) if total is None else (cell, *grads, total)
    if not last:
        outs = (pltpu.VMEM((width, cell.shape[1]), F32),)
    else:
        outs = tuple(
            pltpu.VMEM((nodes, width), F32 if panel == 0 else BF16) for panel in chosen
        )
    flops = 2 * len(panels) * len(chosen) * nodes * nodes * width
    return pl.pallas_call(
        lambda *refs: back_kernel(panels, chosen, last, total is not None, *refs),
        out_shape=outs,
        in_specs=[spec] * len(operands),
        out_specs=[spec] * len(outs),
        compiler_params=pltpu.CompilerParams(vmem_limit_bytes=24 << 20),
        cost_estimate=pl.CostEstimate(
            flops=flops, bytes_accessed=flops // 512, transcendentals=0
        ),
        name="back_last" if last else "back",
    )(*operands)


def finish_kernel(factor, value_ref, part_ref, other_ref, out_ref, weight_ref, bias_ref):
    out_ref[...] = value_ref[...].astype(out_ref.dtype)
    summed = (part_ref[...].astype(F32) + other_ref[...].astype(F32)) * factor
    width = weight_ref.shape[0]
    weight_ref[...] = summed[:width]
    bias_ref[...] = summed[width : width + 1]


def finish(value, part, other, factor):
    spec = pl.BlockSpec(memory_space=pltpu.VMEM)
    nodes, width = value.shape
    return pl.pallas_call(
        lambda *refs: finish_kernel(factor, *refs),
        out_shape=(
            jax.ShapeDtypeStruct((nodes, width), BF16),
            jax.ShapeDtypeStruct((width, width), F32),
            jax.ShapeDtypeStruct((1, width), F32),
        ),
        in_specs=[spec] * 3,
        out_specs=(spec,) * 3,
        compiler_params=pltpu.CompilerParams(vmem_limit_bytes=16 << 20),
        cost_estimate=pl.CostEstimate(
            flops=8 * nodes * width, bytes_accessed=16 * nodes * width, transcendentals=0
        ),
        name="finish",
    )(value, part, other)


def swap(value, axis, mask):
    count = lax.axis_size(axis)
    return lax.ppermute(value, axis, [(i, i ^ mask) for i in range(count)])


def move(value, pairs):
    pairs = [(2 * a + core, 2 * b + core) for a, b in pairs for core in range(2)]
    return lax.ppermute(value, "col", pairs)


def sum_far(far, chunk, ready):
    if lax.axis_size("col") != 8:
        count = lax.axis_size("col") // 2
        parts = [swap(chunk(k, far).astype(BF16), "col", 2 * k) for k in range(1, count - 1)]
        return [*parts, swap(far, "col", 2 * (count - 1))], chunk(0, far)
    passed = jnp.where(at_end(), 0.0, swap(far, "col", 2).astype(F32))
    later, ready = lax.optimization_barrier((far, ready))
    middle = move(later, [(1, 2), (2, 1)])
    both = (chunk(2, passed) + passed).astype(BF16)
    across = swap(both, "col", 4)
    near = swap(chunk(1, both).astype(BF16), "col", 2)
    return [near, across, middle], chunk(0, both)


def gather_far(value, count, hold):
    if count != 4:
        return [value] + [swap(value, "col", 2 * k) for k in range(1, count)], hold
    across, hold = lax.optimization_barrier((swap(value, "col", 4), hold))
    near = swap(value, "col", 2)
    passed = swap(across, "col", 2)
    middle = move(value, [(1, 2), (2, 1)])
    return [value, near, across, jnp.where(at_end(), passed, middle)], hold


def at_end():
    place = lax.axis_index("col") // 2
    return (place == 0) | (place == lax.axis_size("col") // 2 - 1)


def sum_over(value, axis, masks):
    for mask in masks:
        value = value.astype(F32) + swap(value, axis, mask).astype(F32)
        value = lax.optimization_barrier(value.astype(BF16))
    return value


def doublings(first, end):
    return [first << power for power in range((end // first).bit_length() - 1)]


def per_device(features, weight, bias, cotangent, tiles, tile_rows, tile_cols, tile_counts):
    block = tiles.shape[-1]
    nodes, width = features.shape
    row_count = lax.axis_size("row")
    col_count = lax.axis_size("col")
    half = col_count // 2
    factor = 1.0 / math.sqrt(nodes * row_count * col_count)

    source = jnp.zeros((row_count * nodes, width), BF16).at[:nodes].set(features)
    for k in range(row_count - 1, 0, -1):
        source = source.at[k * nodes : (k + 1) * nodes].set(swap(features, "row", k))
    cell = densify(
        tiles[0, 0], tile_rows, tile_cols, tile_counts, nodes // block, col_count, row_count
    )

    def cell_rows(core, k):
        top = (core * half + k) * nodes
        return cell[top : top + nodes]


    def cell_product(core, k, source):
        return jnp.dot(cell_rows(core, k), source, preferred_element_type=F32)

    far = half - 1
    from_mate = {
        k: swap(cell_product(1, k, source).astype(BF16), "col", 1) for k in (far, far - 1)
    }
    own_far = lax.optimization_barrier(cell_product(0, far, source))
    own_far = (own_far + from_mate[far].astype(F32)).astype(BF16)

    later, from_mate[far - 1] = lax.optimization_barrier((source, from_mate[far - 1]))
    for k in range(far - 1):
        from_mate[k] = swap(cell_product(1, k, later).astype(BF16), "col", 1)

    def chunk(k, hold):
        after, hold = lax.optimization_barrier((source, hold))
        return cell_product(0, k, after) + from_mate[k].astype(F32)

    parts, own = sum_far(own_far, chunk, from_mate[far - 1])
    hidden, grad_agg, local = dense(own, parts, weight, bias, cotangent)

    first, *masks = doublings(1, row_count)
    own_grads, other = gather_far(grad_agg, half, swap(local, "row", first))
    part = lax.optimization_barrier((local.astype(F32) + other.astype(F32)).astype(BF16))
    part = sum_over(part, "row", masks)
    part = sum_over(part, "col", [1])
    mate_grads = [swap(grads, "col", 1) for grads in own_grads[:far]]

    if cell.size * 2 <= CELL_IN_VMEM:
        every = list(range(row_count))
        (total,) = back(list(range(far)), every, own_grads[:far], cell)
        (total,) = back(list(range(half, half + far)), every, mate_grads, cell, total)
        panels = [far, half + far]
        grads = [own_grads[far], swap(own_grads[far], "col", 1)]
        outer, inner = row_count - 1, list(range(row_count - 2, 0, -1))
        pieces = dict(zip([outer], back(panels, [outer], grads, cell, total, True)))
        rest, part, pieces[outer] = lax.optimization_barrier((total, part, pieces[outer]))
        landed = {outer: swap(pieces[outer], "row", outer)}
        pieces.update(zip(inner, back(panels, inner, grads, cell, rest, True)))
        rest, landed[outer] = lax.optimization_barrier((total, landed[outer]))
        pieces.update(zip([0], back(panels, [0], grads, cell, rest, True)))
    else:
        own = jnp.concatenate(own_grads, axis=1)
        mate_grads.append(swap(own_grads[far], "col", 1))
        mate = jnp.concatenate(mate_grads, axis=1)
        total = jnp.dot(own, cell[: half * nodes], preferred_element_type=F32)
        total = total + jnp.dot(mate, cell[half * nodes :], preferred_element_type=F32)
        pieces = {
            k: total[:, k * nodes : (k + 1) * nodes].T.astype(F32 if k == 0 else BF16)
            for k in range(row_count)
        }
        landed = {}
    for k in range(1, row_count):
        if k not in landed:
            landed[k] = swap(pieces[k], "row", k)
    *masks, mask = doublings(2, col_count)
    part = sum_over(part, "col", masks)
    value = pieces[0]
    for piece in landed.values():
        value = value + piece.astype(F32)
    grad_features, grad_weight, grad_bias = finish(value, part, swap(part, "col", mask), factor)
    return (hidden, grad_weight, grad_bias[0], grad_features)


def solution(mesh):
    in_specs = (
        P(("col", "row"), None),
        P(),
        P(),
        P(("row", "col"), None),
        P("row", "col", None, None, None),
        P("row", "col", None),
        P("row", "col", None),
        P("row", "col"),
    )
    out_specs = (P(("row", "col"), None), P(), P(), P(("col", "row"), None))
    return jax.shard_map(
        per_device, mesh=mesh, in_specs=in_specs, out_specs=out_specs, check_vma=False
    )
```

```python
import math

import jax
import jax.numpy as jnp
from jax import lax
from jax.experimental import pallas as pl
from jax.experimental.pallas import tpu as pltpu
from jax.sharding import PartitionSpec as P

BF16 = jnp.bfloat16
F32 = jnp.float32
CELL_IN_VMEM = 1 << 24


def densify_kernel(per, half, one_band, rows_ref, cols_ref, count_ref, *refs):
    *window_refs, cell_ref = refs
    group, block, _ = window_refs[0].shape
    band = pl.program_id(0)
    step = pl.program_id(1)
    row_pos = lax.axis_index("row")
    col_pos = lax.axis_index("col")

    @pl.when(step == 0)
    def _():
        def clear(index, carry):
            cell_ref[pl.ds(pl.multiple_of(index * block, block), block), :] = jnp.zeros(
                (block, cell_ref.shape[1]), cell_ref.dtype
            )
            return carry

        lax.fori_loop(0, cell_ref.shape[0] // block, clear, 0)

    def put(window_ref, start, first, number):
        places = []
        for index in range(number):
            row = rows_ref[0, 0, start + first + index]
            col = cols_ref[0, 0, start + first + index]
            panel = lax.div(row, per)
            down = panel ^ col_pos
            down = (down & 1) * half + (down >> 1)
            top = ((down - panel) * per + row) * block - band * cell_ref.shape[0]
            panel = lax.div(col, per)
            left = (((panel ^ row_pos) - panel) * per + col) * block
            places.append((top, left))
        values = [window_ref[first + index] for index in range(number)]
        for (top, left), value in zip(places, values):

            def store(top=top, left=left, value=value):
                cell_ref[
                    pl.ds(pl.multiple_of(top, block), block),
                    pl.ds(pl.multiple_of(left, block), block),
                ] = value

            if one_band:
                store()
            else:
                pl.when((top >= 0) & (top < cell_ref.shape[0]))(store)

    for part, window_ref in enumerate(window_refs):
        start = (step * len(window_refs) + part) * group
        live = jnp.clip(count_ref[0, 0] - start, 0, group)

        def put_four(index, carry, window_ref=window_ref, start=start):
            put(window_ref, start, index * 4, 4)
            return carry

        lax.fori_loop(0, live >> 2, put_four, 0)

        def put_one(index, carry, window_ref=window_ref, start=start):
            put(window_ref, start, index, 1)
            return carry

        lax.fori_loop((live >> 2) << 2, live, put_one, 0)


def densify(tiles, rows, cols, count, per, col_count, row_count):
    slots, block, _ = tiles.shape
    group = math.gcd(slots, 32)
    windows = math.gcd(slots // group, 3)
    shape = (per * col_count * block, per * row_count * block)
    size = shape[0] * shape[1] * 2
    bands = max(1, size // CELL_IN_VMEM)
    space = pltpu.VMEM if bands == 1 else pltpu.HBM

    def tile_spec(part):
        def tile_map(band, step, rows_ref, cols_ref, count_ref):
            last = jnp.maximum(count_ref[0, 0] - 1, 0) // group
            return (jnp.minimum(step * windows + part, last), 0, 0)

        return pl.BlockSpec((group, block, block), tile_map)

    tiles = pltpu.with_memory_space_constraint(tiles, pltpu.HBM)
    return pl.pallas_call(
        lambda *refs: densify_kernel(per, col_count // 2, bands == 1, *refs),
        out_shape=space(shape, tiles.dtype),
        grid_spec=pltpu.PrefetchScalarGridSpec(
            num_scalar_prefetch=3,
            grid=(bands, slots // (group * windows)),
            in_specs=[tile_spec(part) for part in range(windows)],
            out_specs=pl.BlockSpec(
                (shape[0] // bands, shape[1]),
                lambda band, step, *refs: (band, 0),
                pipeline_mode=pl.Buffered(1),
            ),
        ),
        compiler_params=pltpu.CompilerParams(
            vmem_limit_bytes=size // bands + (10 << 20)
        ),
        cost_estimate=pl.CostEstimate(
            flops=0, bytes_accessed=2 * size, transcendentals=0
        ),
        name="densify",
    )(
        pltpu.with_memory_space_constraint(rows, pltpu.HBM),
        pltpu.with_memory_space_constraint(cols, pltpu.HBM),
        count,
        *[tiles] * windows,
    )


def dense_kernel(part_count, *refs):
    own_ref = refs[0]
    part_refs = refs[1 : 1 + part_count]
    weight_ref, bias_ref, cotangent_ref = refs[1 + part_count : 4 + part_count]
    hidden_ref, grad_ref, local_ref = refs[4 + part_count :]
    total = own_ref[...]
    for part_ref in part_refs:
        total = total + part_ref[...].astype(F32)
    aggregated = total.astype(BF16)
    weight = weight_ref[...]
    preact = jnp.dot(aggregated, weight, preferred_element_type=F32) + bias_ref[...]
    sigma = jax.nn.sigmoid(preact)
    hidden_ref[...] = (preact * sigma).astype(BF16)
    slope = sigma * (1.0 + preact * (1.0 - sigma))
    grad_pre = (cotangent_ref[...].astype(F32) * slope).astype(BF16)
    grad_ref[...] = lax.dot_general(
        weight, grad_pre, (((1,), (1,)), ((), ())), preferred_element_type=F32
    ).astype(BF16)
    width = weight.shape[0]
    local_ref[:width] = lax.dot_general(
        aggregated, grad_pre, (((0,), (0,)), ((), ())), preferred_element_type=F32
    ).astype(BF16)
    local_ref[width:] = jnp.broadcast_to(
        jnp.sum(grad_pre.astype(F32), axis=0, keepdims=True),
        (local_ref.shape[0] - width, width),
    ).astype(BF16)


def dense(own, parts, weight, bias, cotangent):
    nodes, width = own.shape
    spec = pl.BlockSpec(memory_space=pltpu.VMEM)
    shapes = (
        jax.ShapeDtypeStruct((nodes, width), BF16),
        jax.ShapeDtypeStruct((width, nodes), BF16),
        jax.ShapeDtypeStruct((width + 16, width), BF16),
    )
    return pl.pallas_call(
        lambda *refs: dense_kernel(len(parts), *refs),
        out_shape=shapes,
        in_specs=[spec] * (4 + len(parts)),
        out_specs=(spec,) * 3,
        compiler_params=pltpu.CompilerParams(vmem_limit_bytes=16 << 20),
        cost_estimate=pl.CostEstimate(
            flops=6 * nodes * width * width,
            bytes_accessed=8 * nodes * width,
            transcendentals=nodes * width,
        ),
        name="dense",
    )(own, *parts, weight, bias.reshape(1, width), cotangent)


def back_kernel(panels, chosen, last, with_total, *refs):
    cell_ref, *grad_refs = refs[: 1 + len(panels)]
    rest = refs[1 + len(panels) :]
    width, nodes = grad_refs[0].shape
    runs = []
    for panel, ref in zip(panels, grad_refs):
        if runs and runs[-1][0] + len(runs[-1][1]) == panel:
            runs[-1][1].append(ref[...])
        else:
            runs.append((panel, [ref[...]]))
    runs = [(panel * nodes, jnp.concatenate(grads, axis=1)) for panel, grads in runs]

    def product(columns):
        value = None
        for top, grads in runs:
            part = jnp.dot(
                grads,
                cell_ref[top : top + grads.shape[1], columns],
                preferred_element_type=F32,
            )
            value = part if value is None else value + part
        return value

    out_refs = rest[with_total:]
    for index, panel in enumerate(chosen):
        columns = slice(panel * nodes, (panel + 1) * nodes)
        value = product(columns)
        if with_total:
            value = rest[0][:, columns] + value
        if last:
            out_refs[index][...] = value.T.astype(out_refs[index].dtype)
        else:
            out_refs[0][:, columns] = value


def back(panels, chosen, grads, cell, total=None, last=False):
    width, nodes = grads[0].shape
    spec = pl.BlockSpec(memory_space=pltpu.VMEM)
    operands = (cell, *grads) if total is None else (cell, *grads, total)
    if not last:
        outs = (pltpu.VMEM((width, cell.shape[1]), F32),)
    else:
        outs = tuple(
            pltpu.VMEM((nodes, width), F32 if panel == 0 else BF16) for panel in chosen
        )
    flops = 2 * len(panels) * len(chosen) * nodes * nodes * width
    return pl.pallas_call(
        lambda *refs: back_kernel(panels, chosen, last, total is not None, *refs),
        out_shape=outs,
        in_specs=[spec] * len(operands),
        out_specs=[spec] * len(outs),
        compiler_params=pltpu.CompilerParams(vmem_limit_bytes=24 << 20),
        cost_estimate=pl.CostEstimate(
            flops=flops, bytes_accessed=flops // 512, transcendentals=0
        ),
        name="back_last" if last else "back",
    )(*operands)


def finish_kernel(factor, value_ref, part_ref, other_ref, out_ref, weight_ref, bias_ref):
    out_ref[...] = value_ref[...].astype(out_ref.dtype)
    summed = (part_ref[...].astype(F32) + other_ref[...].astype(F32)) * factor
    width = weight_ref.shape[0]
    weight_ref[...] = summed[:width]
    bias_ref[...] = summed[width : width + 1]


def finish(value, part, other, factor):
    spec = pl.BlockSpec(memory_space=pltpu.VMEM)
    nodes, width = value.shape
    return pl.pallas_call(
        lambda *refs: finish_kernel(factor, *refs),
        out_shape=(
            jax.ShapeDtypeStruct((nodes, width), BF16),
            jax.ShapeDtypeStruct((width, width), F32),
            jax.ShapeDtypeStruct((1, width), F32),
        ),
        in_specs=[spec] * 3,
        out_specs=(spec,) * 3,
        compiler_params=pltpu.CompilerParams(vmem_limit_bytes=16 << 20),
        cost_estimate=pl.CostEstimate(
            flops=8 * nodes * width, bytes_accessed=16 * nodes * width, transcendentals=0
        ),
        name="finish",
    )(value, part, other)


def swap(value, axis, mask):
    count = lax.axis_size(axis)
    return lax.ppermute(value, axis, [(i, i ^ mask) for i in range(count)])


def move(value, pairs):
    pairs = [(2 * a + core, 2 * b + core) for a, b in pairs for core in range(2)]
    return lax.ppermute(value, "col", pairs)


def sum_far(far, chunk, ready):
    if lax.axis_size("col") != 8:
        count = lax.axis_size("col") // 2
        parts = [swap(chunk(k, far).astype(BF16), "col", 2 * k) for k in range(1, count - 1)]
        return [*parts, swap(far, "col", 2 * (count - 1))], chunk(0, far)
    passed = jnp.where(at_end(), 0.0, swap(far, "col", 2).astype(F32))
    later, ready = lax.optimization_barrier((far, ready))
    middle = move(later, [(1, 2), (2, 1)])
    both = (chunk(2, passed) + passed).astype(BF16)
    across = swap(both, "col", 4)
    near = swap(chunk(1, both).astype(BF16), "col", 2)
    return [near, across, middle], chunk(0, both)


def gather_far(value, count, hold):
    if count != 4:
        return [value] + [swap(value, "col", 2 * k) for k in range(1, count)], hold
    later, hold = lax.optimization_barrier((value, hold))
    across, hold = lax.optimization_barrier((swap(value, "col", 4), hold))
    near = swap(value, "col", 2)
    passed = swap(across, "col", 2)
    middle = move(later, [(1, 2), (2, 1)])
    return [value, near, across, jnp.where(at_end(), passed, middle)], hold


def at_end():
    place = lax.axis_index("col") // 2
    return (place == 0) | (place == lax.axis_size("col") // 2 - 1)


def sum_over(value, axis, masks):
    for mask in masks:
        value = value.astype(F32) + swap(value, axis, mask).astype(F32)
        value = lax.optimization_barrier(value.astype(BF16))
    return value


def doublings(first, end):
    return [first << power for power in range((end // first).bit_length() - 1)]


def per_device(features, weight, bias, cotangent, tiles, tile_rows, tile_cols, tile_counts):
    block = tiles.shape[-1]
    nodes, width = features.shape
    row_count = lax.axis_size("row")
    col_count = lax.axis_size("col")
    half = col_count // 2
    factor = 1.0 / math.sqrt(nodes * row_count * col_count)

    source = jnp.zeros((row_count * nodes, width), BF16).at[:nodes].set(features)
    for k in range(row_count - 1, 0, -1):
        source = source.at[k * nodes : (k + 1) * nodes].set(swap(features, "row", k))
    cell = densify(
        tiles[0, 0], tile_rows, tile_cols, tile_counts, nodes // block, col_count, row_count
    )

    def cell_rows(core, k):
        top = (core * half + k) * nodes
        return cell[top : top + nodes]


    def cell_product(core, k, source):
        return jnp.dot(cell_rows(core, k), source, preferred_element_type=F32)

    far = half - 1
    from_mate = {
        k: swap(cell_product(1, k, source).astype(BF16), "col", 1) for k in (far, far - 1)
    }
    own_far = lax.optimization_barrier(cell_product(0, far, source))
    own_far = (own_far + from_mate[far].astype(F32)).astype(BF16)

    later, from_mate[far - 1] = lax.optimization_barrier((source, from_mate[far - 1]))
    for k in range(far - 1):
        from_mate[k] = swap(cell_product(1, k, later).astype(BF16), "col", 1)

    def chunk(k, hold):
        after, hold = lax.optimization_barrier((source, hold))
        return cell_product(0, k, after) + from_mate[k].astype(F32)

    parts, own = sum_far(own_far, chunk, from_mate[far - 1])
    hidden, grad_agg, local = dense(own, parts, weight, bias, cotangent)

    first, *masks = doublings(1, row_count)
    own_grads, other = gather_far(grad_agg, half, swap(local, "row", first))
    part = lax.optimization_barrier((local.astype(F32) + other.astype(F32)).astype(BF16))
    part = sum_over(part, "row", masks)
    part = sum_over(part, "col", [1])
    mate_grads = [swap(grads, "col", 1) for grads in own_grads[:far]]

    if cell.size * 2 <= CELL_IN_VMEM:
        every = list(range(row_count))
        (total,) = back(list(range(far)), every, own_grads[:far], cell)
        (total,) = back(list(range(half, half + far)), every, mate_grads, cell, total)
        panels = [far, half + far]
        grads = [own_grads[far], swap(own_grads[far], "col", 1)]
        outer, inner = row_count - 1, list(range(row_count - 2, 0, -1))
        pieces = dict(zip([outer], back(panels, [outer], grads, cell, total, True)))
        rest, part, pieces[outer] = lax.optimization_barrier((total, part, pieces[outer]))
        landed = {outer: swap(pieces[outer], "row", outer)}
        pieces.update(zip(inner, back(panels, inner, grads, cell, rest, True)))
        rest, landed[outer] = lax.optimization_barrier((total, landed[outer]))
        pieces.update(zip([0], back(panels, [0], grads, cell, rest, True)))
    else:
        own = jnp.concatenate(own_grads, axis=1)
        mate_grads.append(swap(own_grads[far], "col", 1))
        mate = jnp.concatenate(mate_grads, axis=1)
        total = jnp.dot(own, cell[: half * nodes], preferred_element_type=F32)
        total = total + jnp.dot(mate, cell[half * nodes :], preferred_element_type=F32)
        pieces = {
            k: total[:, k * nodes : (k + 1) * nodes].T.astype(F32 if k == 0 else BF16)
            for k in range(row_count)
        }
        landed = {}
    for k in range(1, row_count):
        if k not in landed:
            landed[k] = swap(pieces[k], "row", k)
    *masks, mask = doublings(2, col_count)
    part = sum_over(part, "col", masks)
    value = pieces[0]
    for piece in landed.values():
        value = value + piece.astype(F32)
    grad_features, grad_weight, grad_bias = finish(value, part, swap(part, "col", mask), factor)
    return (hidden, grad_weight, grad_bias[0], grad_features)


def solution(mesh):
    in_specs = (
        P(("col", "row"), None),
        P(),
        P(),
        P(("row", "col"), None),
        P("row", "col", None, None, None),
        P("row", "col", None),
        P("row", "col", None),
        P("row", "col"),
    )
    out_specs = (P(("row", "col"), None), P(), P(), P(("col", "row"), None))
    return jax.shard_map(
        per_device, mesh=mesh, in_specs=in_specs, out_specs=out_specs, check_vma=False
    )
```

```python
import math

import jax
import jax.numpy as jnp
from jax import lax
from jax.experimental import pallas as pl
from jax.experimental.pallas import tpu as pltpu
from jax.sharding import PartitionSpec as P

BF16 = jnp.bfloat16
F32 = jnp.float32
CELL_IN_VMEM = 1 << 24


def densify_kernel(per, half, one_band, rows_ref, cols_ref, count_ref, *refs):
    *window_refs, cell_ref = refs
    group, block, _ = window_refs[0].shape
    band = pl.program_id(0)
    step = pl.program_id(1)
    row_pos = lax.axis_index("row")
    col_pos = lax.axis_index("col")

    @pl.when(step == 0)
    def _():
        def clear(index, carry):
            cell_ref[pl.ds(pl.multiple_of(index * block, block), block), :] = jnp.zeros(
                (block, cell_ref.shape[1]), cell_ref.dtype
            )
            return carry

        lax.fori_loop(0, cell_ref.shape[0] // block, clear, 0)

    def put(window_ref, start, first, number):
        places = []
        for index in range(number):
            row = rows_ref[0, 0, start + first + index]
            col = cols_ref[0, 0, start + first + index]
            panel = lax.div(row, per)
            down = panel ^ col_pos
            down = (down & 1) * half + (down >> 1)
            top = ((down - panel) * per + row) * block - band * cell_ref.shape[0]
            panel = lax.div(col, per)
            left = (((panel ^ row_pos) - panel) * per + col) * block
            places.append((top, left))
        values = [window_ref[first + index] for index in range(number)]
        for (top, left), value in zip(places, values):

            def store(top=top, left=left, value=value):
                cell_ref[
                    pl.ds(pl.multiple_of(top, block), block),
                    pl.ds(pl.multiple_of(left, block), block),
                ] = value

            if one_band:
                store()
            else:
                pl.when((top >= 0) & (top < cell_ref.shape[0]))(store)

    for part, window_ref in enumerate(window_refs):
        start = (step * len(window_refs) + part) * group
        live = jnp.clip(count_ref[0, 0] - start, 0, group)

        def put_four(index, carry, window_ref=window_ref, start=start):
            put(window_ref, start, index * 4, 4)
            return carry

        lax.fori_loop(0, live >> 2, put_four, 0)

        def put_one(index, carry, window_ref=window_ref, start=start):
            put(window_ref, start, index, 1)
            return carry

        lax.fori_loop((live >> 2) << 2, live, put_one, 0)


def densify(tiles, rows, cols, count, per, col_count, row_count):
    slots, block, _ = tiles.shape
    group = math.gcd(slots, 32)
    windows = math.gcd(slots // group, 3)
    shape = (per * col_count * block, per * row_count * block)
    size = shape[0] * shape[1] * 2
    bands = max(1, size // CELL_IN_VMEM)
    space = pltpu.VMEM if bands == 1 else pltpu.HBM

    def tile_spec(part):
        def tile_map(band, step, rows_ref, cols_ref, count_ref):
            last = jnp.maximum(count_ref[0, 0] - 1, 0) // group
            return (jnp.minimum(step * windows + part, last), 0, 0)

        return pl.BlockSpec((group, block, block), tile_map)

    tiles = pltpu.with_memory_space_constraint(tiles, pltpu.HBM)
    return pl.pallas_call(
        lambda *refs: densify_kernel(per, col_count // 2, bands == 1, *refs),
        out_shape=space(shape, tiles.dtype),
        grid_spec=pltpu.PrefetchScalarGridSpec(
            num_scalar_prefetch=3,
            grid=(bands, slots // (group * windows)),
            in_specs=[tile_spec(part) for part in range(windows)],
            out_specs=pl.BlockSpec(
                (shape[0] // bands, shape[1]),
                lambda band, step, *refs: (band, 0),
                pipeline_mode=pl.Buffered(1),
            ),
        ),
        compiler_params=pltpu.CompilerParams(
            vmem_limit_bytes=size // bands + (10 << 20)
        ),
        cost_estimate=pl.CostEstimate(
            flops=0, bytes_accessed=2 * size, transcendentals=0
        ),
        name="densify",
    )(
        pltpu.with_memory_space_constraint(rows, pltpu.HBM),
        pltpu.with_memory_space_constraint(cols, pltpu.HBM),
        count,
        *[tiles] * windows,
    )


def dense_kernel(part_count, *refs):
    own_ref = refs[0]
    part_refs = refs[1 : 1 + part_count]
    weight_ref, bias_ref, cotangent_ref = refs[1 + part_count : 4 + part_count]
    hidden_ref, grad_ref, local_ref = refs[4 + part_count :]
    total = own_ref[...]
    for part_ref in part_refs:
        total = total + part_ref[...].astype(F32)
    aggregated = total.astype(BF16)
    weight = weight_ref[...]
    preact = jnp.dot(aggregated, weight, preferred_element_type=F32) + bias_ref[...]
    sigma = jax.nn.sigmoid(preact)
    hidden_ref[...] = (preact * sigma).astype(BF16)
    slope = sigma * (1.0 + preact * (1.0 - sigma))
    grad_pre = (cotangent_ref[...].astype(F32) * slope).astype(BF16)
    grad_ref[...] = lax.dot_general(
        weight, grad_pre, (((1,), (1,)), ((), ())), preferred_element_type=F32
    ).astype(BF16)
    width = weight.shape[0]
    local_ref[:width] = lax.dot_general(
        aggregated, grad_pre, (((0,), (0,)), ((), ())), preferred_element_type=F32
    ).astype(BF16)
    local_ref[width:] = jnp.broadcast_to(
        jnp.sum(grad_pre.astype(F32), axis=0, keepdims=True),
        (local_ref.shape[0] - width, width),
    ).astype(BF16)


def dense(own, parts, weight, bias, cotangent):
    nodes, width = own.shape
    spec = pl.BlockSpec(memory_space=pltpu.VMEM)
    shapes = (
        jax.ShapeDtypeStruct((nodes, width), BF16),
        jax.ShapeDtypeStruct((width, nodes), BF16),
        jax.ShapeDtypeStruct((width + 16, width), BF16),
    )
    return pl.pallas_call(
        lambda *refs: dense_kernel(len(parts), *refs),
        out_shape=shapes,
        in_specs=[spec] * (4 + len(parts)),
        out_specs=(spec,) * 3,
        compiler_params=pltpu.CompilerParams(vmem_limit_bytes=16 << 20),
        cost_estimate=pl.CostEstimate(
            flops=6 * nodes * width * width,
            bytes_accessed=8 * nodes * width,
            transcendentals=nodes * width,
        ),
        name="dense",
    )(own, *parts, weight, bias.reshape(1, width), cotangent)


def back_kernel(panels, chosen, last, with_total, *refs):
    cell_ref, *grad_refs = refs[: 1 + len(panels)]
    rest = refs[1 + len(panels) :]
    width, nodes = grad_refs[0].shape
    runs = []
    for panel, ref in zip(panels, grad_refs):
        if runs and runs[-1][0] + len(runs[-1][1]) == panel:
            runs[-1][1].append(ref[...])
        else:
            runs.append((panel, [ref[...]]))
    runs = [(panel * nodes, jnp.concatenate(grads, axis=1)) for panel, grads in runs]

    def product(columns):
        value = None
        for top, grads in runs:
            part = jnp.dot(
                grads,
                cell_ref[top : top + grads.shape[1], columns],
                preferred_element_type=F32,
            )
            value = part if value is None else value + part
        return value

    out_refs = rest[with_total:]
    for index, panel in enumerate(chosen):
        columns = slice(panel * nodes, (panel + 1) * nodes)
        value = product(columns)
        if with_total:
            value = rest[0][:, columns] + value
        if last:
            out_refs[index][...] = value.T.astype(out_refs[index].dtype)
        else:
            out_refs[0][:, columns] = value


def back(panels, chosen, grads, cell, total=None, last=False):
    width, nodes = grads[0].shape
    spec = pl.BlockSpec(memory_space=pltpu.VMEM)
    operands = (cell, *grads) if total is None else (cell, *grads, total)
    if not last:
        outs = (pltpu.VMEM((width, cell.shape[1]), F32),)
    else:
        outs = tuple(
            pltpu.VMEM((nodes, width), F32 if panel == 0 else BF16) for panel in chosen
        )
    flops = 2 * len(panels) * len(chosen) * nodes * nodes * width
    return pl.pallas_call(
        lambda *refs: back_kernel(panels, chosen, last, total is not None, *refs),
        out_shape=outs,
        in_specs=[spec] * len(operands),
        out_specs=[spec] * len(outs),
        compiler_params=pltpu.CompilerParams(vmem_limit_bytes=24 << 20),
        cost_estimate=pl.CostEstimate(
            flops=flops, bytes_accessed=flops // 512, transcendentals=0
        ),
        name="back_last" if last else "back",
    )(*operands)


def finish_kernel(factor, value_ref, part_ref, other_ref, out_ref, weight_ref, bias_ref):
    out_ref[...] = value_ref[...].astype(out_ref.dtype)
    summed = (part_ref[...].astype(F32) + other_ref[...].astype(F32)) * factor
    width = weight_ref.shape[0]
    weight_ref[...] = summed[:width]
    bias_ref[...] = summed[width : width + 1]


def finish(value, part, other, factor):
    spec = pl.BlockSpec(memory_space=pltpu.VMEM)
    nodes, width = value.shape
    return pl.pallas_call(
        lambda *refs: finish_kernel(factor, *refs),
        out_shape=(
            jax.ShapeDtypeStruct((nodes, width), BF16),
            jax.ShapeDtypeStruct((width, width), F32),
            jax.ShapeDtypeStruct((1, width), F32),
        ),
        in_specs=[spec] * 3,
        out_specs=(spec,) * 3,
        compiler_params=pltpu.CompilerParams(vmem_limit_bytes=16 << 20),
        cost_estimate=pl.CostEstimate(
            flops=8 * nodes * width, bytes_accessed=16 * nodes * width, transcendentals=0
        ),
        name="finish",
    )(value, part, other)


def swap(value, axis, mask):
    count = lax.axis_size(axis)
    return lax.ppermute(value, axis, [(i, i ^ mask) for i in range(count)])


def move(value, pairs):
    pairs = [(2 * a + core, 2 * b + core) for a, b in pairs for core in range(2)]
    return lax.ppermute(value, "col", pairs)


def sum_far(far, chunk, ready):
    if lax.axis_size("col") != 8:
        count = lax.axis_size("col") // 2
        parts = [swap(chunk(k, far).astype(BF16), "col", 2 * k) for k in range(1, count - 1)]
        return [*parts, swap(far, "col", 2 * (count - 1))], chunk(0, far)
    near = chunk(1, far).astype(BF16)
    landed = swap(jnp.where(at_end(), far, near), "col", 2)
    passed = jnp.where(at_end(), 0.0, landed.astype(F32))
    later, ready = lax.optimization_barrier((far, ready))
    middle = move(later, [(1, 2), (2, 1)])
    across = swap((chunk(2, passed) + passed).astype(BF16), "col", 4)
    near = move(near, [(0, 1), (3, 2)])
    return [jnp.where(at_end(), landed, near), across, middle], chunk(0, far)


def gather_far(value, count, hold):
    if count != 4:
        return [value] + [swap(value, "col", 2 * k) for k in range(1, count)], hold
    across, hold = lax.optimization_barrier((swap(value, "col", 4), hold))
    near = swap(value, "col", 2)
    passed = swap(across, "col", 2)
    middle = move(value, [(1, 2), (2, 1)])
    return [value, near, across, jnp.where(at_end(), passed, middle)], hold


def at_end():
    place = lax.axis_index("col") // 2
    return (place == 0) | (place == lax.axis_size("col") // 2 - 1)


def sum_over(value, axis, masks):
    for mask in masks:
        value = value.astype(F32) + swap(value, axis, mask).astype(F32)
        value = lax.optimization_barrier(value.astype(BF16))
    return value


def doublings(first, end):
    return [first << power for power in range((end // first).bit_length() - 1)]


def per_device(features, weight, bias, cotangent, tiles, tile_rows, tile_cols, tile_counts):
    block = tiles.shape[-1]
    nodes, width = features.shape
    row_count = lax.axis_size("row")
    col_count = lax.axis_size("col")
    half = col_count // 2
    factor = 1.0 / math.sqrt(nodes * row_count * col_count)

    source = jnp.zeros((row_count * nodes, width), BF16).at[:nodes].set(features)
    for k in range(row_count - 1, 0, -1):
        source = source.at[k * nodes : (k + 1) * nodes].set(swap(features, "row", k))
    cell = densify(
        tiles[0, 0], tile_rows, tile_cols, tile_counts, nodes // block, col_count, row_count
    )

    def cell_rows(core, k):
        top = (core * half + k) * nodes
        return cell[top : top + nodes]


    def cell_product(core, k, source):
        return jnp.dot(cell_rows(core, k), source, preferred_element_type=F32)

    far = half - 1
    from_mate = {
        k: swap(cell_product(1, k, source).astype(BF16), "col", 1) for k in (far, far - 1)
    }
    own_far = lax.optimization_barrier(cell_product(0, far, source))
    own_far = (own_far + from_mate[far].astype(F32)).astype(BF16)

    later, from_mate[far - 1] = lax.optimization_barrier((source, from_mate[far - 1]))
    for k in range(far - 1):
        from_mate[k] = swap(cell_product(1, k, later).astype(BF16), "col", 1)

    def chunk(k, hold):
        after, hold = lax.optimization_barrier((source, hold))
        return cell_product(0, k, after) + from_mate[k].astype(F32)

    parts, own = sum_far(own_far, chunk, from_mate[far - 1])
    hidden, grad_agg, local = dense(own, parts, weight, bias, cotangent)

    first, *masks = doublings(1, row_count)
    own_grads, other = gather_far(grad_agg, half, swap(local, "row", first))
    part = lax.optimization_barrier((local.astype(F32) + other.astype(F32)).astype(BF16))
    part = sum_over(part, "row", masks)
    part = sum_over(part, "col", [1])
    mate_grads = [swap(grads, "col", 1) for grads in own_grads[:far]]

    if cell.size * 2 <= CELL_IN_VMEM:
        every = list(range(row_count))
        (total,) = back(list(range(far)), every, own_grads[:far], cell)
        (total,) = back(list(range(half, half + far)), every, mate_grads, cell, total)
        panels = [far, half + far]
        grads = [own_grads[far], swap(own_grads[far], "col", 1)]
        outer, inner = row_count - 1, list(range(row_count - 2, 0, -1))
        pieces = dict(zip([outer], back(panels, [outer], grads, cell, total, True)))
        rest, part, pieces[outer] = lax.optimization_barrier((total, part, pieces[outer]))
        landed = {outer: swap(pieces[outer], "row", outer)}
        pieces.update(zip(inner, back(panels, inner, grads, cell, rest, True)))
        rest, landed[outer] = lax.optimization_barrier((total, landed[outer]))
        pieces.update(zip([0], back(panels, [0], grads, cell, rest, True)))
    else:
        own = jnp.concatenate(own_grads, axis=1)
        mate_grads.append(swap(own_grads[far], "col", 1))
        mate = jnp.concatenate(mate_grads, axis=1)
        total = jnp.dot(own, cell[: half * nodes], preferred_element_type=F32)
        total = total + jnp.dot(mate, cell[half * nodes :], preferred_element_type=F32)
        pieces = {
            k: total[:, k * nodes : (k + 1) * nodes].T.astype(F32 if k == 0 else BF16)
            for k in range(row_count)
        }
        landed = {}
    for k in range(1, row_count):
        if k not in landed:
            landed[k] = swap(pieces[k], "row", k)
    *masks, mask = doublings(2, col_count)
    part = sum_over(part, "col", masks)
    value = pieces[0]
    for piece in landed.values():
        value = value + piece.astype(F32)
    grad_features, grad_weight, grad_bias = finish(value, part, swap(part, "col", mask), factor)
    return (hidden, grad_weight, grad_bias[0], grad_features)


def solution(mesh):
    in_specs = (
        P(("col", "row"), None),
        P(),
        P(),
        P(("row", "col"), None),
        P("row", "col", None, None, None),
        P("row", "col", None),
        P("row", "col", None),
        P("row", "col"),
    )
    out_specs = (P(("row", "col"), None), P(), P(), P(("col", "row"), None))
    return jax.shard_map(
        per_device, mesh=mesh, in_specs=in_specs, out_specs=out_specs, check_vma=False
    )
```

```python
import math

import jax
import jax.numpy as jnp
from jax import lax
from jax.experimental import pallas as pl
from jax.experimental.pallas import tpu as pltpu
from jax.sharding import PartitionSpec as P

BF16 = jnp.bfloat16
F32 = jnp.float32
CELL_IN_VMEM = 1 << 24


def densify_kernel(per, half, one_band, rows_ref, cols_ref, count_ref, *refs):
    *window_refs, cell_ref = refs
    group, block, _ = window_refs[0].shape
    band = pl.program_id(0)
    step = pl.program_id(1)
    row_pos = lax.axis_index("row")
    col_pos = lax.axis_index("col")

    @pl.when(step == 0)
    def _():
        def clear(index, carry):
            cell_ref[pl.ds(pl.multiple_of(index * block, block), block), :] = jnp.zeros(
                (block, cell_ref.shape[1]), cell_ref.dtype
            )
            return carry

        lax.fori_loop(0, cell_ref.shape[0] // block, clear, 0)

    def put(window_ref, start, first, number):
        places = []
        for index in range(number):
            row = rows_ref[0, 0, start + first + index]
            col = cols_ref[0, 0, start + first + index]
            panel = lax.div(row, per)
            down = panel ^ col_pos
            down = (down & 1) * half + (down >> 1)
            top = ((down - panel) * per + row) * block - band * cell_ref.shape[0]
            panel = lax.div(col, per)
            left = (((panel ^ row_pos) - panel) * per + col) * block
            places.append((top, left))
        values = [window_ref[first + index] for index in range(number)]
        for (top, left), value in zip(places, values):

            def store(top=top, left=left, value=value):
                cell_ref[
                    pl.ds(pl.multiple_of(top, block), block),
                    pl.ds(pl.multiple_of(left, block), block),
                ] = value

            if one_band:
                store()
            else:
                pl.when((top >= 0) & (top < cell_ref.shape[0]))(store)

    for part, window_ref in enumerate(window_refs):
        start = (step * len(window_refs) + part) * group
        live = jnp.clip(count_ref[0, 0] - start, 0, group)

        def put_four(index, carry, window_ref=window_ref, start=start):
            put(window_ref, start, index * 4, 4)
            return carry

        lax.fori_loop(0, live >> 2, put_four, 0)

        def put_one(index, carry, window_ref=window_ref, start=start):
            put(window_ref, start, index, 1)
            return carry

        lax.fori_loop((live >> 2) << 2, live, put_one, 0)


def densify(tiles, rows, cols, count, per, col_count, row_count):
    slots, block, _ = tiles.shape
    group = math.gcd(slots, 32)
    windows = math.gcd(slots // group, 3)
    shape = (per * col_count * block, per * row_count * block)
    size = shape[0] * shape[1] * 2
    bands = max(1, size // CELL_IN_VMEM)
    space = pltpu.VMEM if bands == 1 else pltpu.HBM

    def tile_spec(part):
        def tile_map(band, step, rows_ref, cols_ref, count_ref):
            last = jnp.maximum(count_ref[0, 0] - 1, 0) // group
            return (jnp.minimum(step * windows + part, last), 0, 0)

        return pl.BlockSpec((group, block, block), tile_map)

    tiles = pltpu.with_memory_space_constraint(tiles, pltpu.HBM)
    return pl.pallas_call(
        lambda *refs: densify_kernel(per, col_count // 2, bands == 1, *refs),
        out_shape=space(shape, tiles.dtype),
        grid_spec=pltpu.PrefetchScalarGridSpec(
            num_scalar_prefetch=3,
            grid=(bands, slots // (group * windows)),
            in_specs=[tile_spec(part) for part in range(windows)],
            out_specs=pl.BlockSpec(
                (shape[0] // bands, shape[1]),
                lambda band, step, *refs: (band, 0),
                pipeline_mode=pl.Buffered(1),
            ),
        ),
        compiler_params=pltpu.CompilerParams(
            vmem_limit_bytes=size // bands + (10 << 20)
        ),
        cost_estimate=pl.CostEstimate(
            flops=0, bytes_accessed=2 * size, transcendentals=0
        ),
        name="densify",
    )(
        pltpu.with_memory_space_constraint(rows, pltpu.HBM),
        pltpu.with_memory_space_constraint(cols, pltpu.HBM),
        count,
        *[tiles] * windows,
    )


def dense_kernel(part_count, *refs):
    own_ref = refs[0]
    part_refs = refs[1 : 1 + part_count]
    weight_ref, bias_ref, cotangent_ref = refs[1 + part_count : 4 + part_count]
    hidden_ref, grad_ref, local_ref = refs[4 + part_count :]
    total = own_ref[...]
    for part_ref in part_refs:
        total = total + part_ref[...].astype(F32)
    aggregated = total.astype(BF16)
    weight = weight_ref[...]
    preact = jnp.dot(aggregated, weight, preferred_element_type=F32) + bias_ref[...]
    sigma = jax.nn.sigmoid(preact)
    hidden_ref[...] = (preact * sigma).astype(BF16)
    slope = sigma * (1.0 + preact * (1.0 - sigma))
    grad_pre = (cotangent_ref[...].astype(F32) * slope).astype(BF16)
    grad_ref[...] = lax.dot_general(
        weight, grad_pre, (((1,), (1,)), ((), ())), preferred_element_type=F32
    ).astype(BF16)
    width = weight.shape[0]
    local_ref[:width] = lax.dot_general(
        aggregated, grad_pre, (((0,), (0,)), ((), ())), preferred_element_type=F32
    ).astype(BF16)
    local_ref[width:] = jnp.broadcast_to(
        jnp.sum(grad_pre.astype(F32), axis=0, keepdims=True),
        (local_ref.shape[0] - width, width),
    ).astype(BF16)


def dense(own, parts, weight, bias, cotangent):
    nodes, width = own.shape
    spec = pl.BlockSpec(memory_space=pltpu.VMEM)
    shapes = (
        jax.ShapeDtypeStruct((nodes, width), BF16),
        jax.ShapeDtypeStruct((width, nodes), BF16),
        jax.ShapeDtypeStruct((width + 16, width), BF16),
    )
    return pl.pallas_call(
        lambda *refs: dense_kernel(len(parts), *refs),
        out_shape=shapes,
        in_specs=[spec] * (4 + len(parts)),
        out_specs=(spec,) * 3,
        compiler_params=pltpu.CompilerParams(vmem_limit_bytes=16 << 20),
        cost_estimate=pl.CostEstimate(
            flops=6 * nodes * width * width,
            bytes_accessed=8 * nodes * width,
            transcendentals=nodes * width,
        ),
        name="dense",
    )(own, *parts, weight, bias.reshape(1, width), cotangent)


def back_kernel(panels, chosen, last, with_total, *refs):
    cell_ref, *grad_refs = refs[: 1 + len(panels)]
    rest = refs[1 + len(panels) :]
    width, nodes = grad_refs[0].shape
    runs = []
    for panel, ref in zip(panels, grad_refs):
        if runs and runs[-1][0] + len(runs[-1][1]) == panel:
            runs[-1][1].append(ref[...])
        else:
            runs.append((panel, [ref[...]]))
    runs = [(panel * nodes, jnp.concatenate(grads, axis=1)) for panel, grads in runs]

    def product(columns):
        value = None
        for top, grads in runs:
            part = jnp.dot(
                grads,
                cell_ref[top : top + grads.shape[1], columns],
                preferred_element_type=F32,
            )
            value = part if value is None else value + part
        return value

    out_refs = rest[with_total:]
    for index, panel in enumerate(chosen):
        columns = slice(panel * nodes, (panel + 1) * nodes)
        value = product(columns)
        if with_total:
            value = rest[0][:, columns] + value
        if last:
            out_refs[index][...] = value.T.astype(out_refs[index].dtype)
        else:
            out_refs[0][:, columns] = value


def back(panels, chosen, grads, cell, total=None, last=False):
    width, nodes = grads[0].shape
    spec = pl.BlockSpec(memory_space=pltpu.VMEM)
    operands = (cell, *grads) if total is None else (cell, *grads, total)
    if not last:
        outs = (pltpu.VMEM((width, cell.shape[1]), F32),)
    else:
        outs = tuple(
            pltpu.VMEM((nodes, width), F32 if panel == 0 else BF16) for panel in chosen
        )
    flops = 2 * len(panels) * len(chosen) * nodes * nodes * width
    return pl.pallas_call(
        lambda *refs: back_kernel(panels, chosen, last, total is not None, *refs),
        out_shape=outs,
        in_specs=[spec] * len(operands),
        out_specs=[spec] * len(outs),
        compiler_params=pltpu.CompilerParams(vmem_limit_bytes=24 << 20),
        cost_estimate=pl.CostEstimate(
            flops=flops, bytes_accessed=flops // 512, transcendentals=0
        ),
        name="back_last" if last else "back",
    )(*operands)


def finish_kernel(factor, value_ref, part_ref, other_ref, out_ref, weight_ref, bias_ref):
    out_ref[...] = value_ref[...].astype(out_ref.dtype)
    summed = (part_ref[...].astype(F32) + other_ref[...].astype(F32)) * factor
    width = weight_ref.shape[0]
    weight_ref[...] = summed[:width]
    bias_ref[...] = summed[width : width + 1]


def finish(value, part, other, factor):
    spec = pl.BlockSpec(memory_space=pltpu.VMEM)
    nodes, width = value.shape
    return pl.pallas_call(
        lambda *refs: finish_kernel(factor, *refs),
        out_shape=(
            jax.ShapeDtypeStruct((nodes, width), BF16),
            jax.ShapeDtypeStruct((width, width), F32),
            jax.ShapeDtypeStruct((1, width), F32),
        ),
        in_specs=[spec] * 3,
        out_specs=(spec,) * 3,
        compiler_params=pltpu.CompilerParams(vmem_limit_bytes=16 << 20),
        cost_estimate=pl.CostEstimate(
            flops=8 * nodes * width, bytes_accessed=16 * nodes * width, transcendentals=0
        ),
        name="finish",
    )(value, part, other)


def swap(value, axis, mask):
    count = lax.axis_size(axis)
    return lax.ppermute(value, axis, [(i, i ^ mask) for i in range(count)])


def move(value, pairs):
    pairs = [(2 * a + core, 2 * b + core) for a, b in pairs for core in range(2)]
    return lax.ppermute(value, "col", pairs)


def sum_far(far, chunk, ready):
    if lax.axis_size("col") != 8:
        count = lax.axis_size("col") // 2
        parts = [swap(chunk(k, far).astype(BF16), "col", 2 * k) for k in range(1, count - 1)]
        return [*parts, swap(far, "col", 2 * (count - 1))], chunk(0, far)
    passed = jnp.where(at_end(), 0.0, swap(far, "col", 2).astype(F32))
    later, ready = lax.optimization_barrier((far, ready))
    middle = move(later, [(1, 2), (2, 1)])
    both = (chunk(2, passed) + passed).astype(BF16)
    across = swap(both, "col", 4)
    near = swap(chunk(1, both).astype(BF16), "col", 2)
    return [near, across, middle], chunk(0, both)


def gather_far(value, count, hold):
    if count != 4:
        return [value] + [swap(value, "col", 2 * k) for k in range(1, count)], hold
    across, hold = lax.optimization_barrier((swap(value, "col", 4), hold))
    near = swap(value, "col", 2)
    passed = swap(across, "col", 2)
    middle = move(value, [(1, 2), (2, 1)])
    return [value, near, across, jnp.where(at_end(), passed, middle)], hold


def at_end():
    place = lax.axis_index("col") // 2
    return (place == 0) | (place == lax.axis_size("col") // 2 - 1)


def sum_over(value, axis, masks):
    for mask in masks:
        value = value.astype(F32) + swap(value, axis, mask).astype(F32)
        value = lax.optimization_barrier(value.astype(BF16))
    return value


def doublings(first, end):
    return [first << power for power in range((end // first).bit_length() - 1)]


def per_device(features, weight, bias, cotangent, tiles, tile_rows, tile_cols, tile_counts):
    block = tiles.shape[-1]
    nodes, width = features.shape
    row_count = lax.axis_size("row")
    col_count = lax.axis_size("col")
    half = col_count // 2
    factor = 1.0 / math.sqrt(nodes * row_count * col_count)

    source = jnp.zeros((row_count * nodes, width), BF16).at[:nodes].set(features)
    for k in range(row_count - 1, 0, -1):
        source = source.at[k * nodes : (k + 1) * nodes].set(swap(features, "row", k))
    cell = densify(
        tiles[0, 0], tile_rows, tile_cols, tile_counts, nodes // block, col_count, row_count
    )

    def cell_rows(core, k):
        top = (core * half + k) * nodes
        return cell[top : top + nodes]


    def cell_product(core, k, source):
        return jnp.dot(cell_rows(core, k), source, preferred_element_type=F32)

    far = half - 1
    for_mate = cell_product(1, far, source).astype(BF16)
    after, for_mate = lax.optimization_barrier((source, for_mate))
    from_mate = {far: swap(for_mate, "col", 1)}
    from_mate[far - 1] = swap(cell_product(1, far - 1, after).astype(BF16), "col", 1)
    own_far = lax.optimization_barrier(cell_product(0, far, after))
    own_far = (own_far + from_mate[far].astype(F32)).astype(BF16)
    later, own_far = lax.optimization_barrier((after, own_far))
    for k in range(far - 1):
        from_mate[k] = swap(cell_product(1, k, later).astype(BF16), "col", 1)

    def chunk(k, hold):
        after, hold = lax.optimization_barrier((source, hold))
        return cell_product(0, k, after) + from_mate[k].astype(F32)

    parts, own = sum_far(own_far, chunk, from_mate[far - 1])
    hidden, grad_agg, local = dense(own, parts, weight, bias, cotangent)

    first, *masks = doublings(1, row_count)
    own_grads, other = gather_far(grad_agg, half, swap(local, "row", first))
    part = lax.optimization_barrier((local.astype(F32) + other.astype(F32)).astype(BF16))
    part = sum_over(part, "row", masks)
    part = sum_over(part, "col", [1])
    mate_grads = [swap(grads, "col", 1) for grads in own_grads[:far]]

    if cell.size * 2 <= CELL_IN_VMEM:
        every = list(range(row_count))
        (total,) = back(list(range(far)), every, own_grads[:far], cell)
        (total,) = back(list(range(half, half + far)), every, mate_grads, cell, total)
        panels = [far, half + far]
        grads = [own_grads[far], swap(own_grads[far], "col", 1)]
        outer, inner = row_count - 1, list(range(row_count - 2, 0, -1))
        pieces = dict(zip([outer], back(panels, [outer], grads, cell, total, True)))
        rest, part, pieces[outer] = lax.optimization_barrier((total, part, pieces[outer]))
        landed = {outer: swap(pieces[outer], "row", outer)}
        pieces.update(zip(inner, back(panels, inner, grads, cell, rest, True)))
        rest, landed[outer] = lax.optimization_barrier((total, landed[outer]))
        pieces.update(zip([0], back(panels, [0], grads, cell, rest, True)))
    else:
        own = jnp.concatenate(own_grads, axis=1)
        mate_grads.append(swap(own_grads[far], "col", 1))
        mate = jnp.concatenate(mate_grads, axis=1)
        total = jnp.dot(own, cell[: half * nodes], preferred_element_type=F32)
        total = total + jnp.dot(mate, cell[half * nodes :], preferred_element_type=F32)
        pieces = {
            k: total[:, k * nodes : (k + 1) * nodes].T.astype(F32 if k == 0 else BF16)
            for k in range(row_count)
        }
        landed = {}
    for k in range(1, row_count):
        if k not in landed:
            landed[k] = swap(pieces[k], "row", k)
    *masks, mask = doublings(2, col_count)
    part = sum_over(part, "col", masks)
    value = pieces[0]
    for piece in landed.values():
        value = value + piece.astype(F32)
    grad_features, grad_weight, grad_bias = finish(value, part, swap(part, "col", mask), factor)
    return (hidden, grad_weight, grad_bias[0], grad_features)


def solution(mesh):
    in_specs = (
        P(("col", "row"), None),
        P(),
        P(),
        P(("row", "col"), None),
        P("row", "col", None, None, None),
        P("row", "col", None),
        P("row", "col", None),
        P("row", "col"),
    )
    out_specs = (P(("row", "col"), None), P(), P(), P(("col", "row"), None))
    return jax.shard_map(
        per_device, mesh=mesh, in_specs=in_specs, out_specs=out_specs, check_vma=False
    )
```

```python
import math

import jax
import jax.numpy as jnp
from jax import lax
from jax.experimental import pallas as pl
from jax.experimental.pallas import tpu as pltpu
from jax.sharding import PartitionSpec as P

BF16 = jnp.bfloat16
F32 = jnp.float32
CELL_IN_VMEM = 1 << 24


def densify_kernel(per, half, one_band, rows_ref, cols_ref, count_ref, *refs):
    *window_refs, cell_ref = refs
    group, block, _ = window_refs[0].shape
    band = pl.program_id(0)
    step = pl.program_id(1)
    row_pos = lax.axis_index("row")
    col_pos = lax.axis_index("col")

    @pl.when(step == 0)
    def _():
        def clear(index, carry):
            cell_ref[pl.ds(pl.multiple_of(index * block, block), block), :] = jnp.zeros(
                (block, cell_ref.shape[1]), cell_ref.dtype
            )
            return carry

        lax.fori_loop(0, cell_ref.shape[0] // block, clear, 0)

    def put(window_ref, start, first, number):
        places = []
        for index in range(number):
            row = rows_ref[0, 0, start + first + index]
            col = cols_ref[0, 0, start + first + index]
            panel = lax.div(row, per)
            down = panel ^ col_pos
            down = (down & 1) * half + (down >> 1)
            top = ((down - panel) * per + row) * block - band * cell_ref.shape[0]
            panel = lax.div(col, per)
            left = (((panel ^ row_pos) - panel) * per + col) * block
            places.append((top, left))
        values = [window_ref[first + index] for index in range(number)]
        for (top, left), value in zip(places, values):

            def store(top=top, left=left, value=value):
                cell_ref[
                    pl.ds(pl.multiple_of(top, block), block),
                    pl.ds(pl.multiple_of(left, block), block),
                ] = value

            if one_band:
                store()
            else:
                pl.when((top >= 0) & (top < cell_ref.shape[0]))(store)

    for part, window_ref in enumerate(window_refs):
        start = (step * len(window_refs) + part) * group
        live = jnp.clip(count_ref[0, 0] - start, 0, group)

        def put_four(index, carry, window_ref=window_ref, start=start):
            put(window_ref, start, index * 4, 4)
            return carry

        lax.fori_loop(0, live >> 2, put_four, 0)

        def put_one(index, carry, window_ref=window_ref, start=start):
            put(window_ref, start, index, 1)
            return carry

        lax.fori_loop((live >> 2) << 2, live, put_one, 0)


def densify(tiles, rows, cols, count, per, col_count, row_count):
    slots, block, _ = tiles.shape
    group = math.gcd(slots, 32)
    windows = math.gcd(slots // group, 3)
    shape = (per * col_count * block, per * row_count * block)
    size = shape[0] * shape[1] * 2
    bands = max(1, size // CELL_IN_VMEM)
    space = pltpu.VMEM if bands == 1 else pltpu.HBM

    def tile_spec(part):
        def tile_map(band, step, rows_ref, cols_ref, count_ref):
            last = jnp.maximum(count_ref[0, 0] - 1, 0) // group
            return (jnp.minimum(step * windows + part, last), 0, 0)

        return pl.BlockSpec((group, block, block), tile_map)

    tiles = pltpu.with_memory_space_constraint(tiles, pltpu.HBM)
    return pl.pallas_call(
        lambda *refs: densify_kernel(per, col_count // 2, bands == 1, *refs),
        out_shape=space(shape, tiles.dtype),
        grid_spec=pltpu.PrefetchScalarGridSpec(
            num_scalar_prefetch=3,
            grid=(bands, slots // (group * windows)),
            in_specs=[tile_spec(part) for part in range(windows)],
            out_specs=pl.BlockSpec(
                (shape[0] // bands, shape[1]),
                lambda band, step, *refs: (band, 0),
                pipeline_mode=pl.Buffered(1),
            ),
        ),
        compiler_params=pltpu.CompilerParams(
            vmem_limit_bytes=size // bands + (10 << 20)
        ),
        cost_estimate=pl.CostEstimate(
            flops=0, bytes_accessed=2 * size, transcendentals=0
        ),
        name="densify",
    )(
        pltpu.with_memory_space_constraint(rows, pltpu.HBM),
        pltpu.with_memory_space_constraint(cols, pltpu.HBM),
        count,
        *[tiles] * windows,
    )


def dense_kernel(part_count, *refs):
    own_ref = refs[0]
    part_refs = refs[1 : 1 + part_count]
    weight_ref, bias_ref, cotangent_ref = refs[1 + part_count : 4 + part_count]
    hidden_ref, grad_ref, local_ref = refs[4 + part_count :]
    total = own_ref[...]
    for part_ref in part_refs:
        total = total + part_ref[...].astype(F32)
    aggregated = total.astype(BF16)
    weight = weight_ref[...]
    preact = jnp.dot(aggregated, weight, preferred_element_type=F32) + bias_ref[...]
    sigma = jax.nn.sigmoid(preact)
    hidden_ref[...] = (preact * sigma).astype(BF16)
    slope = sigma * (1.0 + preact * (1.0 - sigma))
    grad_pre = (cotangent_ref[...].astype(F32) * slope).astype(BF16)
    grad_ref[...] = lax.dot_general(
        weight, grad_pre, (((1,), (1,)), ((), ())), preferred_element_type=F32
    ).astype(BF16)
    width = weight.shape[0]
    local_ref[:width] = lax.dot_general(
        aggregated, grad_pre, (((0,), (0,)), ((), ())), preferred_element_type=F32
    ).astype(BF16)
    local_ref[width:] = jnp.broadcast_to(
        jnp.sum(grad_pre.astype(F32), axis=0, keepdims=True),
        (local_ref.shape[0] - width, width),
    ).astype(BF16)


def dense(own, parts, weight, bias, cotangent):
    nodes, width = own.shape
    spec = pl.BlockSpec(memory_space=pltpu.VMEM)
    shapes = (
        jax.ShapeDtypeStruct((nodes, width), BF16),
        jax.ShapeDtypeStruct((width, nodes), BF16),
        jax.ShapeDtypeStruct((width + 16, width), BF16),
    )
    return pl.pallas_call(
        lambda *refs: dense_kernel(len(parts), *refs),
        out_shape=shapes,
        in_specs=[spec] * (4 + len(parts)),
        out_specs=(spec,) * 3,
        compiler_params=pltpu.CompilerParams(vmem_limit_bytes=16 << 20),
        cost_estimate=pl.CostEstimate(
            flops=6 * nodes * width * width,
            bytes_accessed=8 * nodes * width,
            transcendentals=nodes * width,
        ),
        name="dense",
    )(own, *parts, weight, bias.reshape(1, width), cotangent)


def back_kernel(panels, chosen, last, with_total, *refs):
    cell_ref, *grad_refs = refs[: 1 + len(panels)]
    rest = refs[1 + len(panels) :]
    width, nodes = grad_refs[0].shape
    runs = []
    for panel, ref in zip(panels, grad_refs):
        if runs and runs[-1][0] + len(runs[-1][1]) == panel:
            runs[-1][1].append(ref[...])
        else:
            runs.append((panel, [ref[...]]))
    runs = [(panel * nodes, jnp.concatenate(grads, axis=1)) for panel, grads in runs]

    def product(columns):
        value = None
        for top, grads in runs:
            part = jnp.dot(
                grads,
                cell_ref[top : top + grads.shape[1], columns],
                preferred_element_type=F32,
            )
            value = part if value is None else value + part
        return value

    out_refs = rest[with_total:]
    for index, panel in enumerate(chosen):
        columns = slice(panel * nodes, (panel + 1) * nodes)
        value = product(columns)
        if with_total:
            value = rest[0][:, columns] + value
        if last:
            out_refs[index][...] = value.T.astype(out_refs[index].dtype)
        else:
            out_refs[0][:, columns] = value


def back(panels, chosen, grads, cell, total=None, last=False):
    width, nodes = grads[0].shape
    spec = pl.BlockSpec(memory_space=pltpu.VMEM)
    operands = (cell, *grads) if total is None else (cell, *grads, total)
    if not last:
        outs = (pltpu.VMEM((width, cell.shape[1]), F32),)
    else:
        outs = tuple(
            pltpu.VMEM((nodes, width), F32 if panel == 0 else BF16) for panel in chosen
        )
    flops = 2 * len(panels) * len(chosen) * nodes * nodes * width
    return pl.pallas_call(
        lambda *refs: back_kernel(panels, chosen, last, total is not None, *refs),
        out_shape=outs,
        in_specs=[spec] * len(operands),
        out_specs=[spec] * len(outs),
        compiler_params=pltpu.CompilerParams(vmem_limit_bytes=24 << 20),
        cost_estimate=pl.CostEstimate(
            flops=flops, bytes_accessed=flops // 512, transcendentals=0
        ),
        name="back_last" if last else "back",
    )(*operands)


def finish_kernel(factor, value_ref, part_ref, other_ref, out_ref, weight_ref, bias_ref):
    out_ref[...] = value_ref[...].astype(out_ref.dtype)
    summed = (part_ref[...].astype(F32) + other_ref[...].astype(F32)) * factor
    width = weight_ref.shape[0]
    weight_ref[...] = summed[:width]
    bias_ref[...] = summed[width : width + 1]


def finish(value, part, other, factor):
    spec = pl.BlockSpec(memory_space=pltpu.VMEM)
    nodes, width = value.shape
    return pl.pallas_call(
        lambda *refs: finish_kernel(factor, *refs),
        out_shape=(
            jax.ShapeDtypeStruct((nodes, width), BF16),
            jax.ShapeDtypeStruct((width, width), F32),
            jax.ShapeDtypeStruct((1, width), F32),
        ),
        in_specs=[spec] * 3,
        out_specs=(spec,) * 3,
        compiler_params=pltpu.CompilerParams(vmem_limit_bytes=16 << 20),
        cost_estimate=pl.CostEstimate(
            flops=8 * nodes * width, bytes_accessed=16 * nodes * width, transcendentals=0
        ),
        name="finish",
    )(value, part, other)


def swap(value, axis, mask):
    count = lax.axis_size(axis)
    return lax.ppermute(value, axis, [(i, i ^ mask) for i in range(count)])


def move(value, pairs):
    pairs = [(2 * a + core, 2 * b + core) for a, b in pairs for core in range(2)]
    return lax.ppermute(value, "col", pairs)


def sum_far(far, chunk, ready):
    if lax.axis_size("col") != 8:
        count = lax.axis_size("col") // 2
        parts = [swap(chunk(k, far).astype(BF16), "col", 2 * k) for k in range(1, count - 1)]
        return [*parts, swap(far, "col", 2 * (count - 1))], chunk(0, far)
    passed = jnp.where(at_end(), 0.0, swap(far, "col", 2).astype(F32))
    later, ready = lax.optimization_barrier((far, ready))
    middle = move(later, [(1, 2), (2, 1)])
    both = (chunk(2, passed) + passed).astype(BF16)
    across = swap(both, "col", 4)
    near = swap(chunk(1, both).astype(BF16), "col", 2)
    return [near, across, middle], chunk(0, both)


def gather_far(value, count, hold):
    if count != 4:
        return [value] + [swap(value, "col", 2 * k) for k in range(1, count)], hold
    across, hold = lax.optimization_barrier((swap(value, "col", 4), hold))
    near = swap(value, "col", 2)
    passed = swap(across, "col", 2)
    middle = move(value, [(1, 2), (2, 1)])
    return [value, near, across, jnp.where(at_end(), passed, middle)], hold


def at_end():
    place = lax.axis_index("col") // 2
    return (place == 0) | (place == lax.axis_size("col") // 2 - 1)


def sum_over(value, axis, masks):
    for mask in masks:
        value = value.astype(F32) + swap(value, axis, mask).astype(F32)
        value = lax.optimization_barrier(value.astype(BF16))
    return value


def doublings(first, end):
    return [first << power for power in range((end // first).bit_length() - 1)]


def per_device(features, weight, bias, cotangent, tiles, tile_rows, tile_cols, tile_counts):
    block = tiles.shape[-1]
    nodes, width = features.shape
    row_count = lax.axis_size("row")
    col_count = lax.axis_size("col")
    half = col_count // 2
    factor = 1.0 / math.sqrt(nodes * row_count * col_count)

    source = jnp.zeros((row_count * nodes, width), BF16).at[:nodes].set(features)
    for k in range(row_count - 1, 0, -1):
        source = source.at[k * nodes : (k + 1) * nodes].set(swap(features, "row", k))
    cell = densify(
        tiles[0, 0], tile_rows, tile_cols, tile_counts, nodes // block, col_count, row_count
    )

    def cell_rows(core, k):
        top = (core * half + k) * nodes
        return cell[top : top + nodes]


    def cell_product(core, k, source):
        return jnp.dot(cell_rows(core, k), source, preferred_element_type=F32)

    far = half - 1
    for_mate = cell_product(1, far, source).astype(BF16)
    after, for_mate = lax.optimization_barrier((source, for_mate))
    from_mate = {far: swap(for_mate, "col", 1)}
    own_far, after = lax.optimization_barrier((cell_product(0, far, after), after))
    from_mate[far - 1] = swap(cell_product(1, far - 1, after).astype(BF16), "col", 1)
    own_far = (own_far + from_mate[far].astype(F32)).astype(BF16)
    later, own_far = lax.optimization_barrier((after, own_far))
    for k in range(far - 1):
        from_mate[k] = swap(cell_product(1, k, later).astype(BF16), "col", 1)

    def chunk(k, hold):
        after, hold = lax.optimization_barrier((source, hold))
        return cell_product(0, k, after) + from_mate[k].astype(F32)

    parts, own = sum_far(own_far, chunk, from_mate[far - 1])
    hidden, grad_agg, local = dense(own, parts, weight, bias, cotangent)

    first, *masks = doublings(1, row_count)
    own_grads, other = gather_far(grad_agg, half, swap(local, "row", first))
    part = lax.optimization_barrier((local.astype(F32) + other.astype(F32)).astype(BF16))
    part = sum_over(part, "row", masks)
    part = sum_over(part, "col", [1])
    mate_grads = [swap(grads, "col", 1) for grads in own_grads[:far]]

    if cell.size * 2 <= CELL_IN_VMEM:
        every = list(range(row_count))
        (total,) = back(list(range(far)), every, own_grads[:far], cell)
        (total,) = back(list(range(half, half + far)), every, mate_grads, cell, total)
        panels = [far, half + far]
        grads = [own_grads[far], swap(own_grads[far], "col", 1)]
        outer, inner = row_count - 1, list(range(row_count - 2, 0, -1))
        pieces = dict(zip([outer], back(panels, [outer], grads, cell, total, True)))
        rest, part, pieces[outer] = lax.optimization_barrier((total, part, pieces[outer]))
        landed = {outer: swap(pieces[outer], "row", outer)}
        pieces.update(zip(inner, back(panels, inner, grads, cell, rest, True)))
        rest, landed[outer] = lax.optimization_barrier((total, landed[outer]))
        pieces.update(zip([0], back(panels, [0], grads, cell, rest, True)))
    else:
        own = jnp.concatenate(own_grads, axis=1)
        mate_grads.append(swap(own_grads[far], "col", 1))
        mate = jnp.concatenate(mate_grads, axis=1)
        total = jnp.dot(own, cell[: half * nodes], preferred_element_type=F32)
        total = total + jnp.dot(mate, cell[half * nodes :], preferred_element_type=F32)
        pieces = {
            k: total[:, k * nodes : (k + 1) * nodes].T.astype(F32 if k == 0 else BF16)
            for k in range(row_count)
        }
        landed = {}
    for k in range(1, row_count):
        if k not in landed:
            landed[k] = swap(pieces[k], "row", k)
    *masks, mask = doublings(2, col_count)
    part = sum_over(part, "col", masks)
    value = pieces[0]
    for piece in landed.values():
        value = value + piece.astype(F32)
    grad_features, grad_weight, grad_bias = finish(value, part, swap(part, "col", mask), factor)
    return (hidden, grad_weight, grad_bias[0], grad_features)


def solution(mesh):
    in_specs = (
        P(("col", "row"), None),
        P(),
        P(),
        P(("row", "col"), None),
        P("row", "col", None, None, None),
        P("row", "col", None),
        P("row", "col", None),
        P("row", "col"),
    )
    out_specs = (P(("row", "col"), None), P(), P(), P(("col", "row"), None))
    return jax.shard_map(
        per_device, mesh=mesh, in_specs=in_specs, out_specs=out_specs, check_vma=False
    )
```
